32 devices in a mesh: parts: 2 (over y), node: 4 (over z), seg: 2 (over x), feat: 2 (over core).
Axes of the slice: x: 2, y: 2, z: 4, core: 2. Of those that a mesh axis runs over, the one named last changes fastest.
Arguments:
- memory: float32 [4, 8192, 256], P(('parts', 'seg'), 'node', 'feat'), parts along dimension 0, may hold values from -6 to 6
- req_rows: int32 [2, 4, 4, 4, 256], P(None, ('parts', 'seg'), 'node'), parts along dimension 1, may hold values from 0 to 2047, as said below
- req_count: int32 [2, 4, 4, 4], P(None, ('parts', 'seg'), 'node'), parts along dimension 1, may hold values from 85 to 256, as said below
- dst_slot: int32 [2, 4, 4096], P(None, ('parts', 'seg'), 'node'), parts along dimension 1, may hold values from 0 to 1023, as said below
- elapsed: int32 [2, 4, 4096], P(None, ('parts', 'seg'), 'node'), parts along dimension 1, may hold values from 0 to 9999
- edges: bfloat16 [2, 4, 4096, 128], P(None, ('parts', 'seg'), 'node', 'feat'), parts along dimension 1, may hold values from -6 to 6
- upstream: bfloat16 [2, 4, 4096, 256], P(None, ('parts', 'seg'), 'node', 'feat'), parts along dimension 1, may hold values from -0.125 to 0.125
- freq: float32 [128], replicated, may hold values from 0.0001 to 0.1
- phase: float32 [128], replicated, may hold values from -3.140625 to 3.140625
- w_input: bfloat16 [3, 768, 256], P(None, None, 'feat'), may hold values from -0.21875 to 0.21875
- w_hidden: bfloat16 [3, 256, 256], P(None, None, 'feat'), may hold values from -0.375 to 0.375
- bias: float32 [4, 256], P(None, 'feat'), may hold values from -3 to 3
Outputs:
- memory_out: float32 [4, 8192, 256], P(('parts', 'seg'), 'node', 'feat'), parts along dimension 0
- grad_input: float32 [6, 768, 256], P('parts', None, 'feat'), parts along dimension 0
- grad_hidden: float32 [6, 256, 256], P('parts', None, 'feat'), parts along dimension 0
- grad_bias: float32 [8, 256], P('parts', 'feat'), parts along dimension 0
The draws below stay inside these ranges and needn't reach their ends.
There are 2 independent parts, one for each index of `parts`. The reference program is written for one: setup_inputs(seed, part) draws one part's arguments, and reference() takes and returns one part's arrays. A program takes and returns all parts, laid end to end along the dimension named above; an argument that names none is the same for every part. Nothing has to cross between parts.
Inputs may be any that keep to these rules, and one draw needn't show every extreme that they name: `req_rows`: for one batch, segment and owner, the rows named by all requesting devices in their live slots are distinct; slots past the count hold 0. `req_count`: at least one live request from every device to every owner; in every batch and segment some owner receives exactly 256 from every device. `dst_slot`: equals o * 256 + c for some owner o and a live slot c of this device's requests to o.
All inputs are finite; a program needn't handle non-finite values.
Results may differ from the reference program's by a relative error of at most 0.0055.
Values may be sent and summed in bfloat16 or wider, within the bound.
No kernel may reach another device: no remote copies, remote signals or barrier semaphores. Data moves between devices by JAX's collectives and lax.ppermute only.
A program may use at most 64 MiB of HBM per device.

```python
import math
import jax
import jax.numpy as jnp
from jax import lax

M = 256
TE = 128
EDGE = 128
BATCHES = 2
EV_DEV = 1024
NODE_DEV = 2048
IN = 768
OWNERS = 4
CAP = 256
SEGS = 2
EVENTS = 4096
NODES = 8192


def lead_largest(order):
    position = jnp.argmax(order == NODE_DEV - 1)
    first = order[0]
    return order.at[position].set(first).at[0].set(NODE_DEV - 1)


def request_table(key):
    key_count, key_hot, key_perm = jax.random.split(key, 3)
    lowest = max(1, CAP // 3)
    counts = jax.random.randint(key_count, (BATCHES, SEGS, OWNERS, OWNERS), lowest, CAP + 1)
    hot_owner = jax.random.randint(key_hot, (BATCHES, SEGS), 0, OWNERS)
    drawn_owner = (hot_owner + 1) % OWNERS
    owner_ids = jnp.arange(OWNERS)[None, None, :]
    requester_ids = jnp.arange(OWNERS)[None, None, :, None]
    is_drawn = owner_ids == drawn_owner[:, :, None]
    counts = jnp.where(is_drawn[:, :, None, :] & (requester_ids == OWNERS - 1), lowest, counts)
    is_hot = owner_ids == hot_owner[:, :, None]
    counts = jnp.where(is_hot[:, :, None, :], CAP, counts)
    counts = counts.at[:, :, 0, OWNERS - 1].set(CAP)
    perm_keys = jax.random.split(key_perm, BATCHES * SEGS * OWNERS)
    orders = jax.vmap(lambda one_key: lead_largest(jax.random.permutation(one_key, NODE_DEV)))(perm_keys)
    orders = orders.reshape(BATCHES, SEGS, OWNERS, NODE_DEV)[..., :OWNERS * CAP]
    orders = orders.reshape(BATCHES, SEGS, OWNERS, OWNERS, CAP).transpose(0, 1, 3, 2, 4)
    live_mask = jnp.arange(CAP)[None, None, None, None, :] < counts[..., None]
    rows_table = jnp.where(live_mask, orders, 0)
    return (counts.astype(jnp.int32), rows_table.astype(jnp.int32))


def draw_req_rows(key, part):
    counts, rows_table = request_table(key)
    return rows_table


def draw_req_count(key, part):
    counts, rows_table = request_table(key)
    return counts


def draw_dst_slot(key, part):
    counts, rows_table = request_table(key)
    key = jax.random.fold_in(key, 7)
    key_owner, key_slot = jax.random.split(key)
    owner_pick = jax.random.randint(key_owner, (BATCHES, SEGS, OWNERS, EV_DEV), 0, OWNERS)
    limit = jnp.take_along_axis(counts, owner_pick, axis=3)
    slot_pick = jax.random.randint(key_slot, (BATCHES, SEGS, OWNERS, EV_DEV), 0, limit)
    slots = owner_pick * CAP + slot_pick
    slots = slots.at[:, :, 0, 0].set(OWNERS * CAP - 1).at[:, :, 0, 1].set(0)
    return slots.reshape(BATCHES, SEGS, OWNERS * EV_DEV).astype(jnp.int32)


def touch_ends(result, stream_key, least, top_value):
    longest = result.shape.index(max(result.shape))
    spots = []
    for shift in (0, 1):
        where = [jax.random.randint(jax.random.fold_in(stream_key, axis), (), 0, length) for axis, length in enumerate(result.shape)]
        where[longest] = (where[longest] + shift) % result.shape[longest]
        spots.append(tuple(where))
    return result.at[spots[0]].set(least).at[spots[1]].set(top_value)


def block_scale(rng, extent, shards, low, high):
    loudness = 1.0
    for dim, parts in shards:
        steps = jax.random.uniform(jax.random.fold_in(jax.random.fold_in(rng, 6), dim), (parts,), jnp.float32, low / len(shards), high / len(shards))
        loudness = loudness * jnp.repeat(jnp.exp(steps), extent[dim] // parts).reshape((-1,) + (1,) * (len(extent) - 1 - dim))
    return loudness


def noise(key, dims, width, reach, pieces=(), kind=jnp.bfloat16):
    level = block_scale(key, dims, pieces, -0.22, 0.18) if pieces else 1.0
    values = jax.random.normal(key, dims, jnp.float32) * width * level
    return jnp.minimum(jnp.maximum(values, -reach), reach).astype(kind)


def setup_inputs(seed: int = 0, part: int = 0) -> dict:
    seeds = jax.random.split(jax.random.key(seed), 13)
    own_keys = jax.random.split(jax.random.fold_in(seeds[12], part), 13)
    return {
        "memory": noise(own_keys[0], (SEGS, NODES, M), 1.0, 6.0, ((0, 2), (1, 4), (2, 2)), jnp.float32),
        "req_rows": draw_req_rows(jax.random.fold_in(jax.random.fold_in(seeds[12], part), 71), part),
        "req_count": draw_req_count(jax.random.fold_in(jax.random.fold_in(seeds[12], part), 71), part),
        "dst_slot": draw_dst_slot(jax.random.fold_in(jax.random.fold_in(seeds[12], part), 71), part),
        "elapsed": touch_ends(jax.random.randint(own_keys[4], (BATCHES, SEGS, EVENTS), 0, 10000), jax.random.fold_in(own_keys[4], 1), 0, 9999).astype(jnp.int32),
        "edges": noise(own_keys[5], (BATCHES, SEGS, EVENTS, EDGE), 1.0, 6.0, ((1, 2), (2, 4), (3, 2))),
        "upstream": noise(own_keys[6], (BATCHES, SEGS, EVENTS, M), ((BATCHES * SEGS * EVENTS) ** -0.5), 0.125, ((1, 2), (2, 4), (3, 2))),
        "freq": jnp.clip(jnp.exp(jax.random.uniform(seeds[7], (TE,), jnp.float32, math.log(0.0001), math.log(0.1))), 0.0001, 0.1),
        "phase": jnp.clip(jax.random.uniform(seeds[8], (TE,), jnp.float32, -3.140625, 3.140625), -3.140625, 3.140625),
        "w_input": noise(seeds[9], (3, IN, M), IN ** -0.5, 0.21875, ((2, 2),)),
        "w_hidden": noise(seeds[10], (3, M, M), M ** -0.5, 0.375, ((2, 2),)),
        "bias": noise(seeds[11], (4, M), 0.5, 3.0, ((1, 2),), jnp.float32),
    }


def product(left, right, form):
    return jnp.einsum(form, left.astype(jnp.float32), right.astype(jnp.float32), precision=lax.Precision.HIGHEST)


def gate_pass(message, hidden_bf, w_input, w_hidden, bias):
    input_gates = product(message, w_input, "ei,gih->geh")
    hidden_gates = product(hidden_bf, w_hidden, "ei,gih->geh")
    hidden_own = hidden_bf.astype(jnp.float32)
    reset_gate = jax.nn.sigmoid(input_gates[0] + hidden_gates[0] + bias[0])
    update = jax.nn.sigmoid(input_gates[1] + hidden_gates[1] + bias[1])
    recur_term = hidden_gates[2] + bias[3]
    candid = jnp.tanh(input_gates[2] + bias[2] + reset_gate * recur_term)
    fresh_rows = (1.0 - update) * candid + update * hidden_own
    return fresh_rows, reset_gate, update, candid, recur_term


def gate_grads(message, hidden_bf, cotangent, reset_gate, update, candid, recur_term):
    hidden_own = hidden_bf.astype(jnp.float32)
    grad_cand = cotangent * (1.0 - update) * (1.0 - candid * candid)
    grad_upd = cotangent * (hidden_own - candid) * update * (1.0 - update)
    grad_reset = grad_cand * recur_term * reset_gate * (1.0 - reset_gate)
    grad_recur = grad_cand * reset_gate
    gate_in = jnp.stack([grad_reset, grad_upd, grad_cand]).astype(jnp.bfloat16)
    gate_hid = jnp.stack([grad_reset, grad_upd, grad_recur]).astype(jnp.bfloat16)
    grad_in = product(message, gate_in, "ei,geh->gih")
    grad_hid = product(hidden_bf, gate_hid, "ei,geh->gih")
    grad_b = jnp.stack([jnp.sum(grad_reset, 0), jnp.sum(grad_upd, 0), jnp.sum(grad_cand, 0), jnp.sum(grad_recur, 0)])
    return grad_in, grad_hid, grad_b


def reference(memory, req_rows, req_count, dst_slot, elapsed, edges, upstream, freq, phase, w_input, w_hidden, bias):
    states = [memory[segment] for segment in range(SEGS)]
    grad_in = jnp.zeros((3, IN, M), jnp.float32)
    grad_hid = jnp.zeros((3, M, M), jnp.float32)
    grad_b = jnp.zeros((4, M), jnp.float32)
    offsets = (jnp.arange(EVENTS, dtype=jnp.int32) // EV_DEV) * EV_DEV
    row_base = (jnp.arange(OWNERS, dtype=jnp.int32) * NODE_DEV)[None, :, None]
    for batch_idx in range(BATCHES):
        written = []
        for segment in range(SEGS):
            current = states[segment]
            global_rows = (row_base + req_rows[batch_idx, segment]).astype(jnp.int32)
            live_mask = jnp.arange(CAP, dtype=jnp.int32)[None, None, :] < req_count[batch_idx, segment][:, :, None]
            fetched = jnp.take(current, global_rows.reshape(-1), axis=0).astype(jnp.bfloat16)
            dst_rows = jnp.take(fetched, (offsets + dst_slot[batch_idx, segment]).astype(jnp.int32), axis=0)
            time_code = jnp.cos(elapsed[batch_idx, segment].astype(jnp.float32)[:, None] * freq[None, :] + phase[None, :]).astype(jnp.bfloat16)
            message = jnp.concatenate([fetched, dst_rows, time_code, edges[batch_idx, segment]], axis=1)
            fresh_rows, reset_gate, update, candid, recur_term = gate_pass(message, fetched, w_input, w_hidden, bias)
            live_flat = live_mask.reshape(-1).astype(jnp.float32)
            cotangent = upstream[batch_idx, segment].astype(jnp.float32) * live_flat[:, None]
            part_in, part_hid, part_b = gate_grads(message, fetched, cotangent, reset_gate, update, candid, recur_term)
            grad_in = grad_in + part_in
            grad_hid = grad_hid + part_hid
            grad_b = grad_b + part_b
            places = jnp.where(live_mask, global_rows, OWNERS * NODE_DEV).reshape(-1).astype(jnp.int32)
            written.append(current.at[places].set(fresh_rows, mode="drop"))
        if batch_idx + 1 < BATCHES:
            states = [written[0]] + written[:-1]
        else:
            states = written
    return jnp.stack(states), grad_in, grad_hid, grad_b
```

```python
import jax
import jax.numpy as jnp
from jax import lax
from jax.experimental import pallas as pl
from jax.experimental.pallas import tpu as pltpu
from jax.sharding import PartitionSpec as P

BF = jnp.bfloat16
F32 = jnp.float32
LANES = 128
VMEM = pl.BlockSpec(memory_space=pltpu.VMEM)
SMEM = pl.BlockSpec(memory_space=pltpu.SMEM)


def run(kernel, outs, smem, args, scratch=(), flops=0):
    args = list(smem) + list(args)
    specs = [SMEM] * len(smem) + [VMEM] * (len(args) - len(smem))
    moved = sum(a.size * a.dtype.itemsize for a in list(args) + list(outs))
    return pl.pallas_call(
        kernel,
        out_shape=list(outs),
        in_specs=specs,
        out_specs=[VMEM] * len(outs),
        scratch_shapes=list(scratch),
        compiler_params=pltpu.CompilerParams(vmem_limit_bytes=40 * 1024 * 1024),
        cost_estimate=pl.CostEstimate(flops=flops, bytes_accessed=moved, transcendentals=0),
    )(*args)


def shape(dims, kind):
    return jax.ShapeDtypeStruct(tuple(dims), kind)


def pick_rows(row, source):
    count = source.shape[0]
    numbers = jnp.transpose(jnp.broadcast_to(row, (LANES, LANES)))
    lane = lax.broadcasted_iota(jnp.int32, (LANES, LANES), 1)
    hot = jnp.concatenate(
        [jnp.where(numbers == lane + k * LANES, 1.0, 0.0).astype(BF) for k in range(count // LANES)],
        axis=1,
    )
    return jnp.dot(hot, source, preferred_element_type=F32).astype(BF)


def serve(rows_ref, source, held, piece_refs):
    for j in range(held.shape[0] // LANES):
        row = rows_ref[:, j * LANES : (j + 1) * LANES]
        held[j * LANES : (j + 1) * LANES, :] = pick_rows(row, source)
    cap = piece_refs[0].shape[0]
    for k, piece in enumerate(piece_refs):
        piece[...] = held[k * cap : (k + 1) * cap, :]


def set_rows(rows_ref, values, base, out_ref):
    events = values.shape[0]
    tall = 256
    wide = jnp.concatenate([values, jnp.ones((events, LANES), BF)], axis=1)
    row = rows_ref[...]
    for i in range(out_ref.shape[0] // tall):
        own = lax.broadcasted_iota(jnp.int32, (tall, events), 0) + i * tall
        hot = jnp.where(own == jnp.broadcast_to(row, (tall, events)), 1.0, 0.0).astype(BF)
        found = jnp.dot(hot, wide, preferred_element_type=F32)
        span = slice(i * tall, (i + 1) * tall)
        out_ref[span, :] = jnp.where(found[:, LANES:] > 0.5, found[:, :LANES], base[span, :])


def ask_kernel(nodes, ids, counts, rows_ref, *pieces):
    z = ids[0]
    batches, _, cap = rows_ref.shape
    slot = lax.broadcasted_iota(jnp.int32, (1, cap), 1)
    for k in range(nodes):
        owner = z ^ k
        for b in range(batches):
            row = rows_ref[b, pl.ds(owner, 1), :]
            pieces[k][b : b + 1, :] = jnp.where(slot < counts[b, owner], row, -1)


def serve_kernel(nodes, rows_ref, memory_ref, *rest):
    pieces, held = rest[:nodes], rest[nodes]
    serve(rows_ref, memory_ref[...].astype(BF), held, pieces)


def next_kernel(nodes, ids, put_ref, ask_ref, own_ref, handed_ref, *rest):
    own_pieces, handed_pieces = rest[:nodes], rest[nodes : 2 * nodes]
    memory_ref = rest[2 * nodes]
    pieces = rest[2 * nodes + 1 : 3 * nodes + 1]
    values, base, held = rest[3 * nodes + 1 :]
    cap = pieces[0].shape[0]

    @pl.when(ids[1] == 0)
    def _():
        base[...] = own_ref[...]
        for k in range(nodes):
            values[k * cap : (k + 1) * cap, :] = own_pieces[k][...]

    @pl.when(ids[1] != 0)
    def _():
        base[...] = handed_ref[...].astype(F32)
        for k in range(nodes):
            values[k * cap : (k + 1) * cap, :] = handed_pieces[k][...]

    set_rows(put_ref, values[...], base, memory_ref)
    serve(ask_ref, memory_ref[...].astype(BF), held, pieces)


def last_kernel(nodes, put_ref, base_ref, *rest):
    pieces, out_ref, values = rest[:nodes], rest[nodes], rest[nodes + 1]
    cap = pieces[0].shape[0]
    for k in range(nodes):
        values[k * cap : (k + 1) * cap, :] = pieces[k][...]
    set_rows(put_ref, values[...], base_ref, out_ref)


def forward_kernel(nodes, ids, dst_ref, time_ref, edge_ref, w_in, w_hid, bias_ref, *rest):
    own_pieces, other_pieces = rest[:nodes], rest[nodes : 2 * nodes]
    fresh_pieces = rest[2 * nodes : 3 * nodes]
    message, reset_ref, update_ref, candid_ref, recur_ref = rest[3 * nodes : 3 * nodes + 5]
    fresh = rest[3 * nodes + 5]
    cap = own_pieces[0].shape[0]
    z, f = ids[0], ids[2]
    mine = pl.multiple_of(f * LANES, LANES)
    other = pl.multiple_of((1 - f) * LANES, LANES)
    for k in range(nodes):
        at = pl.multiple_of((z ^ k) * cap, cap)
        message[pl.ds(at, cap), pl.ds(mine, LANES)] = own_pieces[k][...]
        message[pl.ds(at, cap), pl.ds(other, LANES)] = other_pieces[k][...]
    width = 2 * LANES
    full = message[:, :width]
    events = full.shape[0]
    for j in range(events // LANES):
        row = dst_ref[:, j * LANES : (j + 1) * LANES]
        message[j * LANES : (j + 1) * LANES, width : 2 * width] = pick_rows(row, full)
    message[:, 2 * width : 2 * width + LANES] = time_ref[...]
    message[:, 2 * width + LANES :] = edge_ref[...]
    w_in01 = jnp.concatenate([w_in[0], w_in[1]], axis=1)
    w_hid01 = jnp.concatenate([w_hid[0], w_hid[1]], axis=1)
    tall = 256
    for i in range(events // tall):
        span = slice(i * tall, (i + 1) * tall)
        rows = message[span, :]
        hidden = rows[:, :width]
        both = jnp.dot(rows, w_in01, preferred_element_type=F32) + jnp.dot(
            hidden, w_hid01, preferred_element_type=F32
        )
        own = message[span, pl.ds(mine, LANES)].astype(F32)
        reset_gate = jax.nn.sigmoid(both[:, :LANES] + bias_ref[0:1, :])
        update = jax.nn.sigmoid(both[:, LANES:] + bias_ref[1:2, :])
        recur_term = jnp.dot(hidden, w_hid[2], preferred_element_type=F32) + bias_ref[3:4, :]
        candid = jnp.tanh(
            jnp.dot(rows, w_in[2], preferred_element_type=F32)
            + bias_ref[2:3, :]
            + reset_gate * recur_term
        )
        fresh[span, :] = ((1.0 - update) * candid + update * own).astype(BF)
        reset_ref[span, :] = reset_gate
        update_ref[span, :] = update
        candid_ref[span, :] = candid
        recur_ref[span, :] = recur_term
    for k in range(nodes):
        at = pl.multiple_of((z ^ k) * cap, cap)
        fresh_pieces[k][...] = fresh[pl.ds(at, cap), :]


def backward_kernel(
    nodes, batch, ids, counts, message, reset_ref, update_ref, candid_ref, recur_ref, up_ref, *rest
):
    before = rest[0] if len(rest) == 3 else None
    out_ref, gates = rest[-2:]
    mine = pl.multiple_of(ids[2] * LANES, LANES)
    events = up_ref.shape[0]
    cap = events // nodes
    sums = [jnp.zeros((1, LANES), F32) for _ in range(4)]
    slot = lax.broadcasted_iota(jnp.int32, (cap, LANES), 0)
    for o in range(nodes):
        span = slice(o * cap, (o + 1) * cap)
        cotangent = jnp.where(slot < counts[batch, o], up_ref[span, :].astype(F32), 0.0)
        own = message[span, pl.ds(mine, LANES)].astype(F32)
        reset_gate, update = reset_ref[span, :], update_ref[span, :]
        candid, recur_term = candid_ref[span, :], recur_ref[span, :]
        grad_cand = cotangent * (1.0 - update) * (1.0 - candid * candid)
        grad_upd = cotangent * (own - candid) * update * (1.0 - update)
        grad_reset = grad_cand * recur_term * reset_gate * (1.0 - reset_gate)
        grad_recur = grad_cand * reset_gate
        parts = (grad_reset, grad_upd, grad_cand, grad_recur)
        for g, part in enumerate(parts):
            sums[g] = sums[g] + jnp.sum(part, axis=0, keepdims=True)
            gates[span, g * LANES : (g + 1) * LANES] = part.astype(BF)
    tall = 256
    width = 2 * LANES
    long = message.shape[1]

    def put(start, value):
        stop = start + value.shape[0]
        if before is not None:
            value = value + before[start:stop, :]
        out_ref[start:stop, :] = value.astype(out_ref.dtype)

    for i in range(long // tall):
        rows = message[:, i * tall : (i + 1) * tall]
        columns = gates[...] if i * tall < width else gates[:, : 3 * LANES]
        product = lax.dot_general(
            rows, columns, (((0,), (0,)), ((), ())), preferred_element_type=F32
        )
        for g in range(3):
            put(g * long + i * tall, product[:, g * LANES : (g + 1) * LANES])
        if i * tall < width:
            put(3 * long + i * tall, product[:, 3 * LANES :])
    top = 3 * long + width
    pad = out_ref.shape[0] - top
    tail = jnp.concatenate(sums + [jnp.zeros((pad - 4, LANES), F32)], axis=0)
    put(top, tail)


def unpack_kernel(nodes, segs, long, ids, *rest):
    pieces = rest[:segs]
    grad_in, grad_hid, grad_bias, held = rest[segs:]
    chunk = pieces[0].shape[0] // nodes
    z, s = ids[0], ids[1]
    for x in range(segs):
        for k in range(nodes):
            at = pl.multiple_of(((s ^ x) * nodes + (z ^ k)) * chunk, chunk)
            held[pl.ds(at, chunk), :] = pieces[x][k * chunk : (k + 1) * chunk, :]
    width = grad_hid.shape[1]
    for g in range(3):
        grad_in[g] = held[g * long : (g + 1) * long, :].astype(F32)
    for g in range(2):
        grad_hid[g] = held[g * long : g * long + width, :].astype(F32)
    grad_hid[2] = held[3 * long : 3 * long + width, :].astype(F32)
    top = 3 * long + width
    grad_bias[...] = held[top : top + 16, :].astype(F32)[:4, :]


def local(
    memory, req_rows, req_count, dst_slot, elapsed, edges, upstream, freq, phase, w_input, w_hidden, bias
):
    nodes, segs = lax.axis_size("node"), lax.axis_size("seg")
    z, s, f = lax.axis_index("node"), lax.axis_index("seg"), lax.axis_index("feat")
    ids = jnp.stack([z, s, f]).astype(jnp.int32)
    memory_now = memory[0]
    node_rows, half = memory_now.shape
    batches, cap = req_rows.shape[0], req_rows.shape[-1]
    events = nodes * cap
    counts = req_count[:, 0, 0]
    piece = shape((cap, half), BF)

    def node_swap(block, k):
        return lax.ppermute(block, "node", [(i, i ^ k) for i in range(nodes)])

    def seg_swap(block, x):
        return lax.ppermute(block, "seg", [(i, i ^ x) for i in range(segs)])

    def seg_next(block):
        return lax.ppermute(block, "seg", [(i, i + 1) for i in range(segs - 1)])

    def feat_swap(block):
        return lax.ppermute(block, "feat", [(0, 1), (1, 0)])

    def to_next(block, k):
        route = [
            (i * segs + j, (i ^ k) * segs + j + 1) for i in range(nodes) for j in range(segs - 1)
        ]
        return lax.ppermute(block, ("node", "seg"), route)

    def to_first(block, k):
        route = [(i * segs, (i ^ k) * segs) for i in range(nodes)]
        return lax.ppermute(block, ("node", "seg"), route)

    def exchange(blocks):
        return [blocks[0]] + [node_swap(blocks[k], k) for k in range(1, nodes)]

    wanted = run(
        lambda *refs: ask_kernel(nodes, *refs),
        [shape((batches, cap), jnp.int32)] * nodes,
        [ids, counts],
        [req_rows[:, 0, 0]],
    )
    asked = jnp.concatenate(exchange(wanted), axis=1)
    asked_before = seg_next(asked)

    edge_other = feat_swap(edges[:, 0])
    edge_full = jnp.where(
        f == 0,
        jnp.concatenate([edges[:, 0], edge_other], axis=-1),
        jnp.concatenate([edge_other, edges[:, 0]], axis=-1),
    )
    time_code = jnp.cos(
        elapsed[:, 0].astype(F32)[:, :, None] * freq[None, None, :] + phase[None, None, :]
    ).astype(BF)

    long = w_input.shape[1]
    held = pltpu.VMEM((events, half), BF)
    total_rows = 3 * long + w_hidden.shape[1] + 16
    chunk = -(-total_rows // (16 * nodes * segs)) * 16
    total_rows = chunk * nodes * segs
    totals = None
    served = run(
        lambda *refs: serve_kernel(nodes, *refs),
        [piece] * nodes,
        [],
        [asked[0:1], memory_now],
        [held],
    )
    for b in range(batches):
        final = b + 1 == batches
        own_pieces = exchange(served)
        if not final:
            memory_before = seg_next(memory_now.astype(BF))
        other_pieces = [feat_swap(p) for p in own_pieces]
        gate = shape((events, half), F32)
        outs = run(
            lambda *refs: forward_kernel(nodes, *refs),
            [piece] * nodes + [shape((events, long), BF)] + [gate] * 4,
            [ids],
            [dst_slot[b], time_code[b], edge_full[b], w_input, w_hidden, bias]
            + own_pieces
            + other_pieces,
            [held],
        )
        fresh, kept = outs[:nodes], outs[nodes:]
        if final:
            returned = exchange(fresh)
        else:
            handed = [to_next(fresh[k], k) for k in range(nodes)]
            stayed = [fresh[0]] + [to_first(fresh[k], k) for k in range(1, nodes)]
        totals = run(
            lambda *refs, b=b: backward_kernel(nodes, b, *refs),
            [shape((total_rows, half), BF if final else F32)],
            [ids, counts],
            list(kept) + [upstream[b, 0]] + ([] if totals is None else [totals]),
            [pltpu.VMEM((events, 4 * half), BF)],
        )[0]
        if final:
            memory_out = run(
                lambda *refs: last_kernel(nodes, *refs),
                [shape((node_rows, half), F32)],
                [],
                [asked[b : b + 1], memory_now] + returned,
                [held],
            )[0]
        else:
            put = jnp.where(s == 0, asked[b : b + 1], asked_before[b : b + 1])
            outs = run(
                lambda *refs: next_kernel(nodes, *refs),
                [shape((node_rows, half), F32)] + [piece] * nodes,
                [ids],
                [put, asked[b + 1 : b + 2], memory_now, memory_before] + stayed + handed,
                [held, pltpu.VMEM((node_rows, half), F32), held],
            )
            memory_now, served = outs[0], outs[1:]

    def at(blocks, i):
        return lax.dynamic_index_in_dim(blocks, i, 0, keepdims=False)

    blocks = totals.reshape(segs, nodes * chunk, half)
    got = [seg_swap(at(blocks, s ^ x), x) for x in range(1, segs)]
    summed = sum((g.astype(F32) for g in got), at(blocks, s).astype(F32)).astype(BF)
    blocks = summed.reshape(nodes, chunk, half)
    got = [node_swap(at(blocks, z ^ k), k) for k in range(1, nodes)]
    summed = sum((g.astype(F32) for g in got), at(blocks, z).astype(F32)).astype(BF)
    gathered = jnp.concatenate([summed] + [node_swap(summed, k) for k in range(1, nodes)], axis=0)
    gathered = [gathered] + [seg_swap(gathered, x) for x in range(1, segs)]
    grads = run(
        lambda *refs: unpack_kernel(nodes, segs, long, *refs),
        [shape(w_input.shape, F32), shape(w_hidden.shape, F32), shape(bias.shape, F32)],
        [ids],
        gathered,
        [pltpu.VMEM((total_rows, half), BF)],
    )
    return (memory_out[None], *grads)


def solution(mesh):
    in_specs = (
        P(("parts", "seg"), "node", "feat"),
        P(None, ("parts", "seg"), "node", None, None),
        P(None, ("parts", "seg"), "node", None),
        P(None, ("parts", "seg"), "node"),
        P(None, ("parts", "seg"), "node"),
        P(None, ("parts", "seg"), "node", "feat"),
        P(None, ("parts", "seg"), "node", "feat"),
        P(),
        P(),
        P(None, None, "feat"),
        P(None, None, "feat"),
        P(None, "feat"),
    )
    out_specs = (
        P(("parts", "seg"), "node", "feat"),
        P("parts", None, "feat"),
        P("parts", None, "feat"),
        P("parts", "feat"),
    )
    return jax.shard_map(local, mesh=mesh, in_specs=in_specs, out_specs=out_specs, check_vma=False)
```

```python
import jax
import jax.numpy as jnp
from jax import lax
from jax.experimental import pallas as pl
from jax.experimental.pallas import tpu as pltpu
from jax.sharding import PartitionSpec as P

BF = jnp.bfloat16
F32 = jnp.float32
I32 = jnp.int32
LANES = 128
VMEM = pl.BlockSpec(memory_space=pltpu.VMEM)
SMEM = pl.BlockSpec(memory_space=pltpu.SMEM)
ANY = pl.BlockSpec(memory_space=pl.ANY)


def shape(dims, kind):
    return jax.ShapeDtypeStruct(tuple(dims), kind)


def run(kernel, outs, args, smem=(), scratch=(), copies=1, flops=0):
    counts = (len(smem), len(args), len(outs))

    def body(*refs):
        a, b, c = counts
        scalars, given, made = refs[:a], refs[a : a + b], refs[a + b : a + b + c]
        kernel(refs[-1], scalars, given, made, refs[a + b + c : -1])

    moved = sum(a.size * a.dtype.itemsize for a in list(args) + list(outs))
    return pl.pallas_call(
        body,
        out_shape=list(outs),
        in_specs=[SMEM] * len(smem) + [ANY] * len(args),
        out_specs=[VMEM] * len(outs),
        scratch_shapes=list(scratch) + [pltpu.SemaphoreType.DMA((copies,))],
        compiler_params=pltpu.CompilerParams(vmem_limit_bytes=32 * 1024 * 1024),
        cost_estimate=pl.CostEstimate(flops=flops, bytes_accessed=moved, transcendentals=0),
    )(*smem, *args)


def begin(sems, pairs, first=0):
    copies = [
        pltpu.make_async_copy(source, target, sems.at[first + i])
        for i, (source, target) in enumerate(pairs)
    ]
    for copy in copies:
        copy.start()
    return copies


def end(copies):
    for copy in copies:
        copy.wait()


def down(row):
    return jnp.transpose(jnp.broadcast_to(row, (LANES, LANES)))


def ones_at(where):
    return jnp.where(where, 1.0, 0.0).astype(BF)


def pick_rows(row, source):
    numbers = down(row)
    lane = lax.broadcasted_iota(I32, (LANES, LANES), 1)
    hot = jnp.concatenate(
        [ones_at(numbers == lane + k * LANES) for k in range(source.shape[0] // LANES)], axis=1
    )
    return jnp.dot(hot, source, preferred_element_type=F32).astype(BF)


def set_rows(row, values, base_ref, out_ref):
    events = values.shape[0]
    tall = 256
    wide = jnp.concatenate([values, jnp.ones((events, LANES), BF)], axis=1)
    for i in range(out_ref.shape[0] // tall):
        own = lax.broadcasted_iota(I32, (tall, events), 0) + i * tall
        hot = ones_at(own == jnp.broadcast_to(row, (tall, events)))
        found = jnp.dot(hot, wide, preferred_element_type=F32)
        span = slice(i * tall, (i + 1) * tall)
        out_ref[span, :] = jnp.where(found[:, LANES:] > 0.5, found[:, :LANES], base_ref[span, :])


def padded(cap):
    return -(-cap // LANES) * LANES


def ask_kernel(sems, smem, given, pieces, scratch):
    (ids, counts), (rows_any,), (rows_ref,) = smem, given, scratch
    end(begin(sems, [(rows_any, rows_ref)]))
    batches, _, cap = rows_ref.shape
    slot = lax.broadcasted_iota(I32, (1, cap), 1)
    for k, piece in enumerate(pieces):
        owner = ids[0] ^ k
        if piece.shape[1] != cap:
            piece[...] = jnp.full(piece.shape, -1, I32)
        for b in range(batches):
            row = rows_ref[b, pl.ds(owner, 1), :]
            piece[b : b + 1, :cap] = jnp.where(slot < counts[b, owner], row, -1)


def give(held, pieces):
    cap = pieces[0].shape[0]
    room = padded(cap)
    for k, piece in enumerate(pieces):
        piece[...] = held[k * room : k * room + cap, :]


def serve_kernel(sems, smem, given, made, scratch):
    *asked_pieces, memory_any = given
    asked_ref, narrow_ref, *pieces = made
    memory_ref, held = scratch
    nodes, room = len(asked_pieces), asked_pieces[0].shape[1]
    pairs = [(memory_any, memory_ref)]
    for k, piece in enumerate(asked_pieces):
        pairs.append((piece, asked_ref.at[:, k * room : (k + 1) * room]))
    end(begin(sems, pairs))
    narrow_ref[...] = memory_ref[...].astype(BF)
    for j in range(nodes * room // LANES):
        span = slice(j * LANES, (j + 1) * LANES)
        held[span, :] = pick_rows(asked_ref[0:1, span], narrow_ref[...])
    give(held, pieces)


def base_kernel(batch, sems, smem, given, made, scratch):
    (ids,) = smem
    asked_any, before_any, memory_any, handed_any = given
    base_ref, put_ref, rows_ref = made
    asked, before, handed, narrow = scratch
    begun = begin(
        sems,
        [(asked_any, asked), (before_any, before), (memory_any, base_ref), (handed_any, handed)],
    )
    end(begun)
    row = slice(batch, batch + 1)
    put_ref[...] = jnp.where(ids[1] == 0, asked[row, :], before[row, :])

    @pl.when(ids[1] != 0)
    def _():
        base_ref[...] = handed[...].astype(F32)

    narrow[...] = base_ref[...].astype(BF)
    for j in range(rows_ref.shape[0] // LANES):
        span = slice(j * LANES, (j + 1) * LANES)
        rows_ref[span, :] = pick_rows(asked[batch + 1 : batch + 2, span], narrow[...])


def gather_values(values, cap, pieces, sems, first):
    room = padded(cap)
    if room != cap:
        values[...] = jnp.zeros(values.shape, values.dtype)
    pairs = [(piece, values.at[k * room : k * room + cap, :]) for k, piece in enumerate(pieces)]
    return begin(sems, pairs, first)


def next_kernel(nodes, batch, sems, smem, given, made, scratch):
    (ids,) = smem
    asked_any, put_any, rows_any = given[:3]
    stayed, handed = given[3 : 3 + nodes], given[3 + nodes :]
    values_ref, pieces = made[0], made[1:]
    asked, put, rows, held = scratch
    cap = pieces[0].shape[0]
    begun = begin(sems, [(asked_any, asked), (put_any, put), (rows_any, rows)])

    @pl.when(ids[1] == 0)
    def _():
        end(gather_values(values_ref, cap, stayed, sems, 3))

    @pl.when(ids[1] != 0)
    def _():
        end(gather_values(values_ref, cap, handed, sems, 3))

    end(begun)
    events = values_ref.shape[0]
    wide = jnp.concatenate([values_ref[...], jnp.ones((events, LANES), BF)], axis=1)
    written = jnp.where(put[...] < 0, -2, put[...])
    for j in range(events // LANES):
        span = slice(j * LANES, (j + 1) * LANES)
        numbers = down(asked[batch + 1 : batch + 2, span])
        hot = jnp.concatenate(
            [
                ones_at(
                    numbers
                    == jnp.broadcast_to(written[:, i * LANES : (i + 1) * LANES], (LANES, LANES))
                )
                for i in range(events // LANES)
            ],
            axis=1,
        )
        found = jnp.dot(hot, wide, preferred_element_type=F32)
        kept = rows[span, :].astype(F32)
        held[span, :] = jnp.where(found[:, LANES:] > 0.5, found[:, :LANES], kept).astype(BF)
    give(held, pieces)


def update_kernel(sems, smem, given, made, scratch):
    put_any, values_any, base_any = given
    put, values, base = scratch
    end(begin(sems, [(put_any, put), (values_any, values), (base_any, base)]))
    set_rows(put[...], values[...], base, made[0])


def last_kernel(batch, sems, smem, given, made, scratch):
    asked_any, base_any, *pieces = given
    asked, values, base = scratch
    begun = begin(sems, [(asked_any, asked), (base_any, base)])
    end(gather_values(values, pieces[0].shape[0], pieces, sems, 2))
    end(begun)
    set_rows(asked[batch : batch + 1, :], values[...], base, made[0])


def batch_kernel(nodes, batch, forward, backward, prior, sems, smem, given, made, scratch):
    ids, counts = smem
    dst_any, time_any, edge_any, w_in_any, w_hid_any, bias_any = given[:6]
    own_pieces, other_pieces = given[6 : 6 + nodes], given[6 + nodes : 6 + 2 * nodes]
    rest = given[6 + 2 * nodes :]
    message, dst, w_in, w_hid, bias_ref, fresh = scratch[:6]
    cap = own_pieces[0].shape[0]
    events = nodes * cap
    z, f = ids[0], ids[2]
    mine = pl.multiple_of(f * LANES, LANES)
    other = pl.multiple_of((1 - f) * LANES, LANES)
    width = 2 * LANES
    long = message.shape[1]
    pairs = [(dst_any.at[batch], dst)]
    for k in range(nodes):
        at = pl.ds(pl.multiple_of((z ^ k) * cap, cap), cap)
        pairs.append((own_pieces[k], message.at[at, pl.ds(mine, LANES)]))
        pairs.append((other_pieces[k], message.at[at, pl.ds(other, LANES)]))
    rows_begun = begin(sems, pairs)
    pairs2 = [
        (w_in_any, w_in),
        (w_hid_any, w_hid),
        (bias_any, bias_ref),
        (time_any.at[batch], message.at[:, 2 * width : 2 * width + LANES]),
        (edge_any.at[batch], message.at[:, 2 * width + LANES :]),
    ]
    begun = begin(sems, pairs2, len(pairs))
    if backward:
        gates, up = scratch[6:8]
        last_pairs = [(rest[0].at[batch], up)]
        if prior:
            before = scratch[8]
            last_pairs.append((rest[1], before))
        last_begun = begin(sems, last_pairs, len(pairs) + len(pairs2))
    end(rows_begun)
    full = message[:, :width]
    for j in range(events // LANES):
        span = slice(j * LANES, (j + 1) * LANES)
        message[span, width : 2 * width] = pick_rows(dst[:, span], full)
    end(begun)
    w_in01 = jnp.concatenate([w_in[0], w_in[1]], axis=1)
    w_hid01 = jnp.concatenate([w_hid[0], w_hid[1]], axis=1)
    sums = [jnp.zeros((1, LANES), F32) for _ in range(4)]
    if backward:
        end(last_begun)
    tall = 256
    for i in range(events // tall):
        span = slice(i * tall, (i + 1) * tall)
        rows = message[span, :]
        hidden = rows[:, :width]
        both = jnp.dot(rows, w_in01, preferred_element_type=F32) + jnp.dot(
            hidden, w_hid01, preferred_element_type=F32
        )
        own = message[span, pl.ds(mine, LANES)].astype(F32)
        reset_gate = jax.nn.sigmoid(both[:, :LANES] + bias_ref[0:1, :])
        update = jax.nn.sigmoid(both[:, LANES:] + bias_ref[1:2, :])
        recur_term = jnp.dot(hidden, w_hid[2], preferred_element_type=F32) + bias_ref[3:4, :]
        candid = jnp.tanh(
            jnp.dot(rows, w_in[2], preferred_element_type=F32)
            + bias_ref[2:3, :]
            + reset_gate * recur_term
        )
        if forward:
            fresh[span, :] = ((1.0 - update) * candid + update * own).astype(BF)
        if backward:
            number = lax.broadcasted_iota(I32, (tall, LANES), 0) + i * tall
            live = number < 0
            for o in range(nodes):
                if o * cap < (i + 1) * tall and (o + 1) * cap > i * tall:
                    live = live | (
                        (number >= o * cap) & (number < o * cap + counts[batch, o])
                    )
            cotangent = jnp.where(live, up[span, :].astype(F32), 0.0)
            grad_cand = cotangent * (1.0 - update) * (1.0 - candid * candid)
            grad_upd = cotangent * (own - candid) * update * (1.0 - update)
            grad_reset = grad_cand * recur_term * reset_gate * (1.0 - reset_gate)
            grad_recur = grad_cand * reset_gate
            for g, part in enumerate((grad_reset, grad_upd, grad_cand, grad_recur)):
                sums[g] = sums[g] + jnp.sum(part, axis=0, keepdims=True)
                gates[span, g * LANES : (g + 1) * LANES] = part.astype(BF)
    if forward:
        for k in range(nodes):
            made[k][...] = fresh[pl.ds(pl.multiple_of((z ^ k) * cap, cap), cap), :]
    if not backward:
        return
    out_ref = made[-1]

    def put(start, value):
        stop = start + value.shape[0]
        if prior:
            value = value + before[start:stop, :]
        out_ref[start:stop, :] = value.astype(out_ref.dtype)

    for i in range(long // tall):
        rows = message[:, i * tall : (i + 1) * tall]
        columns = gates[...] if i * tall < width else gates[:, : 3 * LANES]
        product = lax.dot_general(
            rows, columns, (((0,), (0,)), ((), ())), preferred_element_type=F32
        )
        for g in range(3):
            put(g * long + i * tall, product[:, g * LANES : (g + 1) * LANES])
        if i * tall < width:
            put(3 * long + i * tall, product[:, 3 * LANES :])
    top = 3 * long + width
    pad = out_ref.shape[0] - top
    tail = jnp.concatenate(sums + [jnp.zeros((pad - 4, LANES), F32)], axis=0)
    put(top, tail)


def middle_kernel(segs, sems, smem, given, made, scratch):
    (ids,) = smem
    totals, got = given[0], given[1:segs]
    rows = scratch[:segs]
    whole = scratch[segs]
    nodes, chunk = len(made), made[0].shape[0]
    share = nodes * chunk
    at = pl.ds(pl.multiple_of(ids[1] * share, share), share)
    pairs = [(totals.at[at, :], rows[0])] + list(zip(got, rows[1:]))
    end(begin(sems, pairs))
    total = rows[0][...].astype(F32)
    for x in range(1, segs):
        total = total + rows[x][...].astype(F32)
    whole[...] = total.astype(BF)
    for k in range(nodes):
        made[k][...] = whole[pl.ds(pl.multiple_of((ids[0] ^ k) * chunk, chunk), chunk), :]


def unpack_kernel(nodes, segs, long, sems, smem, pieces, made, scratch):
    (ids,) = smem
    grad_in, grad_hid, grad_bias = made
    (held,) = scratch
    chunk = pieces[0].shape[0] // nodes
    z, s = ids[0], ids[1]
    pairs = []
    for x in range(segs):
        for k in range(nodes):
            at = pl.multiple_of(((s ^ x) * nodes + (z ^ k)) * chunk, chunk)
            pairs.append((pieces[x].at[k * chunk : (k + 1) * chunk, :], held.at[pl.ds(at, chunk), :]))
    end(begin(sems, pairs))
    width = grad_hid.shape[1]
    for g in range(3):
        grad_in[g] = held[g * long : (g + 1) * long, :].astype(F32)
    for g in range(2):
        grad_hid[g] = held[g * long : g * long + width, :].astype(F32)
    grad_hid[2] = held[3 * long : 3 * long + width, :].astype(F32)
    top = 3 * long + width
    grad_bias[...] = held[top : top + 16, :].astype(F32)[:4, :]


def local(
    memory, req_rows, req_count, dst_slot, elapsed, edges, upstream, freq, phase, w_input, w_hidden, bias
):
    nodes, segs = lax.axis_size("node"), lax.axis_size("seg")
    z, s, f = lax.axis_index("node"), lax.axis_index("seg"), lax.axis_index("feat")
    ids = jnp.stack([z, s, f]).astype(I32)
    memory_now = memory[0]
    node_rows, half = memory_now.shape
    batches, cap = req_rows.shape[0], req_rows.shape[-1]
    events = nodes * cap
    room = padded(cap)
    spread = nodes * room
    counts = req_count[:, 0, 0]
    piece = shape((cap, half), BF)
    long, width = w_input.shape[1], w_hidden.shape[1]

    def node_swap(block, k):
        return lax.ppermute(block, "node", [(i, i ^ k) for i in range(nodes)])

    def seg_swap(block, x):
        return lax.ppermute(block, "seg", [(i, i ^ x) for i in range(segs)])

    def seg_next(block):
        return lax.ppermute(block, "seg", [(i, i + 1) for i in range(segs - 1)])

    def feat_swap(block):
        return lax.ppermute(block, "feat", [(0, 1), (1, 0)])

    def to_next(block, k):
        route = [
            (i * segs + j, (i ^ k) * segs + j + 1) for i in range(nodes) for j in range(segs - 1)
        ]
        return lax.ppermute(block, ("node", "seg"), route)

    def to_first(block, k):
        route = [(i * segs, (i ^ k) * segs) for i in range(nodes)]
        return lax.ppermute(block, ("node", "seg"), route)

    def exchange(blocks):
        return [blocks[0]] + [node_swap(blocks[k], k) for k in range(1, nodes)]

    wanted = run(
        ask_kernel,
        [shape((batches, room), I32)] * nodes,
        [req_rows[:, 0, 0]],
        [ids, counts],
        [pltpu.VMEM((batches, nodes, cap), I32)],
    )
    wide_rows = pltpu.VMEM((spread, half), BF)
    asked, narrow, *served = run(
        serve_kernel,
        [shape((batches, spread), I32), shape((node_rows, half), BF)] + [piece] * nodes,
        exchange(wanted) + [memory_now],
        [],
        [pltpu.VMEM((node_rows, half), F32), wide_rows],
        nodes + 1,
    )
    asked_before = seg_next(asked)

    edge_other = feat_swap(edges[:, 0])
    edge_full = jnp.where(
        f == 0,
        jnp.concatenate([edges[:, 0], edge_other], axis=-1),
        jnp.concatenate([edge_other, edges[:, 0]], axis=-1),
    )
    time_code = jnp.cos(
        elapsed[:, 0].astype(F32)[:, :, None] * freq[None, None, :] + phase[None, None, :]
    ).astype(BF)

    chunk = -(-(3 * long + width + 16) // (16 * nodes * segs)) * 16
    total_rows = chunk * nodes * segs
    numbers = pltpu.VMEM((batches, spread), I32)
    line = pltpu.VMEM((1, spread), I32)
    block = pltpu.VMEM((node_rows, half), F32)
    totals = None
    for b in range(batches):
        final = b + 1 == batches
        own_pieces = exchange(served)
        if not final:
            handed_memory = seg_next(narrow)
        other_pieces = [feat_swap(p) for p in own_pieces]
        given = [dst_slot, time_code, edge_full, w_input, w_hidden, bias]
        given = given + own_pieces + other_pieces
        rooms = [
            pltpu.VMEM((events, long), BF),
            pltpu.VMEM((1, events), I32),
            pltpu.VMEM(w_input.shape, BF),
            pltpu.VMEM(w_hidden.shape, BF),
            pltpu.VMEM(bias.shape, F32),
            pltpu.VMEM((events, half), BF),
        ]
        more = [pltpu.VMEM((events, 4 * half), BF), pltpu.VMEM((events, half), BF)]
        if totals is not None:
            more.append(pltpu.VMEM((total_rows, half), F32))
        copies = 8 + 2 * nodes
        prior = [] if totals is None else [totals]
        if not final:
            fresh = run(
                lambda *a, b=b: batch_kernel(nodes, b, True, False, False, *a),
                [piece] * nodes,
                given,
                [ids, counts],
                rooms,
                copies,
            )
            handed = [to_next(fresh[k], k) for k in range(nodes)]
            stayed = [fresh[0]] + [to_first(fresh[k], k) for k in range(1, nodes)]
            base, put, rows = run(
                lambda *a, b=b: base_kernel(b, *a),
                [shape((node_rows, half), F32), shape((1, spread), I32), shape((spread, half), BF)],
                [asked, asked_before, memory_now, handed_memory],
                [ids],
                [numbers, numbers, pltpu.VMEM((node_rows, half), BF)] + [pltpu.VMEM((node_rows, half), BF)],
                4,
            )
            values, *served = run(
                lambda *a, b=b: next_kernel(nodes, b, *a),
                [shape((spread, half), BF)] + [piece] * nodes,
                [asked, put, rows] + stayed + handed,
                [ids],
                [numbers, line, wide_rows, wide_rows],
                3 + nodes,
            )
            memory_now = run(
                update_kernel,
                [shape((node_rows, half), F32)],
                [put, values, base],
                [],
                [line, wide_rows, block],
                3,
            )[0]
            narrow = memory_now.astype(BF)
            totals = run(
                lambda *a, b=b, p=prior: batch_kernel(nodes, b, False, True, len(p) > 0, *a),
                [shape((total_rows, half), F32)],
                given + [upstream[:, 0]] + prior + [handed[0]],
                [ids, counts],
                rooms + more,
                copies,
            )[0]
        else:
            *fresh, totals = run(
                lambda *a, b=b, p=prior: batch_kernel(nodes, b, True, True, len(p) > 0, *a),
                [piece] * nodes + [shape((total_rows, half), BF)],
                given + [upstream[:, 0]] + prior,
                [ids, counts],
                rooms + more,
                copies,
            )
            returned = exchange(fresh)
            memory_out = run(
                lambda *a, b=b: last_kernel(b, *a),
                [shape((node_rows, half), F32)],
                [asked, memory_now] + returned,
                [],
                [numbers, wide_rows, block],
                2 + nodes,
            )[0]

    def at(blocks, i):
        return lax.dynamic_index_in_dim(blocks, i, 0, keepdims=False)

    blocks = totals.reshape(segs, nodes * chunk, half)
    got = [seg_swap(at(blocks, s ^ x), x) for x in range(1, segs)]
    share = pltpu.VMEM((nodes * chunk, half), BF)
    parts = run(
        lambda *a: middle_kernel(segs, *a),
        [shape((chunk, half), BF)] * nodes,
        [totals] + got + returned[1:],
        [ids],
        [share] * (segs + 1),
        segs,
    )
    got = [node_swap(parts[k], k) for k in range(1, nodes)]
    summed = sum((g.astype(F32) for g in got), parts[0].astype(F32)).astype(BF)
    gathered = jnp.concatenate([summed] + [node_swap(summed, k) for k in range(1, nodes)], axis=0)
    gathered = [gathered] + [seg_swap(gathered, x) for x in range(1, segs)]
    grads = run(
        lambda *a: unpack_kernel(nodes, segs, long, *a),
        [shape(w_input.shape, F32), shape(w_hidden.shape, F32), shape(bias.shape, F32)],
        gathered,
        [ids],
        [pltpu.VMEM((total_rows, half), BF)],
        nodes * segs,
    )
    return (memory_out[None], *grads)


def solution(mesh):
    in_specs = (
        P(("parts", "seg"), "node", "feat"),
        P(None, ("parts", "seg"), "node", None, None),
        P(None, ("parts", "seg"), "node", None),
        P(None, ("parts", "seg"), "node"),
        P(None, ("parts", "seg"), "node"),
        P(None, ("parts", "seg"), "node", "feat"),
        P(None, ("parts", "seg"), "node", "feat"),
        P(),
        P(),
        P(None, None, "feat"),
        P(None, None, "feat"),
        P(None, "feat"),
    )
    out_specs = (
        P(("parts", "seg"), "node", "feat"),
        P("parts", None, "feat"),
        P("parts", None, "feat"),
        P("parts", "feat"),
    )
    return jax.shard_map(local, mesh=mesh, in_specs=in_specs, out_specs=out_specs, check_vma=False)
```

```python
import jax
import jax.numpy as jnp
from jax import lax
from jax.experimental import pallas as pl
from jax.experimental.pallas import tpu as pltpu
from jax.sharding import PartitionSpec as P

BF = jnp.bfloat16
F32 = jnp.float32
I32 = jnp.int32
LANES = 128
VMEM = pl.BlockSpec(memory_space=pltpu.VMEM)
ANY = pl.BlockSpec(memory_space=pl.ANY)


def shape(dims, kind):
    return jax.ShapeDtypeStruct(tuple(dims), kind)


def run(kernel, outs, args, scratch=(), copies=1, flops=0):
    b, c = len(args), len(outs)

    def body(*refs):
        kernel(refs[-1], refs[:b], refs[b : b + c], refs[b + c : -1])

    moved = sum(a.size * a.dtype.itemsize for a in list(args) + list(outs))
    return pl.pallas_call(
        body,
        out_shape=list(outs),
        in_specs=[ANY] * len(args),
        out_specs=[VMEM] * len(outs),
        scratch_shapes=list(scratch) + [pltpu.SemaphoreType.DMA((copies,))],
        compiler_params=pltpu.CompilerParams(vmem_limit_bytes=56 * 1024 * 1024),
        cost_estimate=pl.CostEstimate(flops=flops, bytes_accessed=moved, transcendentals=0),
    )(*args)


def begin(sems, pairs, first=0):
    copies = [
        pltpu.make_async_copy(source, target, sems.at[first + i])
        for i, (source, target) in enumerate(pairs)
    ]
    for copy in copies:
        copy.start()
    return copies


def end(copies):
    for copy in copies:
        copy.wait()


def down(row):
    return jnp.transpose(jnp.broadcast_to(row, (LANES, LANES)))


def ones_at(where):
    return jnp.where(where, 1.0, 0.0).astype(BF)


def pick_rows(row, source):
    numbers = down(row)
    lane = lax.broadcasted_iota(I32, (LANES, LANES), 1)
    hot = jnp.concatenate(
        [ones_at(numbers == lane + k * LANES) for k in range(source.shape[0] // LANES)], axis=1
    )
    return jnp.dot(hot, source, preferred_element_type=F32).astype(BF)


def set_rows(row, values, base_ref, out_ref):
    events = values.shape[0]
    tall = 256
    wide = jnp.concatenate([values, jnp.ones((events, LANES), BF)], axis=1)
    for i in range(out_ref.shape[0] // tall):
        own = lax.broadcasted_iota(I32, (tall, events), 0) + i * tall
        hot = ones_at(own == jnp.broadcast_to(row, (tall, events)))
        found = jnp.dot(hot, wide, preferred_element_type=F32)
        span = slice(i * tall, (i + 1) * tall)
        out_ref[span, :] = jnp.where(found[:, LANES:] > 0.5, found[:, :LANES], base_ref[span, :])


def padded(cap):
    return -(-cap // LANES) * LANES


def ask_kernel(sems, given, pieces, scratch):
    rows_any, counts_any = given
    rows_ref, counts = scratch
    end(begin(sems, [(rows_any, rows_ref), (counts_any, counts)]))
    z = lax.axis_index("node")
    batches, _, cap = rows_ref.shape
    slot = lax.broadcasted_iota(I32, (1, cap), 1)
    for k, piece in enumerate(pieces):
        owner = z ^ k
        if piece.shape[1] != cap:
            piece[...] = jnp.full(piece.shape, -1, I32)
        for b in range(batches):
            row = rows_ref[b, pl.ds(owner, 1), :]
            piece[b : b + 1, :cap] = jnp.where(slot < counts[b, owner], row, -1)


def give(held, pieces):
    cap = pieces[0].shape[0]
    room = padded(cap)
    for k, piece in enumerate(pieces):
        piece[...] = held[k * room : k * room + cap, :]


def serve_kernel(sems, given, made, scratch):
    *asked_pieces, memory_any = given
    asked_ref, narrow_ref, *pieces = made
    memory_ref, held = scratch
    nodes, room = len(asked_pieces), asked_pieces[0].shape[1]
    pairs = [(memory_any, memory_ref)]
    for k, piece in enumerate(asked_pieces):
        pairs.append((piece, asked_ref.at[:, k * room : (k + 1) * room]))
    end(begin(sems, pairs))
    narrow_ref[...] = memory_ref[...].astype(BF)
    for j in range(nodes * room // LANES):
        span = slice(j * LANES, (j + 1) * LANES)
        held[span, :] = pick_rows(asked_ref[0:1, span], narrow_ref[...])
    give(held, pieces)


def base_kernel(batch, sems, given, made, scratch):
    asked_any, before_any, memory_any, handed_any = given
    base_ref, put_ref, rows_ref = made
    asked, before, handed, narrow = scratch
    begun = begin(
        sems,
        [(asked_any, asked), (before_any, before), (memory_any, base_ref), (handed_any, handed)],
    )
    end(begun)
    row = slice(batch, batch + 1)
    put_ref[...] = jnp.where(lax.axis_index("seg") == 0, asked[row, :], before[row, :])

    @pl.when(lax.axis_index("seg") != 0)
    def _():
        base_ref[...] = handed[...].astype(F32)

    narrow[...] = base_ref[...].astype(BF)
    for j in range(rows_ref.shape[0] // LANES):
        span = slice(j * LANES, (j + 1) * LANES)
        rows_ref[span, :] = pick_rows(asked[batch + 1 : batch + 2, span], narrow[...])


def gather_values(values, cap, pieces, sems, first):
    room = padded(cap)
    if room != cap:
        values[...] = jnp.zeros(values.shape, values.dtype)
    pairs = [(piece, values.at[k * room : k * room + cap, :]) for k, piece in enumerate(pieces)]
    return begin(sems, pairs, first)


def handed_kernel(sems, given, pieces, scratch):
    z = lax.axis_index("node")
    cap = pieces[0].shape[0]

    def send(source):
        pairs = []
        for k, piece in enumerate(pieces):
            at = pl.multiple_of((z ^ k) * cap, cap)
            pairs.append((source.at[pl.ds(at, cap), :], piece))
        end(begin(sems, pairs))

    @pl.when(lax.axis_index("seg") == 0)
    def _():
        send(given[0])

    @pl.when(lax.axis_index("seg") != 0)
    def _():
        send(given[1])


def next_kernel(batch, sems, given, made, scratch):
    asked_any, put_any, rows_any = given[:3]
    values_ref, pieces = made[0], made[1:]
    asked, put, rows, held = scratch
    cap = pieces[0].shape[0]
    begun = begin(sems, [(asked_any, asked), (put_any, put), (rows_any, rows)])
    end(gather_values(values_ref, cap, given[3:], sems, 3))
    end(begun)
    events = values_ref.shape[0]
    wide = jnp.concatenate([values_ref[...], jnp.ones((events, LANES), BF)], axis=1)
    written = jnp.where(put[...] < 0, -2, put[...])
    for j in range(events // LANES):
        span = slice(j * LANES, (j + 1) * LANES)
        numbers = down(asked[batch + 1 : batch + 2, span])
        hot = jnp.concatenate(
            [
                ones_at(
                    numbers
                    == jnp.broadcast_to(written[:, i * LANES : (i + 1) * LANES], (LANES, LANES))
                )
                for i in range(events // LANES)
            ],
            axis=1,
        )
        found = jnp.dot(hot, wide, preferred_element_type=F32)
        kept = rows[span, :].astype(F32)
        held[span, :] = jnp.where(found[:, LANES:] > 0.5, found[:, :LANES], kept).astype(BF)
    give(held, pieces)


def update_kernel(sems, given, made, scratch):
    put_any, values_any, base_any = given
    put, values, base = scratch
    end(begin(sems, [(put_any, put), (values_any, values), (base_any, base)]))
    set_rows(put[...], values[...], base, made[0])


def last_kernel(batch, sems, given, made, scratch):
    asked_any, base_any, *pieces = given
    asked, values, base = scratch
    begun = begin(sems, [(asked_any, asked), (base_any, base)])
    end(gather_values(values, pieces[0].shape[0], pieces, sems, 2))
    end(begun)
    set_rows(asked[batch : batch + 1, :], values[...], base, made[0])


def cosine(x):
    turns = jnp.round(x * 0.3183098861837907)
    r = x - turns * 3.140625
    r = r - turns * 0.0009670257568359375
    r = r - turns * 6.278329573009626e-07
    odd = turns - 2.0 * jnp.floor(turns * 0.5)
    q = r * r
    p = 2.08767569878681e-09 - q * 1.1470745597729725e-11
    p = q * p - 2.7557319223985893e-07
    p = q * p + 2.48015873015873e-05
    p = q * p - 0.001388888888888889
    p = q * p + 0.041666666666666664
    p = q * p - 0.5
    p = q * p + 1.0
    return p * (1.0 - 2.0 * odd)


def batch_kernel(nodes, batch, final, sems, given, made, scratch):
    dst_any, elapsed_any, edge_any, edge_other_any, w_in_any, w_hid_any, bias_any = given[:7]
    freq_any, phase_any, counts_any, up_any = given[7:11]
    own_pieces, other_pieces = given[11 : 11 + nodes], given[11 + nodes : 11 + 2 * nodes]
    rest = given[11 + 2 * nodes :]
    prior = len(rest) > 0
    message, dst, elapsed, edge, w_in, w_hid, bias_ref, freq, phase, counts = scratch[:10]
    gates, up, fresh = scratch[10:13]
    cap = own_pieces[0].shape[0]
    events = nodes * cap
    z, f = lax.axis_index("node"), lax.axis_index("feat")
    mine = pl.multiple_of(f * LANES, LANES)
    other = pl.multiple_of((1 - f) * LANES, LANES)
    width = 2 * LANES
    long = message.shape[1]
    thin = edge_any.shape[1]
    pairs = [(dst_any.at[batch], dst)]
    for k in range(nodes):
        at = pl.ds(pl.multiple_of((z ^ k) * cap, cap), cap)
        pairs.append((own_pieces[k], message.at[at, pl.ds(mine, LANES)]))
        pairs.append((other_pieces[k], message.at[at, pl.ds(other, LANES)]))
    early = [
        (elapsed_any.at[batch], elapsed),
        (freq_any, freq),
        (phase_any, phase),
        (edge_any.at[batch], edge.at[pl.ds(pl.multiple_of(f * thin, thin), thin), :]),
        (edge_other_any.at[batch], edge.at[pl.ds(pl.multiple_of((1 - f) * thin, thin), thin), :]),
    ]
    late = [(w_in_any, w_in), (w_hid_any, w_hid), (bias_any, bias_ref), (counts_any, counts)]
    late.append((up_any.at[batch], up))
    if prior:
        before = scratch[13]
        late.append((rest[0], before))
    rows_begun = begin(sems, pairs)
    early_begun = begin(sems, early, len(pairs))
    late_begun = begin(sems, late, len(pairs) + len(early))
    end(early_begun)
    for j in range(events // LANES):
        span = slice(j * LANES, (j + 1) * LANES)
        angle = down(elapsed[:, span].astype(F32)) * freq[...] + phase[...]
        message[span, 2 * width : 2 * width + LANES] = cosine(angle).astype(BF)
        message[span, 2 * width + LANES :] = jnp.transpose(edge[:, span].astype(F32)).astype(BF)
    end(rows_begun)
    full = message[:, :width]
    for j in range(events // LANES):
        span = slice(j * LANES, (j + 1) * LANES)
        message[span, width : 2 * width] = pick_rows(dst[:, span], full)
    end(late_begun)
    w_in01 = jnp.concatenate([w_in[0], w_in[1]], axis=1)
    w_hid01 = jnp.concatenate([w_hid[0], w_hid[1]], axis=1)
    sums = [jnp.zeros((1, LANES), F32) for _ in range(4)]
    tall = 256
    for i in range(events // tall):
        span = slice(i * tall, (i + 1) * tall)
        rows = message[span, :]
        hidden = rows[:, :width]
        both = jnp.dot(rows, w_in01, preferred_element_type=F32) + jnp.dot(
            hidden, w_hid01, preferred_element_type=F32
        )
        own = message[span, pl.ds(mine, LANES)].astype(F32)
        reset_gate = jax.nn.sigmoid(both[:, :LANES] + bias_ref[0:1, :])
        update = jax.nn.sigmoid(both[:, LANES:] + bias_ref[1:2, :])
        recur_term = jnp.dot(hidden, w_hid[2], preferred_element_type=F32) + bias_ref[3:4, :]
        candid = jnp.tanh(
            jnp.dot(rows, w_in[2], preferred_element_type=F32)
            + bias_ref[2:3, :]
            + reset_gate * recur_term
        )
        fresh[span, :] = ((1.0 - update) * candid + update * own).astype(BF)
        number = lax.broadcasted_iota(I32, (tall, LANES), 0) + i * tall
        live = number < 0
        for o in range(nodes):
            if o * cap < (i + 1) * tall and (o + 1) * cap > i * tall:
                live = live | ((number >= o * cap) & (number < o * cap + counts[batch, o]))
        cotangent = jnp.where(live, up[span, :].astype(F32), 0.0)
        grad_cand = cotangent * (1.0 - update) * (1.0 - candid * candid)
        grad_upd = cotangent * (own - candid) * update * (1.0 - update)
        grad_reset = grad_cand * recur_term * reset_gate * (1.0 - reset_gate)
        grad_recur = grad_cand * reset_gate
        for g, part in enumerate((grad_reset, grad_upd, grad_cand, grad_recur)):
            sums[g] = sums[g] + jnp.sum(part, axis=0, keepdims=True)
            gates[span, g * LANES : (g + 1) * LANES] = part.astype(BF)
    if final:
        for k in range(nodes):
            made[k][...] = fresh[pl.ds(pl.multiple_of((z ^ k) * cap, cap), cap), :]
    else:
        made[0][...] = fresh[...]
    out_ref = made[-1]

    def put(start, value):
        stop = start + value.shape[0]
        if prior:
            value = value + before[start:stop, :]
        out_ref[start:stop, :] = value.astype(out_ref.dtype)

    for i in range(long // tall):
        rows = message[:, i * tall : (i + 1) * tall]
        columns = gates[...] if i * tall < width else gates[:, : 3 * LANES]
        product = lax.dot_general(
            rows, columns, (((0,), (0,)), ((), ())), preferred_element_type=F32
        )
        for g in range(3):
            put(g * long + i * tall, product[:, g * LANES : (g + 1) * LANES])
        if i * tall < width:
            put(3 * long + i * tall, product[:, 3 * LANES :])
    top = 3 * long + width
    pad = out_ref.shape[0] - top
    tail = jnp.concatenate(sums + [jnp.zeros((pad - 4, LANES), F32)], axis=0)
    put(top, tail)


def middle_kernel(segs, sems, given, made, scratch):
    totals, got = given[0], given[1:segs]
    rows = scratch[:segs]
    whole = scratch[segs]
    nodes, chunk = len(made), made[0].shape[0]
    share = nodes * chunk
    at = pl.ds(pl.multiple_of(lax.axis_index("seg") * share, share), share)
    pairs = [(totals.at[at, :], rows[0])] + list(zip(got, rows[1:]))
    end(begin(sems, pairs))
    total = rows[0][...].astype(F32)
    for x in range(1, segs):
        total = total + rows[x][...].astype(F32)
    whole[...] = total.astype(BF)
    for k in range(nodes):
        made[k][...] = whole[pl.ds(pl.multiple_of((lax.axis_index("node") ^ k) * chunk, chunk), chunk), :]


def unpack_kernel(nodes, segs, long, sems, pieces, made, scratch):
    grad_in, grad_hid, grad_bias = made
    (held,) = scratch
    chunk = pieces[0].shape[0] // nodes
    z, s = lax.axis_index("node"), lax.axis_index("seg")
    pairs = []
    for x in range(segs):
        for k in range(nodes):
            at = pl.multiple_of(((s ^ x) * nodes + (z ^ k)) * chunk, chunk)
            pairs.append((pieces[x].at[k * chunk : (k + 1) * chunk, :], held.at[pl.ds(at, chunk), :]))
    end(begin(sems, pairs))
    width = grad_hid.shape[1]
    for g in range(3):
        grad_in[g] = held[g * long : (g + 1) * long, :].astype(F32)
    for g in range(2):
        grad_hid[g] = held[g * long : g * long + width, :].astype(F32)
    grad_hid[2] = held[3 * long : 3 * long + width, :].astype(F32)
    top = 3 * long + width
    grad_bias[...] = held[top : top + 16, :].astype(F32)[:4, :]


def local(
    memory, req_rows, req_count, dst_slot, elapsed, edges, upstream, freq, phase, w_input, w_hidden, bias
):
    nodes, segs = lax.axis_size("node"), lax.axis_size("seg")
    z, s = lax.axis_index("node"), lax.axis_index("seg")
    memory_now = memory[0]
    node_rows, half = memory_now.shape
    batches, cap = req_rows.shape[0], req_rows.shape[-1]
    events = nodes * cap
    room = padded(cap)
    spread = nodes * room
    counts = req_count[:, 0, 0]
    piece = shape((cap, half), BF)
    long, width = w_input.shape[1], w_hidden.shape[1]

    def node_swap(block, k):
        return lax.ppermute(block, "node", [(i, i ^ k) for i in range(nodes)])

    def seg_swap(block, x):
        return lax.ppermute(block, "seg", [(i, i ^ x) for i in range(segs)])

    def seg_next(block):
        return lax.ppermute(block, "seg", [(i, i + 1) for i in range(segs - 1)])

    def feat_swap(block):
        return lax.ppermute(block, "feat", [(0, 1), (1, 0)])

    def exchange(blocks):
        return [blocks[0]] + [node_swap(blocks[k], k) for k in range(1, nodes)]

    wanted = run(
        ask_kernel,
        [shape((batches, room), I32)] * nodes,
        [req_rows[:, 0, 0], counts],
        [pltpu.VMEM((batches, nodes, cap), I32), pltpu.SMEM((batches, nodes), I32)],
        2,
    )
    wide_rows = pltpu.VMEM((spread, half), BF)
    asked, narrow, *served = run(
        serve_kernel,
        [shape((batches, spread), I32), shape((node_rows, half), BF)] + [piece] * nodes,
        exchange(wanted) + [memory_now],
        [pltpu.VMEM((node_rows, half), F32), wide_rows],
        nodes + 1,
    )
    asked_before = seg_next(asked)

    edge_own = jnp.swapaxes(edges[:, 0], 1, 2)
    edge_other = feat_swap(edge_own)

    chunk = -(-(3 * long + width + 16) // (16 * nodes * segs)) * 16
    total_rows = chunk * nodes * segs
    numbers = pltpu.VMEM((batches, spread), I32)
    line = pltpu.VMEM((1, spread), I32)
    block = pltpu.VMEM((node_rows, half), F32)
    totals = None
    for b in range(batches):
        final = b + 1 == batches
        own_pieces = exchange(served)
        if not final:
            handed_memory = seg_next(narrow)
        other_pieces = [feat_swap(p) for p in own_pieces]
        given = [dst_slot, elapsed, edge_own, edge_other, w_input, w_hidden, bias]
        given = given + [freq[None], phase[None], counts, upstream[:, 0]]
        given = given + own_pieces + other_pieces + ([] if totals is None else [totals])
        rooms = [
            pltpu.VMEM((events, long), BF),
            pltpu.VMEM((1, events), I32),
            pltpu.VMEM((1, events), I32),
            pltpu.VMEM((2 * edges.shape[-1], events), BF),
            pltpu.VMEM(w_input.shape, BF),
            pltpu.VMEM(w_hidden.shape, BF),
            pltpu.VMEM(bias.shape, F32),
            pltpu.VMEM((1, freq.shape[0]), F32),
            pltpu.VMEM((1, freq.shape[0]), F32),
            pltpu.SMEM((batches, nodes), I32),
            pltpu.VMEM((events, 4 * half), BF),
            pltpu.VMEM((events, half), BF),
            pltpu.VMEM((events, half), BF),
        ]
        if totals is not None:
            rooms.append(pltpu.VMEM((total_rows, half), F32))
        copies = 12 + 2 * nodes
        *fresh, totals = run(
            lambda *a, b=b, last=final: batch_kernel(nodes, b, last, *a),
            ([piece] * nodes if final else [shape((events, half), BF)])
            + [shape((total_rows, half), BF if final else F32)],
            given,
            rooms,
            copies,
        )
        if not final:
            values = run(handed_kernel, [piece] * nodes, [fresh[0], seg_next(fresh[0])], [], nodes)
            values = exchange(values)
            base, put, rows = run(
                lambda *a, b=b: base_kernel(b, *a),
                [shape((node_rows, half), F32), shape((1, spread), I32), shape((spread, half), BF)],
                [asked, asked_before, memory_now, handed_memory],
                [numbers, numbers] + [pltpu.VMEM((node_rows, half), BF)] * 2,
                4,
            )
            values, *served = run(
                lambda *a, b=b: next_kernel(b, *a),
                [shape((spread, half), BF)] + [piece] * nodes,
                [asked, put, rows] + values,
                [numbers, line, wide_rows, wide_rows],
                3 + nodes,
            )
            memory_now = run(
                update_kernel,
                [shape((node_rows, half), F32)],
                [put, values, base],
                [line, wide_rows, block],
                3,
            )[0]
            narrow = memory_now.astype(BF)
        else:
            returned = exchange(fresh)
            memory_out = run(
                lambda *a, b=b: last_kernel(b, *a),
                [shape((node_rows, half), F32)],
                [asked, memory_now] + returned,
                [numbers, wide_rows, block],
                2 + nodes,
            )[0]

    def at(blocks, i):
        return lax.dynamic_index_in_dim(blocks, i, 0, keepdims=False)

    blocks = totals.reshape(segs, nodes * chunk, half)
    got = [seg_swap(at(blocks, s ^ x), x) for x in range(1, segs)]
    share = pltpu.VMEM((nodes * chunk, half), BF)
    parts = run(
        lambda *a: middle_kernel(segs, *a),
        [shape((chunk, half), BF)] * nodes,
        [totals] + got + returned[1:],
        [share] * (segs + 1),
        segs,
    )
    got = [node_swap(parts[k], k) for k in range(1, nodes)]
    summed = sum((g.astype(F32) for g in got), parts[0].astype(F32)).astype(BF)
    gathered = jnp.concatenate([summed] + [node_swap(summed, k) for k in range(1, nodes)], axis=0)
    gathered = [gathered] + [seg_swap(gathered, x) for x in range(1, segs)]
    grads = run(
        lambda *a: unpack_kernel(nodes, segs, long, *a),
        [shape(w_input.shape, F32), shape(w_hidden.shape, F32), shape(bias.shape, F32)],
        gathered,
        [pltpu.VMEM((total_rows, half), BF)],
        nodes * segs,
    )
    return (memory_out[None], *grads)


def solution(mesh):
    in_specs = (
        P(("parts", "seg"), "node", "feat"),
        P(None, ("parts", "seg"), "node", None, None),
        P(None, ("parts", "seg"), "node", None),
        P(None, ("parts", "seg"), "node"),
        P(None, ("parts", "seg"), "node"),
        P(None, ("parts", "seg"), "node", "feat"),
        P(None, ("parts", "seg"), "node", "feat"),
        P(),
        P(),
        P(None, None, "feat"),
        P(None, None, "feat"),
        P(None, "feat"),
    )
    out_specs = (
        P(("parts", "seg"), "node", "feat"),
        P("parts", None, "feat"),
        P("parts", None, "feat"),
        P("parts", "feat"),
    )
    return jax.shard_map(local, mesh=mesh, in_specs=in_specs, out_specs=out_specs, check_vma=False)
```

```python
import jax
import jax.numpy as jnp
from jax import lax
from jax.experimental import pallas as pl
from jax.experimental.pallas import tpu as pltpu
from jax.sharding import PartitionSpec as P

BF = jnp.bfloat16
F32 = jnp.float32
I32 = jnp.int32
LANES = 128
VMEM = pl.BlockSpec(memory_space=pltpu.VMEM)
ANY = pl.BlockSpec(memory_space=pl.ANY)
HBM = pl.BlockSpec(memory_space=pltpu.HBM)


def shape(dims, kind):
    return jax.ShapeDtypeStruct(tuple(dims), kind)


def run(kernel, outs, args, scratch=(), copies=1, far=()):
    b, c = len(args), len(outs)

    def body(*refs):
        kernel(refs[-1], refs[:b], refs[b : b + c], refs[b + c : -1])

    moved = sum(a.size * a.dtype.itemsize for a in list(args) + list(outs))
    return pl.pallas_call(
        body,
        out_shape=list(outs),
        in_specs=[HBM if i in far else ANY for i in range(len(args))],
        out_specs=[VMEM] * len(outs),
        scratch_shapes=list(scratch) + [pltpu.SemaphoreType.DMA((copies,))],
        compiler_params=pltpu.CompilerParams(vmem_limit_bytes=24 * 1024 * 1024),
        cost_estimate=pl.CostEstimate(flops=0, bytes_accessed=moved, transcendentals=0),
    )(*args)


def begin(sems, pairs, first=0):
    copies = [
        pltpu.make_async_copy(source, target, sems.at[first + i])
        for i, (source, target) in enumerate(pairs)
    ]
    for copy in copies:
        copy.start()
    return copies


def end(copies):
    for copy in copies:
        copy.wait()


def down(row):
    return jnp.transpose(jnp.broadcast_to(row, (LANES, LANES)))


def ones_at(where):
    return jnp.where(where, 1.0, 0.0).astype(BF)


def pick_rows(row, source):
    numbers = down(row)
    lane = lax.broadcasted_iota(I32, (LANES, LANES), 1)
    hot = jnp.concatenate(
        [ones_at(numbers == lane + k * LANES) for k in range(source.shape[0] // LANES)], axis=1
    )
    return jnp.dot(hot, source, preferred_element_type=F32).astype(BF)


def set_rows(row, values, base_ref, out_ref):
    events = values.shape[0]
    tall = 256
    wide = jnp.concatenate([values, jnp.ones((events, LANES), BF)], axis=1)
    for i in range(out_ref.shape[0] // tall):
        own = lax.broadcasted_iota(I32, (tall, events), 0) + i * tall
        hot = ones_at(own == jnp.broadcast_to(row, (tall, events)))
        found = jnp.dot(hot, wide, preferred_element_type=F32)
        span = slice(i * tall, (i + 1) * tall)
        out_ref[span, :] = jnp.where(found[:, LANES:] > 0.5, found[:, :LANES], base_ref[span, :])


def padded(cap):
    return -(-cap // LANES) * LANES


def give(held, pieces):
    cap = pieces[0].shape[0]
    room = padded(cap)
    for k, piece in enumerate(pieces):
        piece[...] = held[k * room : k * room + cap, :]


def narrow_kernel(sems, given, made, scratch):
    end(begin(sems, [(given[0], scratch[0])]))
    made[0][...] = scratch[0][...].astype(BF)


def bundle_kernel(batch, sems, given, made, scratch):
    narrow_any, asked_any = given
    (out_ref,), (asked,) = made, scratch
    rows = narrow_any.shape[0]
    end(begin(sems, [(narrow_any, out_ref.at[:rows, :]), (asked_any, asked)]))
    lines = (out_ref.shape[0] - rows) // 2
    number = jnp.concatenate(
        [asked[batch : batch + 1, j * LANES : (j + 1) * LANES] for j in range(lines)], axis=0
    )
    high = jnp.floor(number.astype(F32) * (1.0 / 64.0))
    low = number.astype(F32) - 64.0 * high
    out_ref[rows:, :] = jnp.concatenate([high, low], axis=0).astype(BF)


def serve_kernel(sems, given, made, scratch):
    *asked_pieces, narrow_any = given
    asked_ref, *pieces = made
    narrow, held = scratch
    nodes, room = len(asked_pieces), asked_pieces[0].shape[1]
    pairs = [(narrow_any, narrow)]
    for k, piece in enumerate(asked_pieces):
        pairs.append((piece, asked_ref.at[:, k * room : (k + 1) * room]))
    end(begin(sems, pairs))
    for j in range(nodes * room // LANES):
        span = slice(j * LANES, (j + 1) * LANES)
        held[span, :] = pick_rows(asked_ref[0:1, span], narrow[...])
    give(held, pieces)


def pick_base(sems, memory_any, handed_any, base_ref, handed_ref, first):
    @pl.when(lax.axis_index("seg") == 0)
    def _():
        end(begin(sems, [(memory_any, base_ref)], first))

    @pl.when(lax.axis_index("seg") != 0)
    def _():
        end(begin(sems, [(handed_any, handed_ref)], first))
        base_ref[...] = handed_ref[: base_ref.shape[0], :].astype(base_ref.dtype)


def base_kernel(batch, sems, given, made, scratch):
    asked_any, narrow_any, handed_any = given
    put_ref, rows_ref = made
    asked, handed, narrow = scratch
    begun = begin(sems, [(asked_any, asked)])
    pick_base(sems, narrow_any, handed_any, narrow, handed, 1)
    end(begun)
    put_ref[...] = asked[batch : batch + 1, :]

    @pl.when(lax.axis_index("seg") != 0)
    def _():
        top = narrow.shape[0]
        lines = (handed.shape[0] - top) // 2
        digits = handed[top:, :].astype(F32)
        number = digits[:lines, :] * 64.0 + digits[lines:, :]
        for j in range(lines):
            put_ref[:, j * LANES : (j + 1) * LANES] = number[j : j + 1, :].astype(I32)

    for j in range(rows_ref.shape[0] // LANES):
        span = slice(j * LANES, (j + 1) * LANES)
        rows_ref[span, :] = pick_rows(asked[batch + 1 : batch + 2, span], narrow[...])


def gather_values(values, cap, pieces, sems, first):
    room = padded(cap)
    if room != cap:
        values[...] = jnp.zeros(values.shape, values.dtype)
    pairs = [(piece, values.at[k * room : k * room + cap, :]) for k, piece in enumerate(pieces)]
    return begin(sems, pairs, first)


def handed_kernel(sems, given, pieces, scratch):
    z = lax.axis_index("node")
    cap = pieces[0].shape[0]

    def send(source):
        pairs = []
        for k, piece in enumerate(pieces):
            at = pl.multiple_of((z ^ k) * cap, cap)
            pairs.append((source.at[pl.ds(at, cap), :], piece))
        end(begin(sems, pairs))

    @pl.when(lax.axis_index("seg") == 0)
    def _():
        send(given[0])

    @pl.when(lax.axis_index("seg") != 0)
    def _():
        send(given[1])


def next_kernel(batch, sems, given, made, scratch):
    asked_any, put_any, rows_any = given[:3]
    values_ref, pieces = made[0], made[1:]
    asked, put, rows, held = scratch
    cap = pieces[0].shape[0]
    begun = begin(sems, [(asked_any, asked), (put_any, put), (rows_any, rows)])
    end(gather_values(values_ref, cap, given[3:], sems, 3))
    end(begun)
    events = values_ref.shape[0]
    wide = jnp.concatenate([values_ref[...], jnp.ones((events, LANES), BF)], axis=1)
    written = jnp.where(put[...] < 0, -2, put[...])
    for j in range(events // LANES):
        span = slice(j * LANES, (j + 1) * LANES)
        numbers = down(asked[batch + 1 : batch + 2, span])
        hot = jnp.concatenate(
            [
                ones_at(
                    numbers
                    == jnp.broadcast_to(written[:, i * LANES : (i + 1) * LANES], (LANES, LANES))
                )
                for i in range(events // LANES)
            ],
            axis=1,
        )
        found = jnp.dot(hot, wide, preferred_element_type=F32)
        kept = rows[span, :].astype(F32)
        held[span, :] = jnp.where(found[:, LANES:] > 0.5, found[:, :LANES], kept).astype(BF)
    give(held, pieces)


def update_kernel(sems, given, made, scratch):
    put_any, values_any, memory_any, handed_any = given
    put, values, base, handed = scratch
    begun = begin(sems, [(put_any, put), (values_any, values)])
    pick_base(sems, memory_any, handed_any, base, handed, 2)
    end(begun)
    set_rows(put[...], values[...], base, made[0])


def last_kernel(batch, sems, given, made, scratch):
    asked_any, base_any, *pieces = given
    asked, values, base = scratch
    begun = begin(sems, [(asked_any, asked), (base_any, base)])
    end(gather_values(values, pieces[0].shape[0], pieces, sems, 2))
    end(begun)
    set_rows(asked[batch : batch + 1, :], values[...], base, made[0])


def cosine(x):
    turns = jnp.round(x * 0.3183098861837907)
    r = x - turns * 3.140625
    r = r - turns * 0.0009670257568359375
    r = r - turns * 6.278329573009626e-07
    odd = turns - 2.0 * jnp.floor(turns * 0.5)
    q = r * r
    p = 2.08767569878681e-09 - q * 1.1470745597729725e-11
    p = q * p - 2.7557319223985893e-07
    p = q * p + 2.48015873015873e-05
    p = q * p - 0.001388888888888889
    p = q * p + 0.041666666666666664
    p = q * p - 0.5
    p = q * p + 1.0
    return p * (1.0 - 2.0 * odd)


def batch_kernel(nodes, batch, final, prior, sems, given, made, scratch):
    facts_any, edge_any, edge_other_any, w_in_any, w_hid_any, up_any = given[:6]
    own_pieces, other_pieces = given[6 : 6 + nodes], given[6 + nodes : 6 + 2 * nodes]
    rest = given[6 + 2 * nodes :]
    message, facts, edge, w_in, w_hid, gates, up, fresh = scratch[:8]
    cap = own_pieces[0].shape[0]
    events = nodes * cap
    z, f = lax.axis_index("node"), lax.axis_index("feat")
    mine = pl.multiple_of(f * LANES, LANES)
    other = pl.multiple_of((1 - f) * LANES, LANES)
    width = 2 * LANES
    long = message.shape[1]
    thin = edge_any.shape[1]
    pairs = []
    for k in range(nodes):
        at = pl.ds(pl.multiple_of((z ^ k) * cap, cap), cap)
        pairs.append((own_pieces[k], message.at[at, pl.ds(mine, LANES)]))
        pairs.append((other_pieces[k], message.at[at, pl.ds(other, LANES)]))
    early = [
        (facts_any, facts),
        (edge_any.at[batch], edge.at[pl.ds(pl.multiple_of(f * thin, thin), thin), :]),
        (edge_other_any.at[batch], edge.at[pl.ds(pl.multiple_of((1 - f) * thin, thin), thin), :]),
    ]
    late = [(w_in_any, w_in), (w_hid_any, w_hid), (up_any.at[batch], up)]
    if prior:
        before = scratch[8]
        late.append((rest[0], before))
    rows_begun = begin(sems, pairs)
    early_begun = begin(sems, early, len(pairs))
    late_begun = begin(sems, late, len(pairs) + len(early))
    end(early_begun)
    lines = events // LANES
    top = facts.shape[0] - 8
    bias_ref = facts[top : top + 4, :]
    freq, phase = facts[top + 4 : top + 5, :], facts[top + 5 : top + 6, :]
    dst = [facts[2 * lines * batch + j : 2 * lines * batch + j + 1, :] for j in range(lines)]
    start = 2 * lines * batch + lines
    for j in range(lines):
        span = slice(j * LANES, (j + 1) * LANES)
        angle = down(facts[start + j : start + j + 1, :]) * freq + phase
        message[span, 2 * width : 2 * width + LANES] = cosine(angle).astype(BF)
        message[span, 2 * width + LANES :] = jnp.transpose(edge[:, span].astype(F32)).astype(BF)
    end(rows_begun)
    full = message[:, :width]
    for j in range(events // LANES):
        span = slice(j * LANES, (j + 1) * LANES)
        message[span, width : 2 * width] = pick_rows(dst[j].astype(I32), full)
    end(late_begun)
    w_in01 = jnp.concatenate([w_in[0], w_in[1]], axis=1)
    w_hid01 = jnp.concatenate([w_hid[0], w_hid[1]], axis=1)
    sums = [jnp.zeros((1, LANES), F32) for _ in range(4)]
    tall = 256
    for i in range(events // tall):
        span = slice(i * tall, (i + 1) * tall)
        rows = message[span, :]
        hidden = rows[:, :width]
        both = jnp.dot(rows, w_in01, preferred_element_type=F32) + jnp.dot(
            hidden, w_hid01, preferred_element_type=F32
        )
        own = message[span, pl.ds(mine, LANES)].astype(F32)
        reset_gate = jax.nn.sigmoid(both[:, :LANES] + bias_ref[0:1, :])
        update = jax.nn.sigmoid(both[:, LANES:] + bias_ref[1:2, :])
        recur_term = jnp.dot(hidden, w_hid[2], preferred_element_type=F32) + bias_ref[3:4, :]
        candid = jnp.tanh(
            jnp.dot(rows, w_in[2], preferred_element_type=F32)
            + bias_ref[2:3, :]
            + reset_gate * recur_term
        )
        fresh[span, :] = ((1.0 - update) * candid + update * own).astype(BF)
        numbers = [down(dst[j]) for j in range(i * tall // LANES, (i + 1) * tall // LANES)]
        live = jnp.concatenate(numbers, axis=0) >= 0.0
        cotangent = jnp.where(live, up[span, :].astype(F32), 0.0)
        grad_cand = cotangent * (1.0 - update) * (1.0 - candid * candid)
        grad_upd = cotangent * (own - candid) * update * (1.0 - update)
        grad_reset = grad_cand * recur_term * reset_gate * (1.0 - reset_gate)
        grad_recur = grad_cand * reset_gate
        for g, part in enumerate((grad_reset, grad_upd, grad_cand, grad_recur)):
            sums[g] = sums[g] + jnp.sum(part, axis=0, keepdims=True)
            gates[span, g * LANES : (g + 1) * LANES] = part.astype(BF)
    if final:
        for k in range(nodes):
            made[k][...] = fresh[pl.ds(pl.multiple_of((z ^ k) * cap, cap), cap), :]
    else:
        made[0][...] = fresh[...]
    out_ref = made[-1]

    def put(start, value):
        stop = start + value.shape[0]
        if prior:
            value = value + before[start:stop, :]
        out_ref[start:stop, :] = value.astype(out_ref.dtype)

    for i in range(long // tall):
        rows = message[:, i * tall : (i + 1) * tall]
        columns = gates[...] if i * tall < width else gates[:, : 3 * LANES]
        product = lax.dot_general(
            rows, columns, (((0,), (0,)), ((), ())), preferred_element_type=F32
        )
        for g in range(3):
            put(g * long + i * tall, product[:, g * LANES : (g + 1) * LANES])
        if i * tall < width:
            put(3 * long + i * tall, product[:, 3 * LANES :])
    top = 3 * long + width
    pad = out_ref.shape[0] - top
    tail = jnp.concatenate(sums + [jnp.zeros((pad - 4, LANES), F32)], axis=0)
    put(top, tail)


def middle_kernel(segs, sems, given, made, scratch):
    totals, got = given[0], given[1:segs]
    rows = scratch[:segs]
    whole = scratch[segs]
    nodes, chunk = len(made), made[0].shape[0]
    share = nodes * chunk
    at = pl.ds(pl.multiple_of(lax.axis_index("seg") * share, share), share)
    pairs = [(totals.at[at, :], rows[0])] + list(zip(got, rows[1:]))
    end(begin(sems, pairs))
    total = rows[0][...].astype(F32)
    for x in range(1, segs):
        total = total + rows[x][...].astype(F32)
    whole[...] = total.astype(BF)
    for k in range(nodes):
        made[k][...] = whole[pl.ds(pl.multiple_of((lax.axis_index("node") ^ k) * chunk, chunk), chunk), :]


def unpack_kernel(nodes, segs, long, sems, pieces, made, scratch):
    grad_in, grad_hid, grad_bias = made
    (held,) = scratch
    chunk = pieces[0].shape[0] // nodes
    z, s = lax.axis_index("node"), lax.axis_index("seg")
    pairs = []
    for x in range(segs):
        for k in range(nodes):
            at = pl.multiple_of(((s ^ x) * nodes + (z ^ k)) * chunk, chunk)
            pairs.append((pieces[x].at[k * chunk : (k + 1) * chunk, :], held.at[pl.ds(at, chunk), :]))
    end(begin(sems, pairs))
    width = grad_hid.shape[1]
    for g in range(3):
        grad_in[g] = held[g * long : (g + 1) * long, :].astype(F32)
    for g in range(2):
        grad_hid[g] = held[g * long : g * long + width, :].astype(F32)
    grad_hid[2] = held[3 * long : 3 * long + width, :].astype(F32)
    top = 3 * long + width
    grad_bias[...] = held[top : top + 16, :].astype(F32)[:4, :]


def local(
    memory, req_rows, req_count, dst_slot, elapsed, edges, upstream, freq, phase, w_input, w_hidden, bias
):
    nodes, segs = lax.axis_size("node"), lax.axis_size("seg")
    z, s = lax.axis_index("node"), lax.axis_index("seg")
    memory_now = memory[0]
    node_rows, half = memory_now.shape
    batches, cap = req_rows.shape[0], req_rows.shape[-1]
    events = nodes * cap
    room = padded(cap)
    spread = nodes * room
    counts = req_count[:, 0, 0]
    piece = shape((cap, half), BF)
    long, width = w_input.shape[1], w_hidden.shape[1]

    def node_swap(block, k):
        return lax.ppermute(block, "node", [(i, i ^ k) for i in range(nodes)])

    def seg_swap(block, x):
        return lax.ppermute(block, "seg", [(i, i ^ x) for i in range(segs)])

    def seg_next(block):
        return lax.ppermute(block, "seg", [(i, i + 1) for i in range(segs - 1)])

    def feat_swap(block):
        return lax.ppermute(block, "feat", [(0, 1), (1, 0)])

    def exchange(blocks):
        return [blocks[0]] + [node_swap(blocks[k], k) for k in range(1, nodes)]

    live = jnp.arange(cap)[None, None, :] < counts[:, :, None]
    masked = jnp.where(live, req_rows[:, 0, 0], -1)
    masked = jnp.pad(masked, ((0, 0), (0, 0), (0, room - cap)), constant_values=-1)
    wanted = exchange(
        [lax.dynamic_index_in_dim(masked, z ^ k, 1, keepdims=False) for k in range(nodes)]
    )
    wide_rows = pltpu.VMEM((spread, half), BF)
    edge_own = jnp.swapaxes(edges[:, 0], 1, 2)
    edge_other = feat_swap(edge_own)
    lines = events // LANES
    named = jnp.where(live, dst_slot[:, 0].reshape(live.shape), -1)
    facts = jnp.stack([named.reshape(batches, events), elapsed[:, 0]], axis=1).astype(F32)
    facts = facts.reshape(batches * 2 * lines, LANES)
    rest = jnp.zeros((2, half), F32)
    facts = jnp.concatenate([facts, bias, freq[None], phase[None], rest], axis=0)

    narrow = run(
        narrow_kernel,
        [shape((node_rows, half), BF)],
        [memory_now, wanted[1], facts],
        [pltpu.VMEM((node_rows, half), F32)],
        1,
        (0,),
    )[0]
    asked, *served = run(
        serve_kernel,
        [shape((batches, spread), I32)] + [piece] * nodes,
        wanted + [narrow],
        [pltpu.VMEM((node_rows, half), BF), wide_rows],
        nodes + 1,
    )

    chunk = -(-(3 * long + width + 16) // (16 * nodes * segs)) * 16
    total_rows = chunk * nodes * segs
    numbers = pltpu.VMEM((batches, spread), I32)
    line = pltpu.VMEM((1, spread), I32)
    block = pltpu.VMEM((node_rows, half), F32)
    totals = None
    for b in range(batches):
        final = b + 1 == batches
        own_pieces = exchange(served)
        if not final:
            bundle = run(
                lambda *a, b=b: bundle_kernel(b, *a),
                [shape((node_rows + 2 * spread // LANES, half), BF)],
                [narrow, asked],
                [numbers],
                2,
            )[0]
            handed_memory = seg_next(bundle)
        other_pieces = [feat_swap(p) for p in own_pieces]
        given = [facts, edge_own, edge_other, w_input, w_hidden, upstream[:, 0]]
        given = given + own_pieces + other_pieces + ([] if totals is None else [totals])
        rooms = [
            pltpu.VMEM((events, long), BF),
            pltpu.VMEM(facts.shape, F32),
            pltpu.VMEM((2 * edges.shape[-1], events), BF),
            pltpu.VMEM(w_input.shape, BF),
            pltpu.VMEM(w_hidden.shape, BF),
            pltpu.VMEM((events, 4 * half), BF),
            pltpu.VMEM((events, half), BF),
            pltpu.VMEM((events, half), BF),
        ]
        if totals is not None:
            rooms.append(pltpu.VMEM((total_rows, half), F32))
        copies = 7 + 2 * nodes
        *fresh, totals = run(
            lambda *a, b=b, last=final, p=totals is not None: batch_kernel(nodes, b, last, p, *a),
            ([piece] * nodes if final else [shape((events, half), BF)])
            + [shape((total_rows, half), BF if final else F32)],
            given,
            rooms,
            copies,
            (1, 3, 4, 5),
        )
        if not final:
            hop = seg_next(fresh[0])
            put, rows = run(
                lambda *a, b=b: base_kernel(b, *a),
                [shape((1, spread), I32), shape((spread, half), BF)],
                [asked, narrow, handed_memory],
                [numbers, pltpu.VMEM(bundle.shape, BF), pltpu.VMEM((node_rows, half), BF)],
                2,
            )
            values = run(
                handed_kernel, [piece] * nodes, [fresh[0], hop, rows], [], nodes
            )
            values = exchange(values)
            values, *served = run(
                lambda *a, b=b: next_kernel(b, *a),
                [shape((spread, half), BF)] + [piece] * nodes,
                [asked, put, rows] + values,
                [numbers, line, wide_rows, wide_rows],
                3 + nodes,
            )
            memory_now = run(
                update_kernel,
                [shape((node_rows, half), F32)],
                [put, values, memory_now, handed_memory],
                [line, wide_rows, block, pltpu.VMEM(bundle.shape, BF)],
                3,
            )[0]
            if b + 2 < batches:
                narrow = memory_now.astype(BF)
        else:
            returned = exchange(fresh)
            memory_out = run(
                lambda *a, b=b: last_kernel(b, *a),
                [shape((node_rows, half), F32)],
                [asked, memory_now] + returned,
                [numbers, wide_rows, block],
                2 + nodes,
            )[0]

    def at(blocks, i):
        return lax.dynamic_index_in_dim(blocks, i, 0, keepdims=False)

    blocks = totals.reshape(segs, nodes * chunk, half)
    got = [seg_swap(at(blocks, s ^ x), x) for x in range(1, segs)]
    share = pltpu.VMEM((nodes * chunk, half), BF)
    parts = run(
        lambda *a: middle_kernel(segs, *a),
        [shape((chunk, half), BF)] * nodes,
        [totals] + got + returned[1:],
        [share] * (segs + 1),
        segs,
    )
    got = [node_swap(parts[k], k) for k in range(1, nodes)]
    summed = sum((g.astype(F32) for g in got), parts[0].astype(F32)).astype(BF)
    gathered = jnp.concatenate([summed] + [node_swap(summed, k) for k in range(1, nodes)], axis=0)
    gathered = [gathered] + [seg_swap(gathered, x) for x in range(1, segs)]
    grads = run(
        lambda *a: unpack_kernel(nodes, segs, long, *a),
        [shape(w_input.shape, F32), shape(w_hidden.shape, F32), shape(bias.shape, F32)],
        gathered,
        [pltpu.VMEM((total_rows, half), BF)],
        nodes * segs,
    )
    return (memory_out[None], *grads)


def solution(mesh):
    in_specs = (
        P(("parts", "seg"), "node", "feat"),
        P(None, ("parts", "seg"), "node", None, None),
        P(None, ("parts", "seg"), "node", None),
        P(None, ("parts", "seg"), "node"),
        P(None, ("parts", "seg"), "node"),
        P(None, ("parts", "seg"), "node", "feat"),
        P(None, ("parts", "seg"), "node", "feat"),
        P(),
        P(),
        P(None, None, "feat"),
        P(None, None, "feat"),
        P(None, "feat"),
    )
    out_specs = (
        P(("parts", "seg"), "node", "feat"),
        P("parts", None, "feat"),
        P("parts", None, "feat"),
        P("parts", "feat"),
    )
    return jax.shard_map(local, mesh=mesh, in_specs=in_specs, out_specs=out_specs, check_vma=False)
```

```python
import jax
import jax.numpy as jnp
from jax import lax
from jax.experimental import pallas as pl
from jax.experimental.pallas import tpu as pltpu
from jax.sharding import PartitionSpec as P

BF = jnp.bfloat16
F32 = jnp.float32
I32 = jnp.int32
LANES = 128
VMEM = pl.BlockSpec(memory_space=pltpu.VMEM)
ANY = pl.BlockSpec(memory_space=pl.ANY)
HBM = pl.BlockSpec(memory_space=pltpu.HBM)


def shape(dims, kind):
    return jax.ShapeDtypeStruct(tuple(dims), kind)


def run(kernel, outs, args, scratch=(), copies=1, far=()):
    b, c = len(args), len(outs)

    def body(*refs):
        kernel(refs[-1], refs[:b], refs[b : b + c], refs[b + c : -1])

    moved = sum(a.size * a.dtype.itemsize for a in list(args) + list(outs))
    return pl.pallas_call(
        body,
        out_shape=list(outs),
        in_specs=[HBM if i in far else ANY for i in range(len(args))],
        out_specs=[VMEM] * len(outs),
        scratch_shapes=list(scratch) + [pltpu.SemaphoreType.DMA((copies,))],
        compiler_params=pltpu.CompilerParams(vmem_limit_bytes=24 * 1024 * 1024),
        cost_estimate=pl.CostEstimate(flops=0, bytes_accessed=moved, transcendentals=0),
    )(*args)


def begin(sems, pairs, first=0):
    copies = [
        pltpu.make_async_copy(source, target, sems.at[first + i])
        for i, (source, target) in enumerate(pairs)
    ]
    for copy in copies:
        copy.start()
    return copies


def end(copies):
    for copy in copies:
        copy.wait()


def down(row):
    return jnp.transpose(jnp.broadcast_to(row, (LANES, LANES)))


def ones_at(where):
    return jnp.where(where, 1.0, 0.0).astype(BF)


def pick_rows(row, source):
    numbers = down(row)
    lane = lax.broadcasted_iota(I32, (LANES, LANES), 1)
    hot = jnp.concatenate(
        [ones_at(numbers == lane + k * LANES) for k in range(source.shape[0] // LANES)], axis=1
    )
    return jnp.dot(hot, source, preferred_element_type=F32).astype(BF)


def set_rows(row, values, base_ref, out_ref):
    events = values.shape[0]
    tall = 256
    wide = jnp.concatenate([values, jnp.ones((events, LANES), BF)], axis=1)
    for i in range(out_ref.shape[0] // tall):
        own = lax.broadcasted_iota(I32, (tall, events), 0) + i * tall
        hot = ones_at(own == jnp.broadcast_to(row, (tall, events)))
        found = jnp.dot(hot, wide, preferred_element_type=F32)
        span = slice(i * tall, (i + 1) * tall)
        out_ref[span, :] = jnp.where(found[:, LANES:] > 0.5, found[:, :LANES], base_ref[span, :])


def padded(cap):
    return -(-cap // LANES) * LANES


def give(held, pieces):
    cap = pieces[0].shape[0]
    room = padded(cap)
    for k, piece in enumerate(pieces):
        piece[...] = held[k * room : k * room + cap, :]


def narrow_kernel(sems, given, made, scratch):
    end(begin(sems, [(given[0], scratch[0])]))
    made[0][...] = scratch[0][...].astype(BF)


def bundle_kernel(batch, sems, given, made, scratch):
    narrow_any, asked_any = given
    (out_ref,), (asked,) = made, scratch
    rows = narrow_any.shape[0]
    end(begin(sems, [(narrow_any, out_ref.at[:rows, :]), (asked_any, asked)]))
    lines = (out_ref.shape[0] - rows) // 2
    number = jnp.concatenate(
        [asked[batch : batch + 1, j * LANES : (j + 1) * LANES] for j in range(lines)], axis=0
    )
    high = jnp.floor(number.astype(F32) * (1.0 / 64.0))
    low = number.astype(F32) - 64.0 * high
    out_ref[rows:, :] = jnp.concatenate([high, low], axis=0).astype(BF)


def serve_kernel(sems, given, made, scratch):
    *asked_pieces, narrow_any = given
    asked_ref, *pieces = made
    narrow, held = scratch
    nodes, room = len(asked_pieces), asked_pieces[0].shape[1]
    pairs = [(narrow_any, narrow)]
    for k, piece in enumerate(asked_pieces):
        pairs.append((piece, asked_ref.at[:, k * room : (k + 1) * room]))
    end(begin(sems, pairs))
    for j in range(nodes * room // LANES):
        span = slice(j * LANES, (j + 1) * LANES)
        held[span, :] = pick_rows(asked_ref[0:1, span], narrow[...])
    give(held, pieces)


def pick_base(sems, memory_any, handed_any, base_ref, handed_ref, first):
    @pl.when(lax.axis_index("seg") == 0)
    def _():
        end(begin(sems, [(memory_any, base_ref)], first))

    @pl.when(lax.axis_index("seg") != 0)
    def _():
        end(begin(sems, [(handed_any, handed_ref)], first))
        base_ref[...] = handed_ref[: base_ref.shape[0], :].astype(base_ref.dtype)


def base_kernel(batch, sems, given, made, scratch):
    asked_any, narrow_any, handed_any = given
    put_ref, rows_ref = made
    asked, handed, narrow = scratch
    begun = begin(sems, [(asked_any, asked)])
    pick_base(sems, narrow_any, handed_any, narrow, handed, 1)
    end(begun)
    put_ref[...] = asked[batch : batch + 1, :]

    @pl.when(lax.axis_index("seg") != 0)
    def _():
        top = narrow.shape[0]
        lines = (handed.shape[0] - top) // 2
        digits = handed[top:, :].astype(F32)
        number = digits[:lines, :] * 64.0 + digits[lines:, :]
        for j in range(lines):
            put_ref[:, j * LANES : (j + 1) * LANES] = number[j : j + 1, :].astype(I32)

    for j in range(rows_ref.shape[0] // LANES):
        span = slice(j * LANES, (j + 1) * LANES)
        rows_ref[span, :] = pick_rows(asked[batch + 1 : batch + 2, span], narrow[...])


def gather_values(values, cap, pieces, sems, first):
    room = padded(cap)
    if room != cap:
        values[...] = jnp.zeros(values.shape, values.dtype)
    pairs = [(piece, values.at[k * room : k * room + cap, :]) for k, piece in enumerate(pieces)]
    return begin(sems, pairs, first)


def handed_kernel(first, sems, given, pieces, scratch):
    z = lax.axis_index("node")
    cap, few = pieces[0].shape[0], len(pieces)

    def send(source):
        pairs = []
        for k, piece in enumerate(pieces):
            at = pl.multiple_of(((z ^ (first + k)) % few) * cap, cap)
            pairs.append((source.at[pl.ds(at, cap), :], piece))
        end(begin(sems, pairs))

    @pl.when(lax.axis_index("seg") == 0)
    def _():
        send(given[0])

    @pl.when(lax.axis_index("seg") != 0)
    def _():
        send(given[1])


def next_kernel(batch, sems, given, made, scratch):
    asked_any, put_any, rows_any = given[:3]
    values_ref, pieces = made[0], made[1:]
    asked, put, rows, held = scratch
    cap = pieces[0].shape[0]
    begun = begin(sems, [(asked_any, asked), (put_any, put), (rows_any, rows)])
    end(gather_values(values_ref, cap, given[3:], sems, 3))
    end(begun)
    events = values_ref.shape[0]
    wide = jnp.concatenate([values_ref[...], jnp.ones((events, LANES), BF)], axis=1)
    written = jnp.where(put[...] < 0, -2, put[...])
    for j in range(events // LANES):
        span = slice(j * LANES, (j + 1) * LANES)
        numbers = down(asked[batch + 1 : batch + 2, span])
        hot = jnp.concatenate(
            [
                ones_at(
                    numbers
                    == jnp.broadcast_to(written[:, i * LANES : (i + 1) * LANES], (LANES, LANES))
                )
                for i in range(events // LANES)
            ],
            axis=1,
        )
        found = jnp.dot(hot, wide, preferred_element_type=F32)
        kept = rows[span, :].astype(F32)
        held[span, :] = jnp.where(found[:, LANES:] > 0.5, found[:, :LANES], kept).astype(BF)
    give(held, pieces)


def update_kernel(sems, given, made, scratch):
    put_any, values_any, memory_any, handed_any = given
    put, values, base, handed = scratch
    begun = begin(sems, [(put_any, put), (values_any, values)])
    pick_base(sems, memory_any, handed_any, base, handed, 2)
    end(begun)
    set_rows(put[...], values[...], base, made[0])


def last_kernel(batch, sems, given, made, scratch):
    asked_any, base_any, *pieces = given
    asked, values, base = scratch
    begun = begin(sems, [(asked_any, asked), (base_any, base)])
    end(gather_values(values, pieces[0].shape[0], pieces, sems, 2))
    end(begun)
    set_rows(asked[batch : batch + 1, :], values[...], base, made[0])


def cosine(x):
    turns = jnp.round(x * 0.3183098861837907)
    r = x - turns * 3.140625
    r = r - turns * 0.0009670257568359375
    r = r - turns * 6.278329573009626e-07
    odd = turns - 2.0 * jnp.floor(turns * 0.5)
    q = r * r
    p = 2.08767569878681e-09 - q * 1.1470745597729725e-11
    p = q * p - 2.7557319223985893e-07
    p = q * p + 2.48015873015873e-05
    p = q * p - 0.001388888888888889
    p = q * p + 0.041666666666666664
    p = q * p - 0.5
    p = q * p + 1.0
    return p * (1.0 - 2.0 * odd)


def batch_kernel(nodes, batch, final, prior, sems, given, made, scratch):
    facts_any, edge_any, edge_other_any, w_in_any, w_hid_any, up_any = given[:6]
    own_pieces, other_pieces = given[6 : 6 + nodes], given[6 + nodes : 6 + 2 * nodes]
    rest = given[6 + 2 * nodes :]
    message, facts, edge, w_in, w_hid, gates, up, fresh = scratch[:8]
    cap = own_pieces[0].shape[0]
    events = nodes * cap
    z, f = lax.axis_index("node"), lax.axis_index("feat")
    mine = pl.multiple_of(f * LANES, LANES)
    other = pl.multiple_of((1 - f) * LANES, LANES)
    width = 2 * LANES
    long = message.shape[1]
    thin = edge_any.shape[1]
    pairs = []
    for k in range(nodes):
        at = pl.ds(pl.multiple_of((z ^ k) * cap, cap), cap)
        pairs.append((own_pieces[k], message.at[at, pl.ds(mine, LANES)]))
        pairs.append((other_pieces[k], message.at[at, pl.ds(other, LANES)]))
    early = [
        (facts_any, facts),
        (edge_any.at[batch], edge.at[pl.ds(pl.multiple_of(f * thin, thin), thin), :]),
        (edge_other_any.at[batch], edge.at[pl.ds(pl.multiple_of((1 - f) * thin, thin), thin), :]),
    ]
    late = [(w_in_any, w_in), (w_hid_any, w_hid), (up_any.at[batch], up)]
    if prior:
        before = scratch[8]
        late.append((rest[0], before))
    rows_begun = begin(sems, pairs)
    early_begun = begin(sems, early, len(pairs))
    late_begun = begin(sems, late, len(pairs) + len(early))
    end(early_begun)
    lines = events // LANES
    top = facts.shape[0] - 8
    bias_ref = facts[top : top + 4, :]
    freq, phase = facts[top + 4 : top + 5, :], facts[top + 5 : top + 6, :]
    dst = [facts[2 * lines * batch + j : 2 * lines * batch + j + 1, :] for j in range(lines)]
    start = 2 * lines * batch + lines
    for j in range(lines):
        span = slice(j * LANES, (j + 1) * LANES)
        angle = down(facts[start + j : start + j + 1, :]) * freq + phase
        message[span, 2 * width : 2 * width + LANES] = cosine(angle).astype(BF)
        message[span, 2 * width + LANES :] = jnp.transpose(edge[:, span].astype(F32)).astype(BF)
    end(rows_begun)
    full = message[:, :width]
    for j in range(events // LANES):
        span = slice(j * LANES, (j + 1) * LANES)
        message[span, width : 2 * width] = pick_rows(dst[j].astype(I32), full)
    end(late_begun)
    w_in01 = jnp.concatenate([w_in[0], w_in[1]], axis=1)
    w_hid01 = jnp.concatenate([w_hid[0], w_hid[1]], axis=1)
    sums = [jnp.zeros((1, LANES), F32) for _ in range(4)]
    tall = 256
    for i in range(events // tall):
        span = slice(i * tall, (i + 1) * tall)
        rows = message[span, :]
        hidden = rows[:, :width]
        both = jnp.dot(rows, w_in01, preferred_element_type=F32) + jnp.dot(
            hidden, w_hid01, preferred_element_type=F32
        )
        own = message[span, pl.ds(mine, LANES)].astype(F32)
        reset_gate = jax.nn.sigmoid(both[:, :LANES] + bias_ref[0:1, :])
        update = jax.nn.sigmoid(both[:, LANES:] + bias_ref[1:2, :])
        recur_term = jnp.dot(hidden, w_hid[2], preferred_element_type=F32) + bias_ref[3:4, :]
        candid = jnp.tanh(
            jnp.dot(rows, w_in[2], preferred_element_type=F32)
            + bias_ref[2:3, :]
            + reset_gate * recur_term
        )
        fresh[span, :] = ((1.0 - update) * candid + update * own).astype(BF)
        numbers = [down(dst[j]) for j in range(i * tall // LANES, (i + 1) * tall // LANES)]
        live = jnp.concatenate(numbers, axis=0) >= 0.0
        cotangent = jnp.where(live, up[span, :].astype(F32), 0.0)
        grad_cand = cotangent * (1.0 - update) * (1.0 - candid * candid)
        grad_upd = cotangent * (own - candid) * update * (1.0 - update)
        grad_reset = grad_cand * recur_term * reset_gate * (1.0 - reset_gate)
        grad_recur = grad_cand * reset_gate
        for g, part in enumerate((grad_reset, grad_upd, grad_cand, grad_recur)):
            sums[g] = sums[g] + jnp.sum(part, axis=0, keepdims=True)
            gates[span, g * LANES : (g + 1) * LANES] = part.astype(BF)
    if final:
        for k in range(nodes):
            made[k][...] = fresh[pl.ds(pl.multiple_of((z ^ k) * cap, cap), cap), :]
    else:
        few = events // 2
        upper = z // (nodes // 2)
        made[0][...] = fresh[pl.ds(pl.multiple_of((1 - upper) * few, few), few), :]
        made[1][...] = fresh[pl.ds(pl.multiple_of(upper * few, few), few), :]
    out_ref = made[-1]

    def put(start, value):
        stop = start + value.shape[0]
        if prior:
            value = value + before[start:stop, :]
        out_ref[start:stop, :] = value.astype(out_ref.dtype)

    for i in range(long // tall):
        rows = message[:, i * tall : (i + 1) * tall]
        columns = gates[...] if i * tall < width else gates[:, : 3 * LANES]
        product = lax.dot_general(
            rows, columns, (((0,), (0,)), ((), ())), preferred_element_type=F32
        )
        for g in range(3):
            put(g * long + i * tall, product[:, g * LANES : (g + 1) * LANES])
        if i * tall < width:
            put(3 * long + i * tall, product[:, 3 * LANES :])
    top = 3 * long + width
    pad = out_ref.shape[0] - top
    tail = jnp.concatenate(sums + [jnp.zeros((pad - 4, LANES), F32)], axis=0)
    put(top, tail)


def middle_kernel(nodes, segs, first, sems, given, made, scratch):
    totals, got = given[0], given[1:segs]
    rows = scratch[:segs]
    whole = scratch[segs]
    few, chunk = len(made), made[0].shape[0]
    z = lax.axis_index("node")
    side = (z ^ first) // few
    share = few * chunk
    at = pl.ds(pl.multiple_of((lax.axis_index("seg") * 2 + side) * share, share), share)
    pairs = [(totals.at[at, :], rows[0])] + list(zip(got, rows[1:]))
    end(begin(sems, pairs))
    total = rows[0][...].astype(F32)
    for x in range(1, segs):
        total = total + rows[x][...].astype(F32)
    whole[...] = total.astype(BF)
    for k in range(few):
        at = pl.multiple_of(((z ^ (first + k)) % few) * chunk, chunk)
        made[k][...] = whole[pl.ds(at, chunk), :]


def unpack_kernel(nodes, segs, long, sems, pieces, made, scratch):
    grad_in, grad_hid, grad_bias = made
    (held,) = scratch
    few = nodes // 2
    chunk = pieces[0].shape[0] // few
    z, s = lax.axis_index("node"), lax.axis_index("seg")
    pairs = []
    for x in range(segs):
        for k in range(nodes):
            at = pl.multiple_of(((s ^ x) * nodes + (z ^ k)) * chunk, chunk)
            source = pieces[2 * x + k // few]
            i = k % few
            pairs.append(
                (source.at[i * chunk : (i + 1) * chunk, :], held.at[pl.ds(at, chunk), :])
            )
    end(begin(sems, pairs))
    width = grad_hid.shape[1]
    for g in range(3):
        grad_in[g] = held[g * long : (g + 1) * long, :].astype(F32)
    for g in range(2):
        grad_hid[g] = held[g * long : g * long + width, :].astype(F32)
    grad_hid[2] = held[3 * long : 3 * long + width, :].astype(F32)
    top = 3 * long + width
    grad_bias[...] = held[top : top + 16, :].astype(F32)[:4, :]


def local(
    memory, req_rows, req_count, dst_slot, elapsed, edges, upstream, freq, phase, w_input, w_hidden, bias
):
    nodes, segs = lax.axis_size("node"), lax.axis_size("seg")
    z, s = lax.axis_index("node"), lax.axis_index("seg")
    memory_now = memory[0]
    node_rows, half = memory_now.shape
    batches, cap = req_rows.shape[0], req_rows.shape[-1]
    events = nodes * cap
    room = padded(cap)
    spread = nodes * room
    counts = req_count[:, 0, 0]
    piece = shape((cap, half), BF)
    long, width = w_input.shape[1], w_hidden.shape[1]

    def node_swap(block, k):
        return lax.ppermute(block, "node", [(i, i ^ k) for i in range(nodes)])

    def seg_swap(block, x):
        return lax.ppermute(block, "seg", [(i, i ^ x) for i in range(segs)])

    def seg_next(block):
        return lax.ppermute(block, "seg", [(i, i + 1) for i in range(segs - 1)])

    def feat_swap(block):
        return lax.ppermute(block, "feat", [(0, 1), (1, 0)])

    def exchange(blocks):
        return [blocks[0]] + [node_swap(blocks[k], k) for k in range(1, nodes)]

    live = jnp.arange(cap)[None, None, :] < counts[:, :, None]
    masked = jnp.where(live, req_rows[:, 0, 0], -1)
    masked = jnp.pad(masked, ((0, 0), (0, 0), (0, room - cap)), constant_values=-1)
    wanted = exchange(
        [lax.dynamic_index_in_dim(masked, z ^ k, 1, keepdims=False) for k in range(nodes)]
    )
    wide_rows = pltpu.VMEM((spread, half), BF)
    edge_own = jnp.swapaxes(edges[:, 0], 1, 2)
    edge_other = feat_swap(edge_own)
    lines = events // LANES
    named = jnp.where(live, dst_slot[:, 0].reshape(live.shape), -1)
    facts = jnp.stack([named.reshape(batches, events), elapsed[:, 0]], axis=1).astype(F32)
    facts = facts.reshape(batches * 2 * lines, LANES)
    rest = jnp.zeros((2, half), F32)
    facts = jnp.concatenate([facts, bias, freq[None], phase[None], rest], axis=0)

    narrow = run(
        narrow_kernel,
        [shape((node_rows, half), BF)],
        [memory_now, wanted[1], facts],
        [pltpu.VMEM((node_rows, half), F32)],
        1,
        (0,),
    )[0]
    asked, *served = run(
        serve_kernel,
        [shape((batches, spread), I32)] + [piece] * nodes,
        wanted + [narrow],
        [pltpu.VMEM((node_rows, half), BF), wide_rows],
        nodes + 1,
    )

    chunk = -(-(3 * long + width + 16) // (16 * nodes * segs)) * 16
    total_rows = chunk * nodes * segs
    numbers = pltpu.VMEM((batches, spread), I32)
    line = pltpu.VMEM((1, spread), I32)
    block = pltpu.VMEM((node_rows, half), F32)
    totals = None
    for b in range(batches):
        final = b + 1 == batches
        own_pieces = exchange(served)
        if not final:
            bundle = run(
                lambda *a, b=b: bundle_kernel(b, *a),
                [shape((node_rows + 2 * spread // LANES, half), BF)],
                [narrow, asked],
                [numbers],
                2,
            )[0]
            handed_memory = seg_next(bundle)
        other_pieces = [feat_swap(p) for p in own_pieces]
        given = [facts, edge_own, edge_other, w_input, w_hidden, upstream[:, 0]]
        given = given + own_pieces + other_pieces + ([] if totals is None else [totals])
        rooms = [
            pltpu.VMEM((events, long), BF),
            pltpu.VMEM(facts.shape, F32),
            pltpu.VMEM((2 * edges.shape[-1], events), BF),
            pltpu.VMEM(w_input.shape, BF),
            pltpu.VMEM(w_hidden.shape, BF),
            pltpu.VMEM((events, 4 * half), BF),
            pltpu.VMEM((events, half), BF),
            pltpu.VMEM((events, half), BF),
        ]
        if totals is not None:
            rooms.append(pltpu.VMEM((total_rows, half), F32))
        copies = 7 + 2 * nodes
        *fresh, totals = run(
            lambda *a, b=b, last=final, p=totals is not None: batch_kernel(nodes, b, last, p, *a),
            ([piece] * nodes if final else [shape((events // 2, half), BF)] * 2)
            + [shape((total_rows, half), BF if final else F32)],
            given,
            rooms,
            copies,
            (1, 3, 4, 5),
        )
        if not final:
            hops = [seg_next(side) for side in fresh]
            put, rows = run(
                lambda *a, b=b: base_kernel(b, *a),
                [shape((1, spread), I32), shape((spread, half), BF)],
                [asked, narrow, handed_memory],
                [numbers, pltpu.VMEM(bundle.shape, BF), pltpu.VMEM((node_rows, half), BF)],
                2,
            )
            few = nodes // 2
            values = [None] * nodes
            for side, first in ((0, few), (1, 0)):
                values[first : first + few] = run(
                    lambda *a, first=first: handed_kernel(first, *a),
                    [piece] * few,
                    [fresh[side], hops[side]] + ([rows] if side == 1 else []),
                    [],
                    few,
                )
            values = exchange(values)
            values, *served = run(
                lambda *a, b=b: next_kernel(b, *a),
                [shape((spread, half), BF)] + [piece] * nodes,
                [asked, put, rows] + values,
                [numbers, line, wide_rows, wide_rows],
                3 + nodes,
            )
            memory_now = run(
                update_kernel,
                [shape((node_rows, half), F32)],
                [put, values, memory_now, handed_memory],
                [line, wide_rows, block, pltpu.VMEM(bundle.shape, BF)],
                3,
            )[0]
            if b + 2 < batches:
                narrow = memory_now.astype(BF)
        else:
            returned = exchange(fresh)
            memory_out = run(
                lambda *a, b=b: last_kernel(b, *a),
                [shape((node_rows, half), F32)],
                [asked, memory_now] + returned,
                [numbers, wide_rows, block],
                2 + nodes,
            )[0]

    def at(blocks, i):
        return lax.dynamic_index_in_dim(blocks, i, 0, keepdims=False)

    few = nodes // 2
    upper = z // few
    blocks = totals.reshape(segs, 2, few * chunk, half)
    got = [
        [seg_swap(at(at(blocks, s ^ x), side), x) for x in range(1, segs)]
        for side in (1 - upper, upper)
    ]
    share = pltpu.VMEM((few * chunk, half), BF)
    parts = [None] * nodes
    for side, first in ((0, few), (1, 0)):
        parts[first : first + few] = run(
            lambda *a, first=first: middle_kernel(nodes, segs, first, *a),
            [shape((chunk, half), BF)] * few,
            [totals] + got[side] + (returned[1:] if side else []),
            [share] * (segs + 1),
            segs,
        )
    parts = exchange(parts)
    summed = sum((g.astype(F32) for g in parts[1:]), parts[0].astype(F32)).astype(BF)
    around = [summed] + [node_swap(summed, k) for k in range(1, nodes)]
    sides = [jnp.concatenate(around[:few], axis=0), jnp.concatenate(around[few:], axis=0)]
    gathered = list(sides)
    for x in range(1, segs):
        gathered += [seg_swap(side, x) for side in sides]
    grads = run(
        lambda *a: unpack_kernel(nodes, segs, long, *a),
        [shape(w_input.shape, F32), shape(w_hidden.shape, F32), shape(bias.shape, F32)],
        gathered,
        [pltpu.VMEM((total_rows, half), BF)],
        nodes * segs,
    )
    return (memory_out[None], *grads)


def solution(mesh):
    in_specs = (
        P(("parts", "seg"), "node", "feat"),
        P(None, ("parts", "seg"), "node", None, None),
        P(None, ("parts", "seg"), "node", None),
        P(None, ("parts", "seg"), "node"),
        P(None, ("parts", "seg"), "node"),
        P(None, ("parts", "seg"), "node", "feat"),
        P(None, ("parts", "seg"), "node", "feat"),
        P(),
        P(),
        P(None, None, "feat"),
        P(None, None, "feat"),
        P(None, "feat"),
    )
    out_specs = (
        P(("parts", "seg"), "node", "feat"),
        P("parts", None, "feat"),
        P("parts", None, "feat"),
        P("parts", "feat"),
    )
    return jax.shard_map(local, mesh=mesh, in_specs=in_specs, out_specs=out_specs, check_vma=False)
```

```python
import jax
import jax.numpy as jnp
from jax import lax
from jax.experimental import pallas as pl
from jax.experimental.pallas import tpu as pltpu
from jax.sharding import PartitionSpec as P

BF = jnp.bfloat16
F32 = jnp.float32
I32 = jnp.int32
LANES = 128
VMEM = pl.BlockSpec(memory_space=pltpu.VMEM)
ANY = pl.BlockSpec(memory_space=pl.ANY)
HBM = pl.BlockSpec(memory_space=pltpu.HBM)


def shape(dims, kind):
    return jax.ShapeDtypeStruct(tuple(dims), kind)


def run(kernel, outs, args, scratch=(), copies=1, far=(), here=()):
    b, c = len(args), len(outs)

    def body(*refs):
        kernel(refs[-1], refs[:b], refs[b : b + c], refs[b + c : -1])

    moved = sum(a.size * a.dtype.itemsize for a in list(args) + list(outs))
    return pl.pallas_call(
        body,
        out_shape=list(outs),
        in_specs=[HBM if i in far else VMEM if i in here else ANY for i in range(len(args))],
        out_specs=[VMEM] * len(outs),
        scratch_shapes=list(scratch) + [pltpu.SemaphoreType.DMA((copies,))],
        compiler_params=pltpu.CompilerParams(vmem_limit_bytes=24 * 1024 * 1024),
        cost_estimate=pl.CostEstimate(flops=0, bytes_accessed=moved, transcendentals=0),
    )(*args)


def begin(sems, pairs, first=0):
    copies = [
        pltpu.make_async_copy(source, target, sems.at[first + i])
        for i, (source, target) in enumerate(pairs)
    ]
    for copy in copies:
        copy.start()
    return copies


def end(copies):
    for copy in copies:
        copy.wait()


def down(row):
    return jnp.transpose(jnp.broadcast_to(row, (LANES, LANES)))


def ones_at(where):
    return jnp.where(where, 1.0, 0.0).astype(BF)


def pick_rows(row, source):
    numbers = down(row)
    lane = lax.broadcasted_iota(I32, (LANES, LANES), 1)
    hot = jnp.concatenate(
        [ones_at(numbers == lane + k * LANES) for k in range(source.shape[0] // LANES)], axis=1
    )
    return jnp.dot(hot, source, preferred_element_type=F32).astype(BF)


def set_rows(row, values, base_ref, out_ref):
    events = values.shape[0]
    tall = 256
    wide = jnp.concatenate([values, jnp.ones((events, LANES), BF)], axis=1)
    for i in range(out_ref.shape[0] // tall):
        own = lax.broadcasted_iota(I32, (tall, events), 0) + i * tall
        hot = ones_at(own == jnp.broadcast_to(row, (tall, events)))
        found = jnp.dot(hot, wide, preferred_element_type=F32)
        span = slice(i * tall, (i + 1) * tall)
        out_ref[span, :] = jnp.where(found[:, LANES:] > 0.5, found[:, :LANES], base_ref[span, :])


def padded(cap):
    return -(-cap // LANES) * LANES


def give(held, pieces):
    cap = pieces[0].shape[0]
    room = padded(cap)
    for k, piece in enumerate(pieces):
        piece[...] = held[k * room : k * room + cap, :]


def narrow_kernel(sems, given, made, scratch):
    end(begin(sems, [(given[0], scratch[0])]))
    made[0][...] = scratch[0][...].astype(BF)


def bundle_kernel(batch, sems, given, made, scratch):
    narrow_any, asked_any = given
    (out_ref,), (asked,) = made, scratch
    rows = narrow_any.shape[0]
    end(begin(sems, [(narrow_any, out_ref.at[:rows, :]), (asked_any, asked)]))
    lines = (out_ref.shape[0] - rows) // 2
    number = jnp.concatenate(
        [asked[batch : batch + 1, j * LANES : (j + 1) * LANES] for j in range(lines)], axis=0
    )
    high = jnp.floor(number.astype(F32) * (1.0 / 64.0))
    low = number.astype(F32) - 64.0 * high
    out_ref[rows:, :] = jnp.concatenate([high, low], axis=0).astype(BF)


def serve_kernel(sems, given, made, scratch):
    *asked_pieces, narrow_any = given
    asked_ref, *pieces = made
    narrow, held = scratch
    nodes, room = len(asked_pieces), asked_pieces[0].shape[1]
    pairs = [(narrow_any, narrow)]
    for k, piece in enumerate(asked_pieces):
        pairs.append((piece, asked_ref.at[:, k * room : (k + 1) * room]))
    end(begin(sems, pairs))
    for j in range(nodes * room // LANES):
        span = slice(j * LANES, (j + 1) * LANES)
        held[span, :] = pick_rows(asked_ref[0:1, span], narrow[...])
    give(held, pieces)


def pick_base(sems, memory_any, handed_any, base_ref, handed_ref, first):
    @pl.when(lax.axis_index("seg") == 0)
    def _():
        end(begin(sems, [(memory_any, base_ref)], first))

    @pl.when(lax.axis_index("seg") != 0)
    def _():
        end(begin(sems, [(handed_any, handed_ref)], first))
        base_ref[...] = handed_ref[: base_ref.shape[0], :].astype(base_ref.dtype)


def base_kernel(batch, sems, given, made, scratch):
    asked_any, narrow_any, handed_any = given
    put_ref, rows_ref = made
    asked, handed, narrow = scratch
    begun = begin(sems, [(asked_any, asked)])
    pick_base(sems, narrow_any, handed_any, narrow, handed, 1)
    end(begun)
    put_ref[...] = asked[batch : batch + 1, :]

    @pl.when(lax.axis_index("seg") != 0)
    def _():
        top = narrow.shape[0]
        lines = (handed.shape[0] - top) // 2
        digits = handed[top:, :].astype(F32)
        number = digits[:lines, :] * 64.0 + digits[lines:, :]
        for j in range(lines):
            put_ref[:, j * LANES : (j + 1) * LANES] = number[j : j + 1, :].astype(I32)

    for j in range(rows_ref.shape[0] // LANES):
        span = slice(j * LANES, (j + 1) * LANES)
        rows_ref[span, :] = pick_rows(asked[batch + 1 : batch + 2, span], narrow[...])


def gather_values(values, cap, pieces, sems, first):
    room = padded(cap)
    if room != cap:
        values[...] = jnp.zeros(values.shape, values.dtype)
    pairs = [(piece, values.at[k * room : k * room + cap, :]) for k, piece in enumerate(pieces)]
    return begin(sems, pairs, first)


def handed_kernel(first, sems, given, pieces, scratch):
    z = lax.axis_index("node")
    cap, few = pieces[0].shape[0], len(pieces)

    def send(source):
        pairs = []
        for k, piece in enumerate(pieces):
            at = pl.multiple_of(((z ^ (first + k)) % few) * cap, cap)
            pairs.append((source.at[pl.ds(at, cap), :], piece))
        end(begin(sems, pairs))

    @pl.when(lax.axis_index("seg") == 0)
    def _():
        send(given[0])

    @pl.when(lax.axis_index("seg") != 0)
    def _():
        send(given[1])


def next_kernel(batch, sems, given, made, scratch):
    asked_any, put_any, rows_any = given[:3]
    values_ref, pieces = made[0], made[1:]
    asked, put, rows, held = scratch
    cap = pieces[0].shape[0]
    begun = begin(sems, [(asked_any, asked), (put_any, put), (rows_any, rows)])
    end(gather_values(values_ref, cap, given[3:-1], sems, 3))
    end(begun)
    events = values_ref.shape[0]
    wide = jnp.concatenate([values_ref[...], jnp.ones((events, LANES), BF)], axis=1)
    written = jnp.where(put[...] < 0, -2, put[...])
    for j in range(events // LANES):
        span = slice(j * LANES, (j + 1) * LANES)
        numbers = down(asked[batch + 1 : batch + 2, span])
        hot = jnp.concatenate(
            [
                ones_at(
                    numbers
                    == jnp.broadcast_to(written[:, i * LANES : (i + 1) * LANES], (LANES, LANES))
                )
                for i in range(events // LANES)
            ],
            axis=1,
        )
        found = jnp.dot(hot, wide, preferred_element_type=F32)
        kept = rows[span, :].astype(F32)
        held[span, :] = jnp.where(found[:, LANES:] > 0.5, found[:, :LANES], kept).astype(BF)
    give(held, pieces)


def update_kernel(sems, given, made, scratch):
    put_any, values_any, memory_any, handed_any = given
    put, values, base, handed = scratch
    begun = begin(sems, [(put_any, put), (values_any, values)])
    pick_base(sems, memory_any, handed_any, base, handed, 2)
    end(begun)
    set_rows(put[...], values[...], base, made[0])


def last_kernel(batch, sems, given, made, scratch):
    asked_any, base_any, *pieces = given
    asked, values, base = scratch
    begun = begin(sems, [(asked_any, asked), (base_any, base)])
    end(gather_values(values, pieces[0].shape[0], pieces, sems, 2))
    end(begun)
    set_rows(asked[batch : batch + 1, :], values[...], base, made[0])


def cosine(x):
    turns = jnp.round(x * 0.3183098861837907)
    r = x - turns * 3.140625
    r = r - turns * 0.0009670257568359375
    r = r - turns * 6.278329573009626e-07
    odd = turns - 2.0 * jnp.floor(turns * 0.5)
    q = r * r
    p = 2.08767569878681e-09 - q * 1.1470745597729725e-11
    p = q * p - 2.7557319223985893e-07
    p = q * p + 2.48015873015873e-05
    p = q * p - 0.001388888888888889
    p = q * p + 0.041666666666666664
    p = q * p - 0.5
    p = q * p + 1.0
    return p * (1.0 - 2.0 * odd)


def products(message, gates, sums, before, out_ref):
    long, width = message.shape[1], 2 * LANES
    tall = 256

    def put(start, value):
        stop = start + value.shape[0]
        if before is not None:
            value = value + before[start:stop, :]
        out_ref[start:stop, :] = value.astype(out_ref.dtype)

    for i in range(long // tall):
        rows = message[:, i * tall : (i + 1) * tall]
        columns = gates[...] if i * tall < width else gates[:, : 3 * LANES]
        product = lax.dot_general(
            rows, columns, (((0,), (0,)), ((), ())), preferred_element_type=F32
        )
        for g in range(3):
            put(g * long + i * tall, product[:, g * LANES : (g + 1) * LANES])
        if i * tall < width:
            put(3 * long + i * tall, product[:, 3 * LANES :])
    top = 3 * long + width
    pad = out_ref.shape[0] - top
    tail = jnp.concatenate(sums + [jnp.zeros((pad - 4, LANES), F32)], axis=0)
    put(top, tail)


def grads_kernel(sems, given, made, scratch):
    message, gates, sums = given
    products(message, gates, [sums[g : g + 1, :] for g in range(4)], None, made[0])


def batch_kernel(nodes, batch, final, prior, sems, given, made, scratch):
    facts_any, edge_any, edge_other_any, w_in_any, w_hid_any, up_any = given[:6]
    own_pieces, other_pieces = given[6 : 6 + nodes], given[6 + nodes : 6 + 2 * nodes]
    rest = given[6 + 2 * nodes :]
    message, facts, edge, w_in, w_hid, gates, up, fresh = scratch[:8]
    if not final:
        message, gates = made[2:4]
    cap = own_pieces[0].shape[0]
    events = nodes * cap
    z, f = lax.axis_index("node"), lax.axis_index("feat")
    mine = pl.multiple_of(f * LANES, LANES)
    other = pl.multiple_of((1 - f) * LANES, LANES)
    width = 2 * LANES
    long = message.shape[1]
    thin = edge_any.shape[1]
    pairs = []
    for k in range(nodes):
        at = pl.ds(pl.multiple_of((z ^ k) * cap, cap), cap)
        pairs.append((own_pieces[k], message.at[at, pl.ds(mine, LANES)]))
        pairs.append((other_pieces[k], message.at[at, pl.ds(other, LANES)]))
    early = [
        (facts_any, facts),
        (edge_any.at[batch], edge.at[pl.ds(pl.multiple_of(f * thin, thin), thin), :]),
        (edge_other_any.at[batch], edge.at[pl.ds(pl.multiple_of((1 - f) * thin, thin), thin), :]),
    ]
    late = [(w_in_any, w_in), (w_hid_any, w_hid), (up_any.at[batch], up)]
    if prior:
        before = scratch[8]
        late.append((rest[0], before))
    rows_begun = begin(sems, pairs)
    early_begun = begin(sems, early, len(pairs))
    late_begun = begin(sems, late, len(pairs) + len(early))
    end(early_begun)
    lines = events // LANES
    top = facts.shape[0] - 8
    bias_ref = facts[top : top + 4, :]
    freq, phase = facts[top + 4 : top + 5, :], facts[top + 5 : top + 6, :]
    dst = [facts[2 * lines * batch + j : 2 * lines * batch + j + 1, :] for j in range(lines)]
    start = 2 * lines * batch + lines
    for j in range(lines):
        span = slice(j * LANES, (j + 1) * LANES)
        angle = down(facts[start + j : start + j + 1, :]) * freq + phase
        message[span, 2 * width : 2 * width + LANES] = cosine(angle).astype(BF)
        message[span, 2 * width + LANES :] = jnp.transpose(edge[:, span].astype(F32)).astype(BF)
    end(rows_begun)
    full = message[:, :width]
    for j in range(events // LANES):
        span = slice(j * LANES, (j + 1) * LANES)
        message[span, width : 2 * width] = pick_rows(dst[j].astype(I32), full)
    end(late_begun)
    w_in01 = jnp.concatenate([w_in[0], w_in[1]], axis=1)
    w_hid01 = jnp.concatenate([w_hid[0], w_hid[1]], axis=1)
    sums = [jnp.zeros((1, LANES), F32) for _ in range(4)]
    tall = 256
    for i in range(events // tall):
        span = slice(i * tall, (i + 1) * tall)
        rows = message[span, :]
        hidden = rows[:, :width]
        both = jnp.dot(rows, w_in01, preferred_element_type=F32) + jnp.dot(
            hidden, w_hid01, preferred_element_type=F32
        )
        own = message[span, pl.ds(mine, LANES)].astype(F32)
        reset_gate = jax.nn.sigmoid(both[:, :LANES] + bias_ref[0:1, :])
        update = jax.nn.sigmoid(both[:, LANES:] + bias_ref[1:2, :])
        recur_term = jnp.dot(hidden, w_hid[2], preferred_element_type=F32) + bias_ref[3:4, :]
        candid = jnp.tanh(
            jnp.dot(rows, w_in[2], preferred_element_type=F32)
            + bias_ref[2:3, :]
            + reset_gate * recur_term
        )
        fresh[span, :] = ((1.0 - update) * candid + update * own).astype(BF)
        numbers = [down(dst[j]) for j in range(i * tall // LANES, (i + 1) * tall // LANES)]
        live = jnp.concatenate(numbers, axis=0) >= 0.0
        cotangent = jnp.where(live, up[span, :].astype(F32), 0.0)
        grad_cand = cotangent * (1.0 - update) * (1.0 - candid * candid)
        grad_upd = cotangent * (own - candid) * update * (1.0 - update)
        grad_reset = grad_cand * recur_term * reset_gate * (1.0 - reset_gate)
        grad_recur = grad_cand * reset_gate
        for g, part in enumerate((grad_reset, grad_upd, grad_cand, grad_recur)):
            sums[g] = sums[g] + jnp.sum(part, axis=0, keepdims=True)
            gates[span, g * LANES : (g + 1) * LANES] = part.astype(BF)
    if final:
        for k in range(nodes):
            made[k][...] = fresh[pl.ds(pl.multiple_of((z ^ k) * cap, cap), cap), :]
    else:
        few = events // 2
        upper = z // (nodes // 2)
        made[0][...] = fresh[pl.ds(pl.multiple_of((1 - upper) * few, few), few), :]
        made[1][...] = fresh[pl.ds(pl.multiple_of(upper * few, few), few), :]
    if final:
        products(message, gates, sums, before if prior else None, made[-1])
    else:
        made[4][...] = jnp.concatenate(sums + [jnp.zeros((4, LANES), F32)], axis=0)


def middle_kernel(nodes, segs, first, sems, given, made, scratch):
    totals, got = given[0], given[1:segs]
    rows = scratch[:segs]
    whole = scratch[segs]
    few, chunk = len(made), made[0].shape[0]
    z = lax.axis_index("node")
    side = (z ^ first) // few
    share = few * chunk
    at = pl.ds(pl.multiple_of((lax.axis_index("seg") * 2 + side) * share, share), share)
    pairs = [(totals.at[at, :], rows[0])] + list(zip(got, rows[1:]))
    end(begin(sems, pairs))
    total = rows[0][...].astype(F32)
    for x in range(1, segs):
        total = total + rows[x][...].astype(F32)
    whole[...] = total.astype(BF)
    for k in range(few):
        at = pl.multiple_of(((z ^ (first + k)) % few) * chunk, chunk)
        made[k][...] = whole[pl.ds(at, chunk), :]


def unpack_kernel(nodes, segs, long, sems, pieces, made, scratch):
    grad_in, grad_hid, grad_bias = made
    (held,) = scratch
    few = nodes // 2
    chunk = pieces[0].shape[0] // few
    z, s = lax.axis_index("node"), lax.axis_index("seg")
    pairs = []
    for x in range(segs):
        for k in range(nodes):
            at = pl.multiple_of(((s ^ x) * nodes + (z ^ k)) * chunk, chunk)
            source = pieces[2 * x + k // few]
            i = k % few
            pairs.append(
                (source.at[i * chunk : (i + 1) * chunk, :], held.at[pl.ds(at, chunk), :])
            )
    end(begin(sems, pairs))
    width = grad_hid.shape[1]
    for g in range(3):
        grad_in[g] = held[g * long : (g + 1) * long, :].astype(F32)
    for g in range(2):
        grad_hid[g] = held[g * long : g * long + width, :].astype(F32)
    grad_hid[2] = held[3 * long : 3 * long + width, :].astype(F32)
    top = 3 * long + width
    grad_bias[...] = held[top : top + 16, :].astype(F32)[:4, :]


def local(
    memory, req_rows, req_count, dst_slot, elapsed, edges, upstream, freq, phase, w_input, w_hidden, bias
):
    nodes, segs = lax.axis_size("node"), lax.axis_size("seg")
    z, s = lax.axis_index("node"), lax.axis_index("seg")
    memory_now = memory[0]
    node_rows, half = memory_now.shape
    batches, cap = req_rows.shape[0], req_rows.shape[-1]
    events = nodes * cap
    room = padded(cap)
    spread = nodes * room
    counts = req_count[:, 0, 0]
    piece = shape((cap, half), BF)
    long, width = w_input.shape[1], w_hidden.shape[1]

    def node_swap(block, k):
        return lax.ppermute(block, "node", [(i, i ^ k) for i in range(nodes)])

    def seg_swap(block, x):
        return lax.ppermute(block, "seg", [(i, i ^ x) for i in range(segs)])

    def seg_next(block):
        return lax.ppermute(block, "seg", [(i, i + 1) for i in range(segs - 1)])

    def feat_swap(block):
        return lax.ppermute(block, "feat", [(0, 1), (1, 0)])

    def exchange(blocks):
        return [blocks[0]] + [node_swap(blocks[k], k) for k in range(1, nodes)]

    live = jnp.arange(cap)[None, None, :] < counts[:, :, None]
    masked = jnp.where(live, req_rows[:, 0, 0], -1)
    masked = jnp.pad(masked, ((0, 0), (0, 0), (0, room - cap)), constant_values=-1)
    wanted = exchange(
        [lax.dynamic_index_in_dim(masked, z ^ k, 1, keepdims=False) for k in range(nodes)]
    )
    wide_rows = pltpu.VMEM((spread, half), BF)
    edge_own = jnp.swapaxes(edges[:, 0], 1, 2)
    edge_other = feat_swap(edge_own)
    lines = events // LANES
    named = jnp.where(live, dst_slot[:, 0].reshape(live.shape), -1)
    facts = jnp.stack([named.reshape(batches, events), elapsed[:, 0]], axis=1).astype(F32)
    facts = facts.reshape(batches * 2 * lines, LANES)
    rest = jnp.zeros((2, half), F32)
    facts = jnp.concatenate([facts, bias, freq[None], phase[None], rest], axis=0)

    narrow = run(
        narrow_kernel,
        [shape((node_rows, half), BF)],
        [memory_now, wanted[1], facts],
        [pltpu.VMEM((node_rows, half), F32)],
        1,
        (0,),
    )[0]
    asked, *served = run(
        serve_kernel,
        [shape((batches, spread), I32)] + [piece] * nodes,
        wanted + [narrow],
        [pltpu.VMEM((node_rows, half), BF), wide_rows],
        nodes + 1,
    )

    chunk = -(-(3 * long + width + 16) // (16 * nodes * segs)) * 16
    total_rows = chunk * nodes * segs
    numbers = pltpu.VMEM((batches, spread), I32)
    line = pltpu.VMEM((1, spread), I32)
    block = pltpu.VMEM((node_rows, half), F32)
    totals = None
    for b in range(batches):
        final = b + 1 == batches
        own_pieces = exchange(served)
        if not final:
            bundle = run(
                lambda *a, b=b: bundle_kernel(b, *a),
                [shape((node_rows + 2 * spread // LANES, half), BF)],
                [narrow, asked],
                [numbers],
                2,
            )[0]
            handed_memory = seg_next(bundle)
        other_pieces = [feat_swap(p) for p in own_pieces]
        given = [facts, edge_own, edge_other, w_input, w_hidden, upstream[:, 0]]
        given = given + own_pieces + other_pieces + ([] if totals is None else [totals])
        rooms = [
            pltpu.VMEM((events, long), BF),
            pltpu.VMEM(facts.shape, F32),
            pltpu.VMEM((2 * edges.shape[-1], events), BF),
            pltpu.VMEM(w_input.shape, BF),
            pltpu.VMEM(w_hidden.shape, BF),
            pltpu.VMEM((events, 4 * half), BF),
            pltpu.VMEM((events, half), BF),
            pltpu.VMEM((events, half), BF),
        ]
        if totals is not None:
            rooms.append(pltpu.VMEM((total_rows, half), F32))
        copies = 7 + 2 * nodes
        before_grads = [shape((events // 2, half), BF)] * 2 + [
            shape((events, long), BF),
            shape((events, 4 * half), BF),
            shape((8, half), F32),
        ]
        outs = run(
            lambda *a, b=b, last=final, p=totals is not None: batch_kernel(nodes, b, last, p, *a),
            [piece] * nodes + [shape((total_rows, half), BF)] if final else before_grads,
            given,
            rooms,
            copies,
            (1, 3, 4, 5),
        )
        if final:
            fresh, totals = outs[:-1], outs[-1]
        else:
            assert b == 0
            fresh = outs[:2]
            totals = run(
                grads_kernel, [shape((total_rows, half), F32)], outs[2:], [], 1, (), (0, 1, 2)
            )[0]
        if not final:
            hops = [seg_next(side) for side in fresh]
            put, rows = run(
                lambda *a, b=b: base_kernel(b, *a),
                [shape((1, spread), I32), shape((spread, half), BF)],
                [asked, narrow, handed_memory],
                [numbers, pltpu.VMEM(bundle.shape, BF), pltpu.VMEM((node_rows, half), BF)],
                2,
            )
            few = nodes // 2
            values = [None] * nodes
            for side, first in ((0, few), (1, 0)):
                values[first : first + few] = run(
                    lambda *a, first=first: handed_kernel(first, *a),
                    [piece] * few,
                    [fresh[side], hops[side]] + ([rows] if side == 1 else []),
                    [],
                    few,
                )
            values = exchange(values)
            values, *served = run(
                lambda *a, b=b: next_kernel(b, *a),
                [shape((spread, half), BF)] + [piece] * nodes,
                [asked, put, rows] + values + [totals],
                [numbers, line, wide_rows, wide_rows],
                3 + nodes,
            )
            memory_now = run(
                update_kernel,
                [shape((node_rows, half), F32)],
                [put, values, memory_now, handed_memory],
                [line, wide_rows, block, pltpu.VMEM(bundle.shape, BF)],
                3,
            )[0]
            if b + 2 < batches:
                narrow = memory_now.astype(BF)
        else:
            returned = exchange(fresh)
            memory_out = run(
                lambda *a, b=b: last_kernel(b, *a),
                [shape((node_rows, half), F32)],
                [asked, memory_now] + returned,
                [numbers, wide_rows, block],
                2 + nodes,
            )[0]

    def at(blocks, i):
        return lax.dynamic_index_in_dim(blocks, i, 0, keepdims=False)

    few = nodes // 2
    upper = z // few
    blocks = totals.reshape(segs, 2, few * chunk, half)
    got = [
        [seg_swap(at(at(blocks, s ^ x), side), x) for x in range(1, segs)]
        for side in (1 - upper, upper)
    ]
    share = pltpu.VMEM((few * chunk, half), BF)
    parts = [None] * nodes
    for side, first in ((0, few), (1, 0)):
        parts[first : first + few] = run(
            lambda *a, first=first: middle_kernel(nodes, segs, first, *a),
            [shape((chunk, half), BF)] * few,
            [totals] + got[side] + ([] if side else returned[1:]),
            [share] * (segs + 1),
            segs,
        )
    parts = exchange(parts)
    summed = sum((g.astype(F32) for g in parts[1:]), parts[0].astype(F32)).astype(BF)
    around = [summed] + [node_swap(summed, k) for k in range(1, nodes)]
    sides = [jnp.concatenate(around[:few], axis=0), jnp.concatenate(around[few:], axis=0)]
    gathered = list(sides)
    for x in range(1, segs):
        gathered += [seg_swap(side, x) for side in sides]
    grads = run(
        lambda *a: unpack_kernel(nodes, segs, long, *a),
        [shape(w_input.shape, F32), shape(w_hidden.shape, F32), shape(bias.shape, F32)],
        gathered,
        [pltpu.VMEM((total_rows, half), BF)],
        nodes * segs,
    )
    return (memory_out[None], *grads)


def solution(mesh):
    in_specs = (
        P(("parts", "seg"), "node", "feat"),
        P(None, ("parts", "seg"), "node", None, None),
        P(None, ("parts", "seg"), "node", None),
        P(None, ("parts", "seg"), "node"),
        P(None, ("parts", "seg"), "node"),
        P(None, ("parts", "seg"), "node", "feat"),
        P(None, ("parts", "seg"), "node", "feat"),
        P(),
        P(),
        P(None, None, "feat"),
        P(None, None, "feat"),
        P(None, "feat"),
    )
    out_specs = (
        P(("parts", "seg"), "node", "feat"),
        P("parts", None, "feat"),
        P("parts", None, "feat"),
        P("parts", "feat"),
    )
    return jax.shard_map(local, mesh=mesh, in_specs=in_specs, out_specs=out_specs, check_vma=False)
```

```python
import jax
import jax.numpy as jnp
from jax import lax
from jax.experimental import pallas as pl
from jax.experimental.pallas import tpu as pltpu
from jax.sharding import PartitionSpec as P

BF = jnp.bfloat16
F32 = jnp.float32
I32 = jnp.int32
LANES = 128
VMEM = pl.BlockSpec(memory_space=pltpu.VMEM)
ANY = pl.BlockSpec(memory_space=pl.ANY)
HBM = pl.BlockSpec(memory_space=pltpu.HBM)


def shape(dims, kind):
    return jax.ShapeDtypeStruct(tuple(dims), kind)


def run(kernel, outs, args, scratch=(), copies=1, far=(), here=(), flops=0):
    b, c = len(args), len(outs)

    def body(*refs):
        kernel(refs[-1], refs[:b], refs[b : b + c], refs[b + c : -1])

    moved = sum(a.size * a.dtype.itemsize for a in list(args) + list(outs))
    return pl.pallas_call(
        body,
        out_shape=list(outs),
        in_specs=[HBM if i in far else VMEM if i in here else ANY for i in range(len(args))],
        out_specs=[VMEM] * len(outs),
        scratch_shapes=list(scratch) + [pltpu.SemaphoreType.DMA((copies,))],
        compiler_params=pltpu.CompilerParams(vmem_limit_bytes=24 * 1024 * 1024),
        cost_estimate=pl.CostEstimate(flops=flops, bytes_accessed=moved, transcendentals=0),
    )(*args)


def begin(sems, pairs, first=0):
    copies = [
        pltpu.make_async_copy(source, target, sems.at[first + i])
        for i, (source, target) in enumerate(pairs)
    ]
    for copy in copies:
        copy.start()
    return copies


def end(copies):
    for copy in copies:
        copy.wait()


def down(row):
    return jnp.transpose(jnp.broadcast_to(row, (LANES, LANES)))


def ones_at(where):
    return jnp.where(where, 1.0, 0.0).astype(BF)


def pick_rows(row, source):
    numbers = down(row)
    lane = lax.broadcasted_iota(I32, (LANES, LANES), 1)
    hot = jnp.concatenate(
        [ones_at(numbers == lane + k * LANES) for k in range(source.shape[0] // LANES)], axis=1
    )
    return jnp.dot(hot, source, preferred_element_type=F32).astype(BF)


def set_rows(row, values, base_ref, out_ref):
    events = values.shape[0]
    tall = 256
    wide = jnp.concatenate([values, jnp.ones((events, LANES), BF)], axis=1)
    for i in range(out_ref.shape[0] // tall):
        own = lax.broadcasted_iota(I32, (tall, events), 0) + i * tall
        hot = ones_at(own == jnp.broadcast_to(row, (tall, events)))
        found = jnp.dot(hot, wide, preferred_element_type=F32)
        span = slice(i * tall, (i + 1) * tall)
        out_ref[span, :] = jnp.where(found[:, LANES:] > 0.5, found[:, :LANES], base_ref[span, :])


def padded(cap):
    return -(-cap // LANES) * LANES


def give(held, pieces):
    cap = pieces[0].shape[0]
    room = padded(cap)
    for k, piece in enumerate(pieces):
        piece[...] = held[k * room : k * room + cap, :]


def narrow_kernel(sems, given, made, scratch):
    end(begin(sems, [(given[0], scratch[0])]))
    made[0][...] = scratch[0][...].astype(BF)


def bundle_kernel(batch, sems, given, made, scratch):
    narrow_any, asked_any = given
    (out_ref,), (asked,) = made, scratch
    rows = narrow_any.shape[0]
    end(begin(sems, [(narrow_any, out_ref.at[:rows, :]), (asked_any, asked)]))
    lines = (out_ref.shape[0] - rows) // 2
    number = jnp.concatenate(
        [asked[batch : batch + 1, j * LANES : (j + 1) * LANES] for j in range(lines)], axis=0
    )
    high = jnp.floor(number.astype(F32) * (1.0 / 64.0))
    low = number.astype(F32) - 64.0 * high
    out_ref[rows:, :] = jnp.concatenate([high, low], axis=0).astype(BF)


def serve_kernel(sems, given, made, scratch):
    *asked_pieces, narrow_any = given
    asked_ref, *pieces = made
    narrow, held = scratch
    nodes, room = len(asked_pieces), asked_pieces[0].shape[1]
    pairs = [(narrow_any, narrow)]
    for k, piece in enumerate(asked_pieces):
        pairs.append((piece, asked_ref.at[:, k * room : (k + 1) * room]))
    end(begin(sems, pairs))
    for j in range(nodes * room // LANES):
        span = slice(j * LANES, (j + 1) * LANES)
        held[span, :] = pick_rows(asked_ref[0:1, span], narrow[...])
    give(held, pieces)


def pick_base(sems, memory_any, handed_any, base_ref, handed_ref, first):
    @pl.when(lax.axis_index("seg") == 0)
    def _():
        end(begin(sems, [(memory_any, base_ref)], first))

    @pl.when(lax.axis_index("seg") != 0)
    def _():
        end(begin(sems, [(handed_any, handed_ref)], first))
        base_ref[...] = handed_ref[: base_ref.shape[0], :].astype(base_ref.dtype)


def base_kernel(batch, sems, given, made, scratch):
    asked_any, narrow_any, handed_any = given
    put_ref, rows_ref = made
    asked, handed, narrow = scratch
    begun = begin(sems, [(asked_any, asked)])
    pick_base(sems, narrow_any, handed_any, narrow, handed, 1)
    end(begun)
    put_ref[...] = asked[batch : batch + 1, :]

    @pl.when(lax.axis_index("seg") != 0)
    def _():
        top = narrow.shape[0]
        lines = (handed.shape[0] - top) // 2
        digits = handed[top:, :].astype(F32)
        number = digits[:lines, :] * 64.0 + digits[lines:, :]
        for j in range(lines):
            put_ref[:, j * LANES : (j + 1) * LANES] = number[j : j + 1, :].astype(I32)

    for j in range(rows_ref.shape[0] // LANES):
        span = slice(j * LANES, (j + 1) * LANES)
        rows_ref[span, :] = pick_rows(asked[batch + 1 : batch + 2, span], narrow[...])


def gather_values(values, cap, pieces, sems, first):
    room = padded(cap)
    if room != cap:
        values[...] = jnp.zeros(values.shape, values.dtype)
    pairs = [(piece, values.at[k * room : k * room + cap, :]) for k, piece in enumerate(pieces)]
    return begin(sems, pairs, first)


def handed_kernel(first, sems, given, pieces, scratch):
    z = lax.axis_index("node")
    cap, few = pieces[0].shape[0], len(pieces)

    def send(source):
        pairs = []
        for k, piece in enumerate(pieces):
            at = pl.multiple_of(((z ^ (first + k)) % few) * cap, cap)
            pairs.append((source.at[pl.ds(at, cap), :], piece))
        end(begin(sems, pairs))

    @pl.when(lax.axis_index("seg") == 0)
    def _():
        send(given[0])

    @pl.when(lax.axis_index("seg") != 0)
    def _():
        send(given[1])


def next_kernel(batch, sems, given, made, scratch):
    asked_any, put_any, rows_any = given[:3]
    values_ref, pieces = made[0], made[1:]
    asked, put, rows, held = scratch
    cap = pieces[0].shape[0]
    begun = begin(sems, [(asked_any, asked), (put_any, put), (rows_any, rows)])
    end(gather_values(values_ref, cap, given[3:-1], sems, 3))
    end(begun)
    events = values_ref.shape[0]
    wide = jnp.concatenate([values_ref[...], jnp.ones((events, LANES), BF)], axis=1)
    written = jnp.where(put[...] < 0, -2, put[...])
    for j in range(events // LANES):
        span = slice(j * LANES, (j + 1) * LANES)
        numbers = down(asked[batch + 1 : batch + 2, span])
        hot = jnp.concatenate(
            [
                ones_at(
                    numbers
                    == jnp.broadcast_to(written[:, i * LANES : (i + 1) * LANES], (LANES, LANES))
                )
                for i in range(events // LANES)
            ],
            axis=1,
        )
        found = jnp.dot(hot, wide, preferred_element_type=F32)
        kept = rows[span, :].astype(F32)
        held[span, :] = jnp.where(found[:, LANES:] > 0.5, found[:, :LANES], kept).astype(BF)
    give(held, pieces)


def update_kernel(sems, given, made, scratch):
    put_any, values_any, memory_any, handed_any = given
    put, values, base, handed = scratch
    begun = begin(sems, [(put_any, put), (values_any, values)])
    pick_base(sems, memory_any, handed_any, base, handed, 2)
    end(begun)
    set_rows(put[...], values[...], base, made[0])


def last_kernel(batch, sems, given, made, scratch):
    asked_any, base_any, *pieces = given
    asked, values, base = scratch
    begun = begin(sems, [(asked_any, asked), (base_any, base)])
    end(gather_values(values, pieces[0].shape[0], pieces, sems, 2))
    end(begun)
    set_rows(asked[batch : batch + 1, :], values[...], base, made[0])
    made[1][...] = jnp.zeros(made[1].shape, F32)


def cosine(x):
    turns = jnp.round(x * 0.3183098861837907)
    r = x - turns * 3.140625
    r = r - turns * 0.0009670257568359375
    r = r - turns * 6.278329573009626e-07
    odd = turns - 2.0 * jnp.floor(turns * 0.5)
    q = r * r
    p = 2.08767569878681e-09 - q * 1.1470745597729725e-11
    p = q * p - 2.7557319223985893e-07
    p = q * p + 2.48015873015873e-05
    p = q * p - 0.001388888888888889
    p = q * p + 0.041666666666666664
    p = q * p - 0.5
    p = q * p + 1.0
    return p * (1.0 - 2.0 * odd)


def products(message, gates, sums, before, out_ref):
    long, width = message.shape[1], 2 * LANES
    tall = 256

    def put(start, value):
        stop = start + value.shape[0]
        if before is not None:
            value = value + before[start:stop, :]
        out_ref[start:stop, :] = value.astype(out_ref.dtype)

    for i in range(long // tall):
        rows = message[:, i * tall : (i + 1) * tall]
        columns = gates[...] if i * tall < width else gates[:, : 3 * LANES]
        product = lax.dot_general(
            rows, columns, (((0,), (0,)), ((), ())), preferred_element_type=F32
        )
        for g in range(3):
            put(g * long + i * tall, product[:, g * LANES : (g + 1) * LANES])
        if i * tall < width:
            put(3 * long + i * tall, product[:, 3 * LANES :])
    top = 3 * long + width
    pad = out_ref.shape[0] - top
    tail = jnp.concatenate(sums + [jnp.zeros((pad - 4, LANES), F32)], axis=0)
    put(top, tail)


def grads_kernel(sems, given, made, scratch):
    message, gates, sums = given
    products(message, gates, [sums[g : g + 1, :] for g in range(4)], None, made[0])


def side_kernel(batch, sems, given, made, scratch):
    facts_any, edge_any, edge_other_any = given
    facts, edge = scratch
    (side_ref,) = made
    events = side_ref.shape[0]
    thin = edge_any.shape[1]
    f = lax.axis_index("feat")
    own = pl.ds(pl.multiple_of(f * thin, thin), thin)
    other = pl.ds(pl.multiple_of((1 - f) * thin, thin), thin)
    pairs = [
        (facts_any, facts),
        (edge_any.at[batch], edge.at[own, :]),
        (edge_other_any.at[batch], edge.at[other, :]),
    ]
    end(begin(sems, pairs))
    lines = events // LANES
    top = facts.shape[0] - 8
    freq, phase = facts[top + 4 : top + 5, :], facts[top + 5 : top + 6, :]
    start = 2 * lines * batch + lines
    for j in range(lines):
        span = slice(j * LANES, (j + 1) * LANES)
        angle = down(facts[start + j : start + j + 1, :]) * freq + phase
        side_ref[span, :LANES] = cosine(angle).astype(BF)
        side_ref[span, LANES:] = jnp.transpose(edge[:, span].astype(F32)).astype(BF)


def batch_kernel(nodes, batch, final, prior, sems, given, made, scratch):
    facts_any, side_any, w_in_any, w_hid_any, up_any = given[:5]
    own_pieces, other_pieces = given[5 : 5 + nodes], given[5 + nodes : 5 + 2 * nodes]
    rest = given[5 + 2 * nodes :]
    message, facts, w_in, w_hid, gates, up, fresh = scratch[:7]
    if not final:
        message, gates = made[2:4]
    cap = own_pieces[0].shape[0]
    events = nodes * cap
    z, f = lax.axis_index("node"), lax.axis_index("feat")
    mine = pl.multiple_of(f * LANES, LANES)
    other = pl.multiple_of((1 - f) * LANES, LANES)
    width = 2 * LANES
    long = message.shape[1]
    pairs = [(facts_any, facts)]
    for k in range(nodes):
        at = pl.ds(pl.multiple_of((z ^ k) * cap, cap), cap)
        pairs.append((own_pieces[k], message.at[at, pl.ds(mine, LANES)]))
        pairs.append((other_pieces[k], message.at[at, pl.ds(other, LANES)]))
    late = [(side_any, message.at[:, 2 * width :]), (w_in_any, w_in), (w_hid_any, w_hid), (up_any.at[batch], up)]
    if prior:
        before = scratch[7]
        late.append((rest[0], before))
    rows_begun = begin(sems, pairs)
    late_begun = begin(sems, late, len(pairs))
    end(rows_begun)
    lines = events // LANES
    top = facts.shape[0] - 8
    bias_ref = facts[top : top + 4, :]
    dst = [facts[2 * lines * batch + j : 2 * lines * batch + j + 1, :] for j in range(lines)]
    full = message[:, :width]
    for j in range(events // LANES):
        span = slice(j * LANES, (j + 1) * LANES)
        message[span, width : 2 * width] = pick_rows(dst[j].astype(I32), full)
    end(late_begun)
    w_in01 = jnp.concatenate([w_in[0], w_in[1]], axis=1)
    w_hid01 = jnp.concatenate([w_hid[0], w_hid[1]], axis=1)
    sums = [jnp.zeros((1, LANES), F32) for _ in range(4)]
    tall = 256
    for i in range(events // tall):
        span = slice(i * tall, (i + 1) * tall)
        rows = message[span, :]
        hidden = rows[:, :width]
        both = jnp.dot(rows, w_in01, preferred_element_type=F32) + jnp.dot(
            hidden, w_hid01, preferred_element_type=F32
        )
        own = message[span, pl.ds(mine, LANES)].astype(F32)
        reset_gate = jax.nn.sigmoid(both[:, :LANES] + bias_ref[0:1, :])
        update = jax.nn.sigmoid(both[:, LANES:] + bias_ref[1:2, :])
        recur_term = jnp.dot(hidden, w_hid[2], preferred_element_type=F32) + bias_ref[3:4, :]
        candid = jnp.tanh(
            jnp.dot(rows, w_in[2], preferred_element_type=F32)
            + bias_ref[2:3, :]
            + reset_gate * recur_term
        )
        fresh[span, :] = ((1.0 - update) * candid + update * own).astype(BF)
        numbers = [down(dst[j]) for j in range(i * tall // LANES, (i + 1) * tall // LANES)]
        live = jnp.concatenate(numbers, axis=0) >= 0.0
        cotangent = jnp.where(live, up[span, :].astype(F32), 0.0)
        grad_cand = cotangent * (1.0 - update) * (1.0 - candid * candid)
        grad_upd = cotangent * (own - candid) * update * (1.0 - update)
        grad_reset = grad_cand * recur_term * reset_gate * (1.0 - reset_gate)
        grad_recur = grad_cand * reset_gate
        for g, part in enumerate((grad_reset, grad_upd, grad_cand, grad_recur)):
            sums[g] = sums[g] + jnp.sum(part, axis=0, keepdims=True)
            gates[span, g * LANES : (g + 1) * LANES] = part.astype(BF)
    if final:
        for k in range(nodes):
            made[k][...] = fresh[pl.ds(pl.multiple_of((z ^ k) * cap, cap), cap), :]
    else:
        few = events // 2
        upper = z // (nodes // 2)
        made[0][...] = fresh[pl.ds(pl.multiple_of((1 - upper) * few, few), few), :]
        made[1][...] = fresh[pl.ds(pl.multiple_of(upper * few, few), few), :]
    if final:
        products(message, gates, sums, before if prior else None, made[-1])
    else:
        made[4][...] = jnp.concatenate(sums + [jnp.zeros((4, LANES), F32)], axis=0)


def middle_kernel(nodes, segs, first, sems, given, made, scratch):
    totals, got = given[0], given[1:segs]
    rows = scratch[:segs]
    whole = scratch[segs]
    few, chunk = len(made), made[0].shape[0]
    z = lax.axis_index("node")
    side = (z ^ first) // few
    share = few * chunk
    at = pl.ds(pl.multiple_of((lax.axis_index("seg") * 2 + side) * share, share), share)
    pairs = [(totals.at[at, :], rows[0])] + list(zip(got, rows[1:]))
    end(begin(sems, pairs))
    total = rows[0][...].astype(F32)
    for x in range(1, segs):
        total = total + rows[x][...].astype(F32)
    whole[...] = total.astype(BF)
    for k in range(few):
        at = pl.multiple_of(((z ^ (first + k)) % few) * chunk, chunk)
        made[k][...] = whole[pl.ds(at, chunk), :]


def sum_kernel(sems, given, made, scratch):
    end(begin(sems, list(zip(given, scratch))))
    total = scratch[0][...].astype(F32)
    for part in scratch[1:]:
        total = total + part[...].astype(F32)
    made[0][...] = total.astype(BF)


def widen_kernel(sems, given, made, scratch):
    (out_ref,), rows = made, given[0].shape[0]
    end(begin(sems, list(zip(given, scratch))))
    for x, part in enumerate(scratch):
        out_ref[x * rows : (x + 1) * rows, :] = part[...].astype(F32)


def unpack_kernel(nodes, segs, long, sems, pieces, made, scratch):
    grad_in, grad_hid, grad_bias = made
    held, *far = scratch
    few = nodes // 2
    chunk = pieces[1].shape[0] // few
    z, s = lax.axis_index("node"), lax.axis_index("seg")

    def place(x, k):
        at = pl.multiple_of(((s ^ x) * nodes + (z ^ k)) * chunk, chunk)
        return pl.ds(at, chunk)

    pairs = list(zip(pieces[1:], far))
    for x in range(segs):
        for k in range(few):
            i = x * few + k
            pairs.append((pieces[0].at[i * chunk : (i + 1) * chunk, :], held.at[place(x, k), :]))
    end(begin(sems, pairs))
    for x in range(segs):
        for k in range(few):
            held[place(x, few + k), :] = far[x][k * chunk : (k + 1) * chunk, :].astype(F32)
    width = grad_hid.shape[1]
    for g in range(3):
        grad_in[g] = held[g * long : (g + 1) * long, :].astype(F32)
    for g in range(2):
        grad_hid[g] = held[g * long : g * long + width, :].astype(F32)
    grad_hid[2] = held[3 * long : 3 * long + width, :].astype(F32)
    top = 3 * long + width
    grad_bias[...] = held[top : top + 16, :].astype(F32)[:4, :]


def local(
    memory, req_rows, req_count, dst_slot, elapsed, edges, upstream, freq, phase, w_input, w_hidden, bias
):
    nodes, segs = lax.axis_size("node"), lax.axis_size("seg")
    z, s = lax.axis_index("node"), lax.axis_index("seg")
    memory_now = memory[0]
    node_rows, half = memory_now.shape
    batches, cap = req_rows.shape[0], req_rows.shape[-1]
    events = nodes * cap
    room = padded(cap)
    spread = nodes * room
    counts = req_count[:, 0, 0]
    piece = shape((cap, half), BF)
    long, width = w_input.shape[1], w_hidden.shape[1]

    def node_swap(block, k):
        return lax.ppermute(block, "node", [(i, i ^ k) for i in range(nodes)])

    def seg_swap(block, x):
        return lax.ppermute(block, "seg", [(i, i ^ x) for i in range(segs)])

    def seg_next(block):
        return lax.ppermute(block, "seg", [(i, i + 1) for i in range(segs - 1)])

    def feat_swap(block):
        return lax.ppermute(block, "feat", [(0, 1), (1, 0)])

    def exchange(blocks):
        return [blocks[0]] + [node_swap(blocks[k], k) for k in range(1, nodes)]

    live = jnp.arange(cap)[None, None, :] < counts[:, :, None]
    masked = jnp.where(live, req_rows[:, 0, 0], -1)
    masked = jnp.pad(masked, ((0, 0), (0, 0), (0, room - cap)), constant_values=-1)
    wanted = exchange(
        [lax.dynamic_index_in_dim(masked, z ^ k, 1, keepdims=False) for k in range(nodes)]
    )
    wide_rows = pltpu.VMEM((spread, half), BF)
    edge_own = jnp.swapaxes(edges[:, 0], 1, 2)
    edge_other = feat_swap(edge_own)
    lines = events // LANES
    named = jnp.where(live, dst_slot[:, 0].reshape(live.shape), -1)
    facts = jnp.stack([named.reshape(batches, events), elapsed[:, 0]], axis=1).astype(F32)
    facts = facts.reshape(batches * 2 * lines, LANES)
    rest = jnp.zeros((2, half), F32)
    facts = jnp.concatenate([facts, bias, freq[None], phase[None], rest], axis=0)

    narrow = run(
        narrow_kernel,
        [shape((node_rows, half), BF)],
        [memory_now, wanted[1], facts],
        [pltpu.VMEM((node_rows, half), F32)],
        1,
        (0,),
    )[0]
    asked, *served = run(
        serve_kernel,
        [shape((batches, spread), I32)] + [piece] * nodes,
        wanted + [narrow],
        [pltpu.VMEM((node_rows, half), BF), wide_rows],
        nodes + 1,
    )

    chunk = -(-(3 * long + width + 16) // (16 * nodes * segs)) * 16
    total_rows = chunk * nodes * segs
    numbers = pltpu.VMEM((batches, spread), I32)
    line = pltpu.VMEM((1, spread), I32)
    block = pltpu.VMEM((node_rows, half), F32)
    totals = None
    for b in range(batches):
        final = b + 1 == batches
        own_pieces = exchange(served)
        if not final:
            bundle = run(
                lambda *a, b=b: bundle_kernel(b, *a),
                [shape((node_rows + 2 * spread // LANES, half), BF)],
                [narrow, asked],
                [numbers],
                2,
            )[0]
            handed_memory = seg_next(bundle)
        other_pieces = [feat_swap(p) for p in own_pieces]
        beside = run(
            lambda *a, b=b: side_kernel(b, *a),
            [shape((events, 2 * LANES), BF)],
            [facts, edge_own, edge_other],
            [pltpu.VMEM(facts.shape, F32), pltpu.VMEM((2 * edges.shape[-1], events), BF)],
            3,
        )[0]
        given = [facts, beside, w_input, w_hidden, upstream[:, 0]]
        given = given + own_pieces + other_pieces + ([] if totals is None else [totals])
        rooms = [
            pltpu.VMEM((events, long), BF),
            pltpu.VMEM(facts.shape, F32),
            pltpu.VMEM(w_input.shape, BF),
            pltpu.VMEM(w_hidden.shape, BF),
            pltpu.VMEM((events, 4 * half), BF),
            pltpu.VMEM((events, half), BF),
            pltpu.VMEM((events, half), BF),
        ]
        if totals is not None:
            rooms.append(pltpu.VMEM((total_rows, half), F32))
        copies = 7 + 2 * nodes
        before_grads = [shape((events // 2, half), BF)] * 2 + [
            shape((events, long), BF),
            shape((events, 4 * half), BF),
            shape((8, half), F32),
        ]
        outs = run(
            lambda *a, b=b, last=final, p=totals is not None: batch_kernel(nodes, b, last, p, *a),
            [piece] * nodes + [shape((total_rows, half), BF)] if final else before_grads,
            given,
            rooms,
            copies,
            (),
        )
        if final:
            fresh, totals = outs[:-1], outs[-1]
        else:
            assert b == 0
            fresh = outs[:2]
            totals = run(
                grads_kernel, [shape((total_rows, half), F32)], outs[2:], [], 1, (), (0, 1, 2)
            )[0]
        if not final:
            hops = [seg_next(side) for side in fresh]
            put, rows = run(
                lambda *a, b=b: base_kernel(b, *a),
                [shape((1, spread), I32), shape((spread, half), BF)],
                [asked, narrow, handed_memory],
                [numbers, pltpu.VMEM(bundle.shape, BF), pltpu.VMEM((node_rows, half), BF)],
                2,
            )
            few = nodes // 2
            values = [None] * nodes
            for side, first in ((0, few), (1, 0)):
                values[first : first + few] = run(
                    lambda *a, first=first: handed_kernel(first, *a),
                    [piece] * few,
                    [fresh[side], hops[side]] + ([rows] if side == 1 else []),
                    [],
                    few,
                )
            values = exchange(values)
            values, *served = run(
                lambda *a, b=b: next_kernel(b, *a),
                [shape((spread, half), BF)] + [piece] * nodes,
                [asked, put, rows] + values + [totals],
                [numbers, line, wide_rows, wide_rows],
                3 + nodes,
            )
            memory_now = run(
                update_kernel,
                [shape((node_rows, half), F32)],
                [put, values, memory_now, handed_memory],
                [line, wide_rows, block, pltpu.VMEM(bundle.shape, BF)],
                3,
            )[0]
            if b + 2 < batches:
                narrow = memory_now.astype(BF)
        else:
            returned = exchange(fresh)
            memory_out, done = run(
                lambda *a, b=b: last_kernel(b, *a),
                [shape((node_rows, half), F32), shape((8, half), F32)],
                [asked, memory_now] + returned,
                [numbers, wide_rows, block],
                2 + nodes,
            )

    def at(blocks, i):
        return lax.dynamic_index_in_dim(blocks, i, 0, keepdims=False)

    few = nodes // 2
    upper = z // few
    blocks = totals.reshape(segs, 2, few * chunk, half)
    got = [
        [seg_swap(at(at(blocks, s ^ x), side), x) for x in range(1, segs)]
        for side in (1 - upper, upper)
    ]
    share = pltpu.VMEM((few * chunk, half), BF)
    parts = [None] * nodes
    for side, first in ((0, few), (1, 0)):
        parts[first : first + few] = run(
            lambda *a, first=first: middle_kernel(nodes, segs, first, *a),
            [shape((chunk, half), BF)] * few,
            [totals] + got[side] + ([] if side else returned[1:]),
            [share] * (segs + 1),
            segs,
        )
    parts = exchange(parts)
    summed = run(
        sum_kernel,
        [shape((chunk, half), BF)],
        parts + [done],
        [pltpu.VMEM((chunk, half), BF)] * nodes,
        nodes,
    )[0]
    around = [summed] + [node_swap(summed, k) for k in range(1, nodes)]
    sides = [jnp.concatenate(around[:few], axis=0), jnp.concatenate(around[few:], axis=0)]
    near, distant = ([side] + [seg_swap(side, x) for x in range(1, segs)] for side in sides)
    gathered = run(
        widen_kernel,
        [shape((segs * few * chunk, half), F32)],
        near,
        [share] * segs,
        segs,
        flops=0,
    )
    gathered = [gathered[0]] + distant
    grads = run(
        lambda *a: unpack_kernel(nodes, segs, long, *a),
        [shape(w_input.shape, F32), shape(w_hidden.shape, F32), shape(bias.shape, F32)],
        gathered,
        [pltpu.VMEM((total_rows, half), F32)] + [share] * segs,
        segs + few * segs,
    )
    return (memory_out[None], *grads)


def solution(mesh):
    in_specs = (
        P(("parts", "seg"), "node", "feat"),
        P(None, ("parts", "seg"), "node", None, None),
        P(None, ("parts", "seg"), "node", None),
        P(None, ("parts", "seg"), "node"),
        P(None, ("parts", "seg"), "node"),
        P(None, ("parts", "seg"), "node", "feat"),
        P(None, ("parts", "seg"), "node", "feat"),
        P(),
        P(),
        P(None, None, "feat"),
        P(None, None, "feat"),
        P(None, "feat"),
    )
    out_specs = (
        P(("parts", "seg"), "node", "feat"),
        P("parts", None, "feat"),
        P("parts", None, "feat"),
        P("parts", "feat"),
    )
    return jax.shard_map(local, mesh=mesh, in_specs=in_specs, out_specs=out_specs, check_vma=False)
```

```python
import jax
import jax.numpy as jnp
from jax import lax
from jax.experimental import pallas as pl
from jax.experimental.pallas import tpu as pltpu
from jax.sharding import PartitionSpec as P

BF = jnp.bfloat16
F32 = jnp.float32
I32 = jnp.int32
LANES = 128
VMEM = pl.BlockSpec(memory_space=pltpu.VMEM)
ANY = pl.BlockSpec(memory_space=pl.ANY)
HBM = pl.BlockSpec(memory_space=pltpu.HBM)


def shape(dims, kind):
    return jax.ShapeDtypeStruct(tuple(dims), kind)


def run(kernel, outs, args, scratch=(), copies=1, far=(), here=(), flops=0):
    b, c = len(args), len(outs)

    def body(*refs):
        kernel(refs[-1], refs[:b], refs[b : b + c], refs[b + c : -1])

    moved = sum(a.size * a.dtype.itemsize for a in list(args) + list(outs))
    return pl.pallas_call(
        body,
        out_shape=list(outs),
        in_specs=[HBM if i in far else VMEM if i in here else ANY for i in range(len(args))],
        out_specs=[VMEM] * len(outs),
        scratch_shapes=list(scratch) + [pltpu.SemaphoreType.DMA((copies,))],
        compiler_params=pltpu.CompilerParams(vmem_limit_bytes=24 * 1024 * 1024),
        cost_estimate=pl.CostEstimate(flops=flops, bytes_accessed=moved, transcendentals=0),
    )(*args)


def begin(sems, pairs, first=0):
    copies = [
        pltpu.make_async_copy(source, target, sems.at[first + i])
        for i, (source, target) in enumerate(pairs)
    ]
    for copy in copies:
        copy.start()
    return copies


def end(copies):
    for copy in copies:
        copy.wait()


def down(row):
    return jnp.transpose(jnp.broadcast_to(row, (LANES, LANES)))


def ones_at(where):
    return jnp.where(where, 1.0, 0.0).astype(BF)


def pick_rows(row, source):
    numbers = down(row)
    lane = lax.broadcasted_iota(I32, (LANES, LANES), 1)
    hot = jnp.concatenate(
        [ones_at(numbers == lane + k * LANES) for k in range(source.shape[0] // LANES)], axis=1
    )
    return jnp.dot(hot, source, preferred_element_type=F32).astype(BF)


def set_rows(row, values, base_ref, out_ref):
    events = values.shape[0]
    tall = 256
    wide = jnp.concatenate([values, jnp.ones((events, LANES), BF)], axis=1)
    for i in range(out_ref.shape[0] // tall):
        own = lax.broadcasted_iota(I32, (tall, events), 0) + i * tall
        hot = ones_at(own == jnp.broadcast_to(row, (tall, events)))
        found = jnp.dot(hot, wide, preferred_element_type=F32)
        span = slice(i * tall, (i + 1) * tall)
        out_ref[span, :] = jnp.where(found[:, LANES:] > 0.5, found[:, :LANES], base_ref[span, :])


def padded(cap):
    return -(-cap // LANES) * LANES


def give(held, pieces):
    cap = pieces[0].shape[0]
    room = padded(cap)
    for k, piece in enumerate(pieces):
        piece[...] = held[k * room : k * room + cap, :]


def narrow_kernel(sems, given, made, scratch):
    end(begin(sems, [(given[0], scratch[0])]))
    made[0][...] = scratch[0][...].astype(BF)


def bundle_kernel(batch, sems, given, made, scratch):
    narrow_any, asked_any = given
    (out_ref,), (asked,) = made, scratch
    rows = narrow_any.shape[0]
    end(begin(sems, [(narrow_any, out_ref.at[:rows, :]), (asked_any, asked)]))
    lines = (out_ref.shape[0] - rows) // 2
    number = jnp.concatenate(
        [asked[batch : batch + 1, j * LANES : (j + 1) * LANES] for j in range(lines)], axis=0
    )
    high = jnp.floor(number.astype(F32) * (1.0 / 64.0))
    low = number.astype(F32) - 64.0 * high
    out_ref[rows:, :] = jnp.concatenate([high, low], axis=0).astype(BF)


def serve_kernel(sems, given, made, scratch):
    *asked_pieces, narrow_any = given
    asked_ref, *pieces = made
    narrow, held = scratch
    nodes, room = len(asked_pieces), asked_pieces[0].shape[1]
    pairs = [(narrow_any, narrow)]
    for k, piece in enumerate(asked_pieces):
        pairs.append((piece, asked_ref.at[:, k * room : (k + 1) * room]))
    end(begin(sems, pairs))
    for j in range(nodes * room // LANES):
        span = slice(j * LANES, (j + 1) * LANES)
        held[span, :] = pick_rows(asked_ref[0:1, span], narrow[...])
    give(held, pieces)


def pick_base(sems, memory_any, handed_any, base_ref, handed_ref, first):
    @pl.when(lax.axis_index("seg") == 0)
    def _():
        end(begin(sems, [(memory_any, base_ref)], first))

    @pl.when(lax.axis_index("seg") != 0)
    def _():
        end(begin(sems, [(handed_any, handed_ref)], first))
        base_ref[...] = handed_ref[: base_ref.shape[0], :].astype(base_ref.dtype)


def base_kernel(batch, sems, given, made, scratch):
    asked_any, narrow_any, handed_any = given
    put_ref, rows_ref = made
    asked, handed, narrow = scratch
    begun = begin(sems, [(asked_any, asked)])
    pick_base(sems, narrow_any, handed_any, narrow, handed, 1)
    end(begun)
    put_ref[...] = asked[batch : batch + 1, :]

    @pl.when(lax.axis_index("seg") != 0)
    def _():
        top = narrow.shape[0]
        lines = (handed.shape[0] - top) // 2
        digits = handed[top:, :].astype(F32)
        number = digits[:lines, :] * 64.0 + digits[lines:, :]
        for j in range(lines):
            put_ref[:, j * LANES : (j + 1) * LANES] = number[j : j + 1, :].astype(I32)

    for j in range(rows_ref.shape[0] // LANES):
        span = slice(j * LANES, (j + 1) * LANES)
        rows_ref[span, :] = pick_rows(asked[batch + 1 : batch + 2, span], narrow[...])


def gather_values(values, cap, pieces, sems, first):
    room = padded(cap)
    if room != cap:
        values[...] = jnp.zeros(values.shape, values.dtype)
    pairs = [(piece, values.at[k * room : k * room + cap, :]) for k, piece in enumerate(pieces)]
    return begin(sems, pairs, first)


def handed_kernel(first, sems, given, pieces, scratch):
    z = lax.axis_index("node")
    cap, few = pieces[0].shape[0], len(pieces)

    def send(source):
        pairs = []
        for k, piece in enumerate(pieces):
            at = pl.multiple_of(((z ^ (first + k)) % few) * cap, cap)
            pairs.append((source.at[pl.ds(at, cap), :], piece))
        end(begin(sems, pairs))

    @pl.when(lax.axis_index("seg") == 0)
    def _():
        send(given[0])

    @pl.when(lax.axis_index("seg") != 0)
    def _():
        send(given[1])


def next_kernel(batch, sems, given, made, scratch):
    asked_any, put_any, rows_any = given[:3]
    values_ref, pieces = made[0], made[1:]
    asked, put, rows, held = scratch
    cap = pieces[0].shape[0]
    begun = begin(sems, [(asked_any, asked), (put_any, put), (rows_any, rows)])
    end(gather_values(values_ref, cap, given[3:-1], sems, 3))
    end(begun)
    events = values_ref.shape[0]
    wide = jnp.concatenate([values_ref[...], jnp.ones((events, LANES), BF)], axis=1)
    written = jnp.where(put[...] < 0, -2, put[...])
    for j in range(events // LANES):
        span = slice(j * LANES, (j + 1) * LANES)
        numbers = down(asked[batch + 1 : batch + 2, span])
        hot = jnp.concatenate(
            [
                ones_at(
                    numbers
                    == jnp.broadcast_to(written[:, i * LANES : (i + 1) * LANES], (LANES, LANES))
                )
                for i in range(events // LANES)
            ],
            axis=1,
        )
        found = jnp.dot(hot, wide, preferred_element_type=F32)
        kept = rows[span, :].astype(F32)
        held[span, :] = jnp.where(found[:, LANES:] > 0.5, found[:, :LANES], kept).astype(BF)
    give(held, pieces)


def update_kernel(sems, given, made, scratch):
    put_any, values_any, memory_any, handed_any = given
    put, values, base, handed = scratch
    begun = begin(sems, [(put_any, put), (values_any, values)])
    pick_base(sems, memory_any, handed_any, base, handed, 2)
    end(begun)
    set_rows(put[...], values[...], base, made[0])


def last_kernel(batch, sems, given, made, scratch):
    asked_any, base_any, *pieces = given
    asked, values, base = scratch
    begun = begin(sems, [(asked_any, asked), (base_any, base)])
    end(gather_values(values, pieces[0].shape[0], pieces, sems, 2))
    end(begun)
    set_rows(asked[batch : batch + 1, :], values[...], base, made[0])
    made[1][...] = jnp.zeros(made[1].shape, F32)


def cosine(x):
    turns = jnp.round(x * 0.3183098861837907)
    r = x - turns * 3.140625
    r = r - turns * 0.0009670257568359375
    r = r - turns * 6.278329573009626e-07
    odd = turns - 2.0 * jnp.floor(turns * 0.5)
    q = r * r
    p = 2.08767569878681e-09 - q * 1.1470745597729725e-11
    p = q * p - 2.7557319223985893e-07
    p = q * p + 2.48015873015873e-05
    p = q * p - 0.001388888888888889
    p = q * p + 0.041666666666666664
    p = q * p - 0.5
    p = q * p + 1.0
    return p * (1.0 - 2.0 * odd)


def products(message, gates, sums, before, out_ref):
    long, width = message.shape[1], 2 * LANES
    tall = 256

    def put(start, value):
        stop = start + value.shape[0]
        if before is not None:
            value = value + before[start:stop, :]
        out_ref[start:stop, :] = value.astype(out_ref.dtype)

    for i in range(long // tall):
        rows = message[:, i * tall : (i + 1) * tall]
        columns = gates[...] if i * tall < width else gates[:, : 3 * LANES]
        product = lax.dot_general(
            rows, columns, (((0,), (0,)), ((), ())), preferred_element_type=F32
        )
        for g in range(3):
            put(g * long + i * tall, product[:, g * LANES : (g + 1) * LANES])
        if i * tall < width:
            put(3 * long + i * tall, product[:, 3 * LANES :])
    top = 3 * long + width
    pad = out_ref.shape[0] - top
    tail = jnp.concatenate(sums + [jnp.zeros((pad - 4, LANES), F32)], axis=0)
    put(top, tail)


def grads_kernel(sems, given, made, scratch):
    message, gates, sums = given
    products(message, gates, [sums[g : g + 1, :] for g in range(4)], None, made[0])


def side_kernel(batch, sems, given, made, scratch):
    facts_any, edge_any, edge_other_any = given
    facts, edge = scratch
    (side_ref,) = made
    events = side_ref.shape[0]
    thin = edge_any.shape[1]
    f = lax.axis_index("feat")
    own = pl.ds(pl.multiple_of(f * thin, thin), thin)
    other = pl.ds(pl.multiple_of((1 - f) * thin, thin), thin)
    pairs = [
        (facts_any, facts),
        (edge_any.at[batch], edge.at[own, :]),
        (edge_other_any.at[batch], edge.at[other, :]),
    ]
    end(begin(sems, pairs))
    lines = events // LANES
    top = facts.shape[0] - 8
    freq, phase = facts[top + 4 : top + 5, :], facts[top + 5 : top + 6, :]
    start = 2 * lines * batch + lines
    for j in range(lines):
        span = slice(j * LANES, (j + 1) * LANES)
        angle = down(facts[start + j : start + j + 1, :]) * freq + phase
        side_ref[span, :LANES] = cosine(angle).astype(BF)
        side_ref[span, LANES:] = jnp.transpose(edge[:, span].astype(F32)).astype(BF)


def batch_kernel(nodes, batch, final, prior, sems, given, made, scratch):
    facts_any, side_any, w_any, up_any = given[:4]
    own_pieces, other_pieces = given[4 : 4 + nodes], given[4 + nodes : 4 + 2 * nodes]
    rest = given[4 + 2 * nodes :]
    message, facts, w_ref, gates, up, fresh = scratch[:6]
    if not final:
        message, gates = made[2:4]
    cap = own_pieces[0].shape[0]
    events = nodes * cap
    z, f = lax.axis_index("node"), lax.axis_index("feat")
    mine = pl.multiple_of(f * LANES, LANES)
    other = pl.multiple_of((1 - f) * LANES, LANES)
    width = 2 * LANES
    long = message.shape[1]
    pairs = [(facts_any, facts)]
    for k in range(nodes):
        at = pl.ds(pl.multiple_of((z ^ k) * cap, cap), cap)
        pairs.append((own_pieces[k], message.at[at, pl.ds(mine, LANES)]))
        pairs.append((other_pieces[k], message.at[at, pl.ds(other, LANES)]))
    late = [(side_any, message.at[:, 2 * width :]), (w_any, w_ref), (up_any.at[batch], up)]
    if prior:
        before = scratch[6]
        late.append((rest[0], before))
    rows_begun = begin(sems, pairs)
    late_begun = begin(sems, late, len(pairs))
    end(rows_begun)
    lines = events // LANES
    top = facts.shape[0] - 8
    bias_ref = facts[top : top + 4, :]
    dst = [facts[2 * lines * batch + j : 2 * lines * batch + j + 1, :] for j in range(lines)]
    full = message[:, :width]
    for j in range(events // LANES):
        span = slice(j * LANES, (j + 1) * LANES)
        message[span, width : 2 * width] = pick_rows(dst[j].astype(I32), full)
    end(late_begun)
    w_in = [w_ref[g, :long, :] for g in range(3)]
    w_hid = [w_ref[g, long:, :] for g in range(3)]
    w_in01 = jnp.concatenate([w_in[0], w_in[1]], axis=1)
    w_hid01 = jnp.concatenate([w_hid[0], w_hid[1]], axis=1)
    sums = [jnp.zeros((1, LANES), F32) for _ in range(4)]
    tall = 256
    for i in range(events // tall):
        span = slice(i * tall, (i + 1) * tall)
        rows = message[span, :]
        hidden = rows[:, :width]
        both = jnp.dot(rows, w_in01, preferred_element_type=F32) + jnp.dot(
            hidden, w_hid01, preferred_element_type=F32
        )
        own = message[span, pl.ds(mine, LANES)].astype(F32)
        reset_gate = jax.nn.sigmoid(both[:, :LANES] + bias_ref[0:1, :])
        update = jax.nn.sigmoid(both[:, LANES:] + bias_ref[1:2, :])
        recur_term = jnp.dot(hidden, w_hid[2], preferred_element_type=F32) + bias_ref[3:4, :]
        candid = jnp.tanh(
            jnp.dot(rows, w_in[2], preferred_element_type=F32)
            + bias_ref[2:3, :]
            + reset_gate * recur_term
        )
        fresh[span, :] = ((1.0 - update) * candid + update * own).astype(BF)
        numbers = [down(dst[j]) for j in range(i * tall // LANES, (i + 1) * tall // LANES)]
        live = jnp.concatenate(numbers, axis=0) >= 0.0
        cotangent = jnp.where(live, up[span, :].astype(F32), 0.0)
        grad_cand = cotangent * (1.0 - update) * (1.0 - candid * candid)
        grad_upd = cotangent * (own - candid) * update * (1.0 - update)
        grad_reset = grad_cand * recur_term * reset_gate * (1.0 - reset_gate)
        grad_recur = grad_cand * reset_gate
        for g, part in enumerate((grad_reset, grad_upd, grad_cand, grad_recur)):
            sums[g] = sums[g] + jnp.sum(part, axis=0, keepdims=True)
            gates[span, g * LANES : (g + 1) * LANES] = part.astype(BF)
    if final:
        for k in range(nodes):
            made[k][...] = fresh[pl.ds(pl.multiple_of((z ^ k) * cap, cap), cap), :]
    else:
        few = events // 2
        upper = z // (nodes // 2)
        made[0][...] = fresh[pl.ds(pl.multiple_of((1 - upper) * few, few), few), :]
        made[1][...] = fresh[pl.ds(pl.multiple_of(upper * few, few), few), :]
    if final:
        products(message, gates, sums, before if prior else None, made[-1])
    else:
        made[4][...] = jnp.concatenate(sums + [jnp.zeros((4, LANES), F32)], axis=0)


def middle_kernel(nodes, segs, first, sems, given, made, scratch):
    totals, got = given[0], given[1:segs]
    rows = scratch[:segs]
    whole = scratch[segs]
    few, chunk = len(made), made[0].shape[0]
    z = lax.axis_index("node")
    side = (z ^ first) // few
    share = few * chunk
    at = pl.ds(pl.multiple_of((lax.axis_index("seg") * 2 + side) * share, share), share)
    pairs = [(totals.at[at, :], rows[0])] + list(zip(got, rows[1:]))
    end(begin(sems, pairs))
    total = rows[0][...].astype(F32)
    for x in range(1, segs):
        total = total + rows[x][...].astype(F32)
    whole[...] = total.astype(BF)
    for k in range(few):
        at = pl.multiple_of(((z ^ (first + k)) % few) * chunk, chunk)
        made[k][...] = whole[pl.ds(at, chunk), :]


def sum_kernel(sems, given, made, scratch):
    end(begin(sems, list(zip(given, scratch))))
    total = scratch[0][...].astype(F32)
    for part in scratch[1:]:
        total = total + part[...].astype(F32)
    made[0][...] = total.astype(BF)


def widen_kernel(sems, given, made, scratch):
    (out_ref,), rows = made, given[0].shape[0]
    end(begin(sems, list(zip(given, scratch))))
    for x, part in enumerate(scratch):
        out_ref[x * rows : (x + 1) * rows, :] = part[...].astype(F32)


def unpack_kernel(nodes, segs, long, sems, pieces, made, scratch):
    grad_in, grad_hid, grad_bias = made
    held, *far = scratch
    few = nodes // 2
    chunk = pieces[1].shape[0] // few
    z, s = lax.axis_index("node"), lax.axis_index("seg")

    def place(x, k):
        at = pl.multiple_of(((s ^ x) * nodes + (z ^ k)) * chunk, chunk)
        return pl.ds(at, chunk)

    pairs = list(zip(pieces[1:], far))
    for x in range(segs):
        for k in range(few):
            i = x * few + k
            pairs.append((pieces[0].at[i * chunk : (i + 1) * chunk, :], held.at[place(x, k), :]))
    end(begin(sems, pairs))
    for x in range(segs):
        for k in range(few):
            held[place(x, few + k), :] = far[x][k * chunk : (k + 1) * chunk, :].astype(F32)
    width = grad_hid.shape[1]
    for g in range(3):
        grad_in[g] = held[g * long : (g + 1) * long, :].astype(F32)
    for g in range(2):
        grad_hid[g] = held[g * long : g * long + width, :].astype(F32)
    grad_hid[2] = held[3 * long : 3 * long + width, :].astype(F32)
    top = 3 * long + width
    grad_bias[...] = held[top : top + 16, :].astype(F32)[:4, :]


def local(
    memory, req_rows, req_count, dst_slot, elapsed, edges, upstream, freq, phase, w_input, w_hidden, bias
):
    nodes, segs = lax.axis_size("node"), lax.axis_size("seg")
    z, s = lax.axis_index("node"), lax.axis_index("seg")
    memory_now = memory[0]
    node_rows, half = memory_now.shape
    batches, cap = req_rows.shape[0], req_rows.shape[-1]
    events = nodes * cap
    room = padded(cap)
    spread = nodes * room
    counts = req_count[:, 0, 0]
    piece = shape((cap, half), BF)
    long, width = w_input.shape[1], w_hidden.shape[1]

    def node_swap(block, k):
        return lax.ppermute(block, "node", [(i, i ^ k) for i in range(nodes)])

    def seg_swap(block, x):
        return lax.ppermute(block, "seg", [(i, i ^ x) for i in range(segs)])

    def seg_next(block):
        return lax.ppermute(block, "seg", [(i, i + 1) for i in range(segs - 1)])

    def feat_swap(block):
        return lax.ppermute(block, "feat", [(0, 1), (1, 0)])

    def exchange(blocks):
        return [blocks[0]] + [node_swap(blocks[k], k) for k in range(1, nodes)]

    live = jnp.arange(cap)[None, None, :] < counts[:, :, None]
    masked = jnp.where(live, req_rows[:, 0, 0], -1)
    masked = jnp.pad(masked, ((0, 0), (0, 0), (0, room - cap)), constant_values=-1)
    wanted = exchange(
        [lax.dynamic_index_in_dim(masked, z ^ k, 1, keepdims=False) for k in range(nodes)]
    )
    wide_rows = pltpu.VMEM((spread, half), BF)
    edge_own = jnp.swapaxes(edges[:, 0], 1, 2)
    edge_other = feat_swap(edge_own)
    lines = events // LANES
    named = jnp.where(live, dst_slot[:, 0].reshape(live.shape), -1)
    facts = jnp.stack([named.reshape(batches, events), elapsed[:, 0]], axis=1).astype(F32)
    facts = facts.reshape(batches * 2 * lines, LANES)
    rest = jnp.zeros((2, half), F32)
    facts = jnp.concatenate([facts, bias, freq[None], phase[None], rest], axis=0)

    weights = jnp.concatenate([w_input, w_hidden], axis=1)
    narrow = run(
        narrow_kernel,
        [shape((node_rows, half), BF)],
        [memory_now, wanted[1], facts, weights],
        [pltpu.VMEM((node_rows, half), F32)],
        1,
        (0,),
    )[0]
    asked, *served = run(
        serve_kernel,
        [shape((batches, spread), I32)] + [piece] * nodes,
        wanted + [narrow],
        [pltpu.VMEM((node_rows, half), BF), wide_rows],
        nodes + 1,
    )

    chunk = -(-(3 * long + width + 16) // (16 * nodes * segs)) * 16
    total_rows = chunk * nodes * segs
    numbers = pltpu.VMEM((batches, spread), I32)
    line = pltpu.VMEM((1, spread), I32)
    block = pltpu.VMEM((node_rows, half), F32)
    totals = None
    for b in range(batches):
        final = b + 1 == batches
        own_pieces = exchange(served)
        if not final:
            bundle = run(
                lambda *a, b=b: bundle_kernel(b, *a),
                [shape((node_rows + 2 * spread // LANES, half), BF)],
                [narrow, asked],
                [numbers],
                2,
            )[0]
            handed_memory = seg_next(bundle)
        other_pieces = [feat_swap(p) for p in own_pieces]
        beside = run(
            lambda *a, b=b: side_kernel(b, *a),
            [shape((events, 2 * LANES), BF)],
            [facts, edge_own, edge_other],
            [pltpu.VMEM(facts.shape, F32), pltpu.VMEM((2 * edges.shape[-1], events), BF)],
            3,
        )[0]
        given = [facts, beside, weights, upstream[:, 0]]
        given = given + own_pieces + other_pieces + ([] if totals is None else [totals])
        rooms = [
            pltpu.VMEM((events, long), BF),
            pltpu.VMEM(facts.shape, F32),
            pltpu.VMEM(weights.shape, BF),
            pltpu.VMEM((events, 4 * half), BF),
            pltpu.VMEM((events, half), BF),
            pltpu.VMEM((events, half), BF),
        ]
        if totals is not None:
            rooms.append(pltpu.VMEM((total_rows, half), F32))
        copies = 7 + 2 * nodes
        before_grads = [shape((events // 2, half), BF)] * 2 + [
            shape((events, long), BF),
            shape((events, 4 * half), BF),
            shape((8, half), F32),
        ]
        outs = run(
            lambda *a, b=b, last=final, p=totals is not None: batch_kernel(nodes, b, last, p, *a),
            [piece] * nodes + [shape((total_rows, half), BF)] if final else before_grads,
            given,
            rooms,
            copies,
            (),
        )
        if final:
            fresh, totals = outs[:-1], outs[-1]
        else:
            assert b == 0
            fresh = outs[:2]
            totals = run(
                grads_kernel, [shape((total_rows, half), F32)], outs[2:], [], 1, (), (0, 1, 2)
            )[0]
        if not final:
            hops = [seg_next(side) for side in fresh]
            put, rows = run(
                lambda *a, b=b: base_kernel(b, *a),
                [shape((1, spread), I32), shape((spread, half), BF)],
                [asked, narrow, handed_memory],
                [numbers, pltpu.VMEM(bundle.shape, BF), pltpu.VMEM((node_rows, half), BF)],
                2,
            )
            few = nodes // 2
            values = [None] * nodes
            for side, first in ((0, few), (1, 0)):
                values[first : first + few] = run(
                    lambda *a, first=first: handed_kernel(first, *a),
                    [piece] * few,
                    [fresh[side], hops[side]] + ([rows] if side == 1 else []),
                    [],
                    few,
                )
            values = exchange(values)
            values, *served = run(
                lambda *a, b=b: next_kernel(b, *a),
                [shape((spread, half), BF)] + [piece] * nodes,
                [asked, put, rows] + values + [totals],
                [numbers, line, wide_rows, wide_rows],
                3 + nodes,
            )
            memory_now = run(
                update_kernel,
                [shape((node_rows, half), F32)],
                [put, values, memory_now, handed_memory],
                [line, wide_rows, block, pltpu.VMEM(bundle.shape, BF)],
                3,
            )[0]
            if b + 2 < batches:
                narrow = memory_now.astype(BF)
        else:
            returned = exchange(fresh)
            memory_out, done = run(
                lambda *a, b=b: last_kernel(b, *a),
                [shape((node_rows, half), F32), shape((8, half), F32)],
                [asked, memory_now] + returned,
                [numbers, wide_rows, block],
                2 + nodes,
            )

    def at(blocks, i):
        return lax.dynamic_index_in_dim(blocks, i, 0, keepdims=False)

    few = nodes // 2
    upper = z // few
    blocks = totals.reshape(segs, 2, few * chunk, half)
    got = [
        [seg_swap(at(at(blocks, s ^ x), side), x) for x in range(1, segs)]
        for side in (1 - upper, upper)
    ]
    share = pltpu.VMEM((few * chunk, half), BF)
    parts = [None] * nodes
    for side, first in ((0, few), (1, 0)):
        parts[first : first + few] = run(
            lambda *a, first=first: middle_kernel(nodes, segs, first, *a),
            [shape((chunk, half), BF)] * few,
            [totals] + got[side] + ([] if side else returned[1:]),
            [share] * (segs + 1),
            segs,
        )
    parts = exchange(parts)
    summed = run(
        sum_kernel,
        [shape((chunk, half), BF)],
        parts + [done],
        [pltpu.VMEM((chunk, half), BF)] * nodes,
        nodes,
    )[0]
    around = [summed] + [node_swap(summed, k) for k in range(1, nodes)]
    sides = [jnp.concatenate(around[:few], axis=0), jnp.concatenate(around[few:], axis=0)]
    near, distant = ([side] + [seg_swap(side, x) for x in range(1, segs)] for side in sides)
    gathered = run(
        widen_kernel,
        [shape((segs * few * chunk, half), F32)],
        near,
        [share] * segs,
        segs,
        flops=0,
    )
    gathered = [gathered[0]] + distant
    grads = run(
        lambda *a: unpack_kernel(nodes, segs, long, *a),
        [shape(w_input.shape, F32), shape(w_hidden.shape, F32), shape(bias.shape, F32)],
        gathered,
        [pltpu.VMEM((total_rows, half), F32)] + [share] * segs,
        segs + few * segs,
    )
    return (memory_out[None], *grads)


def solution(mesh):
    in_specs = (
        P(("parts", "seg"), "node", "feat"),
        P(None, ("parts", "seg"), "node", None, None),
        P(None, ("parts", "seg"), "node", None),
        P(None, ("parts", "seg"), "node"),
        P(None, ("parts", "seg"), "node"),
        P(None, ("parts", "seg"), "node", "feat"),
        P(None, ("parts", "seg"), "node", "feat"),
        P(),
        P(),
        P(None, None, "feat"),
        P(None, None, "feat"),
        P(None, "feat"),
    )
    out_specs = (
        P(("parts", "seg"), "node", "feat"),
        P("parts", None, "feat"),
        P("parts", None, "feat"),
        P("parts", "feat"),
    )
    return jax.shard_map(local, mesh=mesh, in_specs=in_specs, out_specs=out_specs, check_vma=False)
```

```python
import jax
import jax.numpy as jnp
from jax import lax
from jax.experimental import pallas as pl
from jax.experimental.pallas import tpu as pltpu
from jax.sharding import PartitionSpec as P

BF = jnp.bfloat16
F32 = jnp.float32
I32 = jnp.int32
LANES = 128
VMEM = pl.BlockSpec(memory_space=pltpu.VMEM)
ANY = pl.BlockSpec(memory_space=pl.ANY)
HBM = pl.BlockSpec(memory_space=pltpu.HBM)


def shape(dims, kind):
    return jax.ShapeDtypeStruct(tuple(dims), kind)


def run(kernel, outs, args, scratch=(), copies=1, far=(), here=(), flops=0):
    b, c = len(args), len(outs)

    def body(*refs):
        kernel(refs[-1], refs[:b], refs[b : b + c], refs[b + c : -1])

    moved = sum(a.size * a.dtype.itemsize for a in list(args) + list(outs))
    return pl.pallas_call(
        body,
        out_shape=list(outs),
        in_specs=[HBM if i in far else VMEM if i in here else ANY for i in range(len(args))],
        out_specs=[VMEM] * len(outs),
        scratch_shapes=list(scratch) + [pltpu.SemaphoreType.DMA((copies,))],
        compiler_params=pltpu.CompilerParams(vmem_limit_bytes=24 * 1024 * 1024),
        cost_estimate=pl.CostEstimate(flops=flops, bytes_accessed=moved, transcendentals=0),
    )(*args)


def begin(sems, pairs, first=0):
    copies = [
        pltpu.make_async_copy(source, target, sems.at[first + i])
        for i, (source, target) in enumerate(pairs)
    ]
    for copy in copies:
        copy.start()
    return copies


def end(copies):
    for copy in copies:
        copy.wait()


def down(row):
    return jnp.transpose(jnp.broadcast_to(row, (LANES, LANES)))


def ones_at(where):
    return jnp.where(where, 1.0, 0.0).astype(BF)


def pick_rows(row, source):
    numbers = down(row)
    lane = lax.broadcasted_iota(I32, (LANES, LANES), 1)
    hot = jnp.concatenate(
        [ones_at(numbers == lane + k * LANES) for k in range(source.shape[0] // LANES)], axis=1
    )
    return jnp.dot(hot, source, preferred_element_type=F32).astype(BF)


def set_rows(row, values, base_ref, out_ref):
    events = values.shape[0]
    tall = 256
    wide = jnp.concatenate([values, jnp.ones((events, LANES), BF)], axis=1)
    for i in range(out_ref.shape[0] // tall):
        own = lax.broadcasted_iota(I32, (tall, events), 0) + i * tall
        hot = ones_at(own == jnp.broadcast_to(row, (tall, events)))
        found = jnp.dot(hot, wide, preferred_element_type=F32)
        span = slice(i * tall, (i + 1) * tall)
        out_ref[span, :] = jnp.where(found[:, LANES:] > 0.5, found[:, :LANES], base_ref[span, :])


def padded(cap):
    return -(-cap // LANES) * LANES


def give(held, pieces):
    cap = pieces[0].shape[0]
    room = padded(cap)
    for k, piece in enumerate(pieces):
        piece[...] = held[k * room : k * room + cap, :]


def narrow_kernel(sems, given, made, scratch):
    end(begin(sems, [(given[0], scratch[0])]))
    made[0][...] = scratch[0][...].astype(BF)


def bundle_kernel(batch, sems, given, made, scratch):
    narrow_any, asked_any = given
    (out_ref,), (asked,) = made, scratch
    rows = narrow_any.shape[0]
    end(begin(sems, [(narrow_any, out_ref.at[:rows, :]), (asked_any, asked)]))
    lines = (out_ref.shape[0] - rows) // 2
    number = jnp.concatenate(
        [asked[batch : batch + 1, j * LANES : (j + 1) * LANES] for j in range(lines)], axis=0
    )
    high = jnp.floor(number.astype(F32) * (1.0 / 64.0))
    low = number.astype(F32) - 64.0 * high
    out_ref[rows:, :] = jnp.concatenate([high, low], axis=0).astype(BF)


def serve_kernel(sems, given, made, scratch):
    *asked_pieces, narrow_any = given
    asked_ref, *pieces = made
    narrow, held = scratch
    nodes, room = len(asked_pieces), asked_pieces[0].shape[1]
    pairs = [(narrow_any, narrow)]
    for k, piece in enumerate(asked_pieces):
        pairs.append((piece, asked_ref.at[:, k * room : (k + 1) * room]))
    end(begin(sems, pairs))
    for j in range(nodes * room // LANES):
        span = slice(j * LANES, (j + 1) * LANES)
        held[span, :] = pick_rows(asked_ref[0:1, span], narrow[...])
    give(held, pieces)


def pick_base(sems, memory_any, handed_any, base_ref, handed_ref, first):
    @pl.when(lax.axis_index("seg") == 0)
    def _():
        end(begin(sems, [(memory_any, base_ref)], first))

    @pl.when(lax.axis_index("seg") != 0)
    def _():
        end(begin(sems, [(handed_any, handed_ref)], first))
        base_ref[...] = handed_ref[: base_ref.shape[0], :].astype(base_ref.dtype)


def base_kernel(batch, sems, given, made, scratch):
    asked_any, narrow_any, handed_any = given
    put_ref, rows_ref = made
    asked, handed, narrow = scratch
    begun = begin(sems, [(asked_any, asked)])
    pick_base(sems, narrow_any, handed_any, narrow, handed, 1)
    end(begun)
    put_ref[...] = asked[batch : batch + 1, :]

    @pl.when(lax.axis_index("seg") != 0)
    def _():
        top = narrow.shape[0]
        lines = (handed.shape[0] - top) // 2
        digits = handed[top:, :].astype(F32)
        number = digits[:lines, :] * 64.0 + digits[lines:, :]
        for j in range(lines):
            put_ref[:, j * LANES : (j + 1) * LANES] = number[j : j + 1, :].astype(I32)

    for j in range(rows_ref.shape[0] // LANES):
        span = slice(j * LANES, (j + 1) * LANES)
        rows_ref[span, :] = pick_rows(asked[batch + 1 : batch + 2, span], narrow[...])


def gather_values(values, cap, pieces, sems, first):
    room = padded(cap)
    if room != cap:
        values[...] = jnp.zeros(values.shape, values.dtype)
    pairs = [(piece, values.at[k * room : k * room + cap, :]) for k, piece in enumerate(pieces)]
    return begin(sems, pairs, first)


def handed_kernel(first, sems, given, pieces, scratch):
    z = lax.axis_index("node")
    cap, few = pieces[0].shape[0], len(pieces)

    def send(source):
        pairs = []
        for k, piece in enumerate(pieces):
            at = pl.multiple_of(((z ^ (first + k)) % few) * cap, cap)
            pairs.append((source.at[pl.ds(at, cap), :], piece))
        end(begin(sems, pairs))

    @pl.when(lax.axis_index("seg") == 0)
    def _():
        send(given[0])

    @pl.when(lax.axis_index("seg") != 0)
    def _():
        send(given[1])


def next_kernel(batch, sems, given, made, scratch):
    asked_any, put_any, rows_any = given[:3]
    values_ref, pieces = made[0], made[1:]
    asked, put, rows, held = scratch
    cap = pieces[0].shape[0]
    begun = begin(sems, [(asked_any, asked), (put_any, put), (rows_any, rows)])
    end(gather_values(values_ref, cap, given[3:-1], sems, 3))
    end(begun)
    events = values_ref.shape[0]
    wide = jnp.concatenate([values_ref[...], jnp.ones((events, LANES), BF)], axis=1)
    written = jnp.where(put[...] < 0, -2, put[...])
    for j in range(events // LANES):
        span = slice(j * LANES, (j + 1) * LANES)
        numbers = down(asked[batch + 1 : batch + 2, span])
        hot = jnp.concatenate(
            [
                ones_at(
                    numbers
                    == jnp.broadcast_to(written[:, i * LANES : (i + 1) * LANES], (LANES, LANES))
                )
                for i in range(events // LANES)
            ],
            axis=1,
        )
        found = jnp.dot(hot, wide, preferred_element_type=F32)
        kept = rows[span, :].astype(F32)
        held[span, :] = jnp.where(found[:, LANES:] > 0.5, found[:, :LANES], kept).astype(BF)
    give(held, pieces)


def update_kernel(sems, given, made, scratch):
    put_any, values_any, memory_any, handed_any = given
    put, values, base, handed = scratch
    begun = begin(sems, [(put_any, put), (values_any, values)])
    pick_base(sems, memory_any, handed_any, base, handed, 2)
    end(begun)
    set_rows(put[...], values[...], base, made[0])


def last_kernel(batch, sems, given, made, scratch):
    asked_any, base_any, *pieces = given
    asked, values, base = scratch
    begun = begin(sems, [(asked_any, asked), (base_any, base)])
    end(gather_values(values, pieces[0].shape[0], pieces, sems, 2))
    end(begun)
    set_rows(asked[batch : batch + 1, :], values[...], base, made[0])
    made[1][...] = jnp.zeros(made[1].shape, F32)


def cosine(x):
    turns = jnp.round(x * 0.3183098861837907)
    r = x - turns * 3.140625
    r = r - turns * 0.0009670257568359375
    r = r - turns * 6.278329573009626e-07
    odd = turns - 2.0 * jnp.floor(turns * 0.5)
    q = r * r
    p = 2.08767569878681e-09 - q * 1.1470745597729725e-11
    p = q * p - 2.7557319223985893e-07
    p = q * p + 2.48015873015873e-05
    p = q * p - 0.001388888888888889
    p = q * p + 0.041666666666666664
    p = q * p - 0.5
    p = q * p + 1.0
    return p * (1.0 - 2.0 * odd)


def products(message, gates, sums, before, out_ref):
    long, width = message.shape[1], 2 * LANES
    tall = 256

    def put(start, value):
        stop = start + value.shape[0]
        if before is not None:
            value = value + before[start:stop, :]
        out_ref[start:stop, :] = value.astype(out_ref.dtype)

    for i in range(long // tall):
        rows = message[:, i * tall : (i + 1) * tall]
        columns = gates[...] if i * tall < width else gates[:, : 3 * LANES]
        product = lax.dot_general(
            rows, columns, (((0,), (0,)), ((), ())), preferred_element_type=F32
        )
        for g in range(3):
            put(g * long + i * tall, product[:, g * LANES : (g + 1) * LANES])
        if i * tall < width:
            put(3 * long + i * tall, product[:, 3 * LANES :])
    top = 3 * long + width
    pad = out_ref.shape[0] - top
    tail = jnp.concatenate(sums + [jnp.zeros((pad - 4, LANES), F32)], axis=0)
    put(top, tail)


def grads_kernel(sems, given, made, scratch):
    message, gates, sums = given
    products(message, gates, [sums[g : g + 1, :] for g in range(4)], None, made[0])


def side_kernel(batch, sems, given, made, scratch):
    facts_any, edge_any, edge_other_any = given
    facts, edge = scratch
    (side_ref,) = made
    events = side_ref.shape[0]
    thin = edge_any.shape[1]
    f = lax.axis_index("feat")
    own = pl.ds(pl.multiple_of(f * thin, thin), thin)
    other = pl.ds(pl.multiple_of((1 - f) * thin, thin), thin)
    pairs = [
        (facts_any, facts),
        (edge_any.at[batch], edge.at[own, :]),
        (edge_other_any.at[batch], edge.at[other, :]),
    ]
    end(begin(sems, pairs))
    lines = events // LANES
    top = facts.shape[0] - 8
    freq, phase = facts[top + 4 : top + 5, :], facts[top + 5 : top + 6, :]
    start = 2 * lines * batch + lines
    for j in range(lines):
        span = slice(j * LANES, (j + 1) * LANES)
        angle = down(facts[start + j : start + j + 1, :]) * freq + phase
        side_ref[span, :LANES] = cosine(angle).astype(BF)
        side_ref[span, LANES:] = jnp.transpose(edge[:, span].astype(F32)).astype(BF)


def batch_kernel(nodes, batch, final, prior, sems, given, made, scratch):
    facts_any, side_any, w_any, up_any = given[:4]
    own_pieces, other_pieces = given[4 : 4 + nodes], given[4 + nodes : 4 + 2 * nodes]
    rest = given[4 + 2 * nodes :]
    message, facts, w_ref, gates, up, fresh = scratch[:6]
    if not final:
        message, gates = made[2:4]
    cap = own_pieces[0].shape[0]
    events = nodes * cap
    z, f = lax.axis_index("node"), lax.axis_index("feat")
    mine = pl.multiple_of(f * LANES, LANES)
    other = pl.multiple_of((1 - f) * LANES, LANES)
    width = 2 * LANES
    long = message.shape[1]
    pairs = [(facts_any, facts)]
    for k in range(nodes):
        at = pl.ds(pl.multiple_of((z ^ k) * cap, cap), cap)
        pairs.append((own_pieces[k], message.at[at, pl.ds(mine, LANES)]))
        pairs.append((other_pieces[k], message.at[at, pl.ds(other, LANES)]))
    late = [(side_any, message.at[:, 2 * width :]), (w_any, w_ref), (up_any.at[batch], up)]
    if prior:
        before = scratch[6]
        late.append((rest[0], before))
    rows_begun = begin(sems, pairs)
    late_begun = begin(sems, late, len(pairs))
    end(rows_begun)
    lines = events // LANES
    top = facts.shape[0] - 8
    bias_ref = facts[top : top + 4, :]
    dst = [facts[2 * lines * batch + j : 2 * lines * batch + j + 1, :] for j in range(lines)]
    full = message[:, :width]
    for j in range(events // LANES):
        span = slice(j * LANES, (j + 1) * LANES)
        message[span, width : 2 * width] = pick_rows(dst[j].astype(I32), full)
    end(late_begun)
    w_in = [w_ref[g, :long, :] for g in range(3)]
    w_hid = [w_ref[g, long:, :] for g in range(3)]
    w_in01 = jnp.concatenate([w_in[0], w_in[1]], axis=1)
    w_hid01 = jnp.concatenate([w_hid[0], w_hid[1]], axis=1)
    sums = [jnp.zeros((1, LANES), F32) for _ in range(4)]
    tall = 256
    for i in range(events // tall):
        span = slice(i * tall, (i + 1) * tall)
        rows = message[span, :]
        hidden = rows[:, :width]
        both = jnp.dot(rows, w_in01, preferred_element_type=F32) + jnp.dot(
            hidden, w_hid01, preferred_element_type=F32
        )
        own = message[span, pl.ds(mine, LANES)].astype(F32)
        reset_gate = jax.nn.sigmoid(both[:, :LANES] + bias_ref[0:1, :])
        update = jax.nn.sigmoid(both[:, LANES:] + bias_ref[1:2, :])
        recur_term = jnp.dot(hidden, w_hid[2], preferred_element_type=F32) + bias_ref[3:4, :]
        candid = jnp.tanh(
            jnp.dot(rows, w_in[2], preferred_element_type=F32)
            + bias_ref[2:3, :]
            + reset_gate * recur_term
        )
        fresh[span, :] = ((1.0 - update) * candid + update * own).astype(BF)
        numbers = [down(dst[j]) for j in range(i * tall // LANES, (i + 1) * tall // LANES)]
        live = jnp.concatenate(numbers, axis=0) >= 0.0
        cotangent = jnp.where(live, up[span, :].astype(F32), 0.0)
        grad_cand = cotangent * (1.0 - update) * (1.0 - candid * candid)
        grad_upd = cotangent * (own - candid) * update * (1.0 - update)
        grad_reset = grad_cand * recur_term * reset_gate * (1.0 - reset_gate)
        grad_recur = grad_cand * reset_gate
        for g, part in enumerate((grad_reset, grad_upd, grad_cand, grad_recur)):
            sums[g] = sums[g] + jnp.sum(part, axis=0, keepdims=True)
            gates[span, g * LANES : (g + 1) * LANES] = part.astype(BF)
    if final:
        for k in range(nodes):
            made[k][...] = fresh[pl.ds(pl.multiple_of((z ^ k) * cap, cap), cap), :]
    else:
        few = events // 2
        upper = z // (nodes // 2)
        made[0][...] = fresh[pl.ds(pl.multiple_of((1 - upper) * few, few), few), :]
        made[1][...] = fresh[pl.ds(pl.multiple_of(upper * few, few), few), :]
    if final:
        products(message, gates, sums, before if prior else None, made[-1])
    else:
        made[4][...] = jnp.concatenate(sums + [jnp.zeros((4, LANES), F32)], axis=0)


def middle_kernel(nodes, segs, first, sems, given, made, scratch):
    totals, got = given[0], given[1:segs]
    rows = scratch[:segs]
    whole = scratch[segs]
    few, chunk = len(made), made[0].shape[0]
    z = lax.axis_index("node")
    side = (z ^ first) // few
    share = few * chunk
    at = pl.ds(pl.multiple_of((lax.axis_index("seg") * 2 + side) * share, share), share)
    pairs = [(totals.at[at, :], rows[0])] + list(zip(got, rows[1:]))
    end(begin(sems, pairs))
    total = rows[0][...].astype(F32)
    for x in range(1, segs):
        total = total + rows[x][...].astype(F32)
    whole[...] = total.astype(BF)
    for k in range(few):
        at = pl.multiple_of(((z ^ (first + k)) % few) * chunk, chunk)
        made[k][...] = whole[pl.ds(at, chunk), :]


def sum_kernel(sems, given, made, scratch):
    end(begin(sems, list(zip(given, scratch))))
    total = scratch[0][...].astype(F32)
    for part in scratch[1:]:
        total = total + part[...].astype(F32)
    made[0][...] = total.astype(BF)


def widen_kernel(sems, given, made, scratch):
    (out_ref,), rows = made, given[0].shape[0]
    for x, part in enumerate(given):
        out_ref[x * rows : (x + 1) * rows, :] = part[...].astype(F32)


def unpack_kernel(nodes, segs, long, sems, pieces, made, scratch):
    grad_in, grad_hid, grad_bias = made
    (held,), far = scratch, pieces[1:]
    few = nodes // 2
    chunk = pieces[1].shape[0] // few
    z, s = lax.axis_index("node"), lax.axis_index("seg")

    def place(x, k):
        at = pl.multiple_of(((s ^ x) * nodes + (z ^ k)) * chunk, chunk)
        return pl.ds(at, chunk)

    for x in range(segs):
        for k in range(few):
            i = x * few + k
            held[place(x, k), :] = pieces[0][i * chunk : (i + 1) * chunk, :]
    for x in range(segs):
        for k in range(few):
            held[place(x, few + k), :] = far[x][k * chunk : (k + 1) * chunk, :].astype(F32)
    width = grad_hid.shape[1]
    for g in range(3):
        grad_in[g] = held[g * long : (g + 1) * long, :].astype(F32)
    for g in range(2):
        grad_hid[g] = held[g * long : g * long + width, :].astype(F32)
    grad_hid[2] = held[3 * long : 3 * long + width, :].astype(F32)
    top = 3 * long + width
    grad_bias[...] = held[top : top + 16, :].astype(F32)[:4, :]


def local(
    memory, req_rows, req_count, dst_slot, elapsed, edges, upstream, freq, phase, w_input, w_hidden, bias
):
    nodes, segs = lax.axis_size("node"), lax.axis_size("seg")
    z, s = lax.axis_index("node"), lax.axis_index("seg")
    memory_now = memory[0]
    node_rows, half = memory_now.shape
    batches, cap = req_rows.shape[0], req_rows.shape[-1]
    events = nodes * cap
    room = padded(cap)
    spread = nodes * room
    counts = req_count[:, 0, 0]
    piece = shape((cap, half), BF)
    long, width = w_input.shape[1], w_hidden.shape[1]

    def node_swap(block, k):
        return lax.ppermute(block, "node", [(i, i ^ k) for i in range(nodes)])

    def seg_swap(block, x):
        return lax.ppermute(block, "seg", [(i, i ^ x) for i in range(segs)])

    def seg_next(block):
        return lax.ppermute(block, "seg", [(i, i + 1) for i in range(segs - 1)])

    def feat_swap(block):
        return lax.ppermute(block, "feat", [(0, 1), (1, 0)])

    def exchange(blocks):
        return [blocks[0]] + [node_swap(blocks[k], k) for k in range(1, nodes)]

    live = jnp.arange(cap)[None, None, :] < counts[:, :, None]
    masked = jnp.where(live, req_rows[:, 0, 0], -1)
    masked = jnp.pad(masked, ((0, 0), (0, 0), (0, room - cap)), constant_values=-1)
    wanted = exchange(
        [lax.dynamic_index_in_dim(masked, z ^ k, 1, keepdims=False) for k in range(nodes)]
    )
    wide_rows = pltpu.VMEM((spread, half), BF)
    edge_own = jnp.swapaxes(edges[:, 0], 1, 2)
    edge_other = feat_swap(edge_own)
    lines = events // LANES
    named = jnp.where(live, dst_slot[:, 0].reshape(live.shape), -1)
    facts = jnp.stack([named.reshape(batches, events), elapsed[:, 0]], axis=1).astype(F32)
    facts = facts.reshape(batches * 2 * lines, LANES)
    rest = jnp.zeros((2, half), F32)
    facts = jnp.concatenate([facts, bias, freq[None], phase[None], rest], axis=0)

    weights = jnp.concatenate([w_input, w_hidden], axis=1)
    narrow = run(
        narrow_kernel,
        [shape((node_rows, half), BF)],
        [memory_now, wanted[1], facts, weights],
        [pltpu.VMEM((node_rows, half), F32)],
        1,
        (0,),
    )[0]
    asked, *served = run(
        serve_kernel,
        [shape((batches, spread), I32)] + [piece] * nodes,
        wanted + [narrow],
        [pltpu.VMEM((node_rows, half), BF), wide_rows],
        nodes + 1,
    )

    chunk = -(-(3 * long + width + 16) // (16 * nodes * segs)) * 16
    total_rows = chunk * nodes * segs
    numbers = pltpu.VMEM((batches, spread), I32)
    line = pltpu.VMEM((1, spread), I32)
    block = pltpu.VMEM((node_rows, half), F32)
    totals = None
    for b in range(batches):
        final = b + 1 == batches
        own_pieces = exchange(served)
        if not final:
            bundle = run(
                lambda *a, b=b: bundle_kernel(b, *a),
                [shape((node_rows + 2 * spread // LANES, half), BF)],
                [narrow, asked],
                [numbers],
                2,
            )[0]
            handed_memory = seg_next(bundle)
        other_pieces = [feat_swap(p) for p in own_pieces]
        beside = run(
            lambda *a, b=b: side_kernel(b, *a),
            [shape((events, 2 * LANES), BF)],
            [facts, edge_own, edge_other],
            [pltpu.VMEM(facts.shape, F32), pltpu.VMEM((2 * edges.shape[-1], events), BF)],
            3,
        )[0]
        given = [facts, beside, weights, upstream[:, 0]]
        given = given + own_pieces + other_pieces + ([] if totals is None else [totals])
        rooms = [
            pltpu.VMEM((events, long), BF),
            pltpu.VMEM(facts.shape, F32),
            pltpu.VMEM(weights.shape, BF),
            pltpu.VMEM((events, 4 * half), BF),
            pltpu.VMEM((events, half), BF),
            pltpu.VMEM((events, half), BF),
        ]
        if totals is not None:
            rooms.append(pltpu.VMEM((total_rows, half), F32))
        copies = 7 + 2 * nodes
        before_grads = [shape((events // 2, half), BF)] * 2 + [
            shape((events, long), BF),
            shape((events, 4 * half), BF),
            shape((8, half), F32),
        ]
        outs = run(
            lambda *a, b=b, last=final, p=totals is not None: batch_kernel(nodes, b, last, p, *a),
            [piece] * nodes + [shape((total_rows, half), BF)] if final else before_grads,
            given,
            rooms,
            copies,
            (),
        )
        if final:
            fresh, totals = outs[:-1], outs[-1]
        else:
            assert b == 0
            fresh = outs[:2]
            totals = run(
                grads_kernel, [shape((total_rows, half), F32)], outs[2:], [], 1, (), (0, 1, 2)
            )[0]
        if not final:
            hops = [seg_next(side) for side in fresh]
            put, rows = run(
                lambda *a, b=b: base_kernel(b, *a),
                [shape((1, spread), I32), shape((spread, half), BF)],
                [asked, narrow, handed_memory],
                [numbers, pltpu.VMEM(bundle.shape, BF), pltpu.VMEM((node_rows, half), BF)],
                2,
            )
            few = nodes // 2
            values = [None] * nodes
            for side, first in ((0, few), (1, 0)):
                values[first : first + few] = run(
                    lambda *a, first=first: handed_kernel(first, *a),
                    [piece] * few,
                    [fresh[side], hops[side]] + ([rows] if side == 1 else []),
                    [],
                    few,
                )
            values = exchange(values)
            values, *served = run(
                lambda *a, b=b: next_kernel(b, *a),
                [shape((spread, half), BF)] + [piece] * nodes,
                [asked, put, rows] + values + [totals],
                [numbers, line, wide_rows, wide_rows],
                3 + nodes,
            )
            memory_now = run(
                update_kernel,
                [shape((node_rows, half), F32)],
                [put, values, memory_now, handed_memory],
                [line, wide_rows, block, pltpu.VMEM(bundle.shape, BF)],
                3,
            )[0]
            if b + 2 < batches:
                narrow = memory_now.astype(BF)
        else:
            returned = exchange(fresh)
            memory_out, done = run(
                lambda *a, b=b: last_kernel(b, *a),
                [shape((node_rows, half), F32), shape((8, half), F32)],
                [asked, memory_now] + returned,
                [numbers, wide_rows, block],
                2 + nodes,
            )

    def at(blocks, i):
        return lax.dynamic_index_in_dim(blocks, i, 0, keepdims=False)

    few = nodes // 2
    upper = z // few
    blocks = totals.reshape(segs, 2, few * chunk, half)
    got = [
        [seg_swap(at(at(blocks, s ^ x), side), x) for x in range(1, segs)]
        for side in (1 - upper, upper)
    ]
    share = pltpu.VMEM((few * chunk, half), BF)
    parts = [None] * nodes
    for side, first in ((0, few), (1, 0)):
        parts[first : first + few] = run(
            lambda *a, first=first: middle_kernel(nodes, segs, first, *a),
            [shape((chunk, half), BF)] * few,
            [totals] + got[side] + ([] if side else returned[1:]),
            [share] * (segs + 1),
            segs,
        )
    parts = exchange(parts)
    summed = run(
        sum_kernel,
        [shape((chunk, half), BF)],
        parts + [done],
        [pltpu.VMEM((chunk, half), BF)] * nodes,
        nodes,
    )[0]
    around = [summed] + [node_swap(summed, k) for k in range(1, nodes)]
    sides = [jnp.concatenate(around[:few], axis=0), jnp.concatenate(around[few:], axis=0)]
    near, distant = ([side] + [seg_swap(side, x) for x in range(1, segs)] for side in sides)
    gathered = run(
        widen_kernel,
        [shape((segs * few * chunk, half), F32)],
        near,
        [],
        here=tuple(range(segs)),
        flops=0,
    )
    gathered = [gathered[0]] + distant
    grads = run(
        lambda *a: unpack_kernel(nodes, segs, long, *a),
        [shape(w_input.shape, F32), shape(w_hidden.shape, F32), shape(bias.shape, F32)],
        gathered,
        [pltpu.VMEM((total_rows, half), F32)],
        here=tuple(range(segs + 1)),
    )
    return (memory_out[None], *grads)


def solution(mesh):
    in_specs = (
        P(("parts", "seg"), "node", "feat"),
        P(None, ("parts", "seg"), "node", None, None),
        P(None, ("parts", "seg"), "node", None),
        P(None, ("parts", "seg"), "node"),
        P(None, ("parts", "seg"), "node"),
        P(None, ("parts", "seg"), "node", "feat"),
        P(None, ("parts", "seg"), "node", "feat"),
        P(),
        P(),
        P(None, None, "feat"),
        P(None, None, "feat"),
        P(None, "feat"),
    )
    out_specs = (
        P(("parts", "seg"), "node", "feat"),
        P("parts", None, "feat"),
        P("parts", None, "feat"),
        P("parts", "feat"),
    )
    return jax.shard_map(local, mesh=mesh, in_specs=in_specs, out_specs=out_specs, check_vma=False)
```
